256 devices in a mesh: grp: 2 (over core), gx: 32 (over z, x), gy: 4 (over y).
Axes of the slice: x: 4, y: 4, z: 8, core: 2. Of those that a mesh axis runs over, the one named last changes fastest.
Arguments:
- pressure_start: float32 [128, 32, 256], P('gx', 'gy', 'grp'), may hold values from -6 to 6
- source: float32 [128, 32, 256], P('gx', 'gy', 'grp'), may hold values from -6 to 6
- storage: float32 [128, 32, 256], P('gx', 'gy', 'grp'), may hold values from 0.02 to 0.2
- perm_class: int32 [128, 32, 256], P('gx', 'gy', 'grp'), may hold values from 0 to 15
- class_perm: float32 [16], replicated, may hold values from 0.1 to 10
- block_route: int32 [32, 8, 512], P('gx'), may hold values from 0 to 511, each once within a row
- displacement_start: float32 [3, 131072], P(None, ('grp', 'gx', 'gy')), may hold values from -3 to 3
- load: float32 [3, 131072], P(None, ('grp', 'gx', 'gy')), may hold values from -6 to 6
- support: float32 [3, 131072], P(None, ('grp', 'gx', 'gy')), may hold values from 0.2 to 2
- lame_lambda: float32 [256, 512], P(('grp', 'gx', 'gy')), may hold values from 0.5 to 2
- lame_mu: float32 [256, 512], P(('grp', 'gx', 'gy')), may hold values from 0.3 to 1.5
- stiff_lambda: float32 [24, 24], replicated, may hold values from -0.8 to 0.8, as said below
- stiff_mu: float32 [24, 24], replicated, may hold values from -0.8 to 0.8, as said below
- coupling_vec: float32 [24], replicated, may hold values from -0.36 to 0.36, as said below
Outputs:
- pressure: float32 [128, 32, 256], P('gx', 'gy', 'grp')
- displacement: float32 [3, 131072], P(None, ('grp', 'gx', 'gy'))
The draws below stay inside these ranges and needn't reach their ends.
Inputs may be any that keep to these rules, and one draw needn't show every extreme that they name: For each gx and each k, block_route[gx][k] holds every number of 0 to 511 once. `stiff_lambda`: symmetric; each row sums to zero. `stiff_mu`: symmetric; each row sums to zero. `coupling_vec`: the eight entries of each component sum to zero.
All inputs are finite; a program needn't handle non-finite values.
Results may differ from the reference program's by a relative error of at most 0.0001.
Values sent between devices are 32-bit elements; how exact they have to be, the bound alone decides.
No kernel may reach another device: no remote copies, remote signals or barrier semaphores. Data moves between devices by JAX's collectives and lax.ppermute only.
A program may use at most 64 MiB of HBM per device.

```python
import math
import jax
import jax.numpy as jnp
from jax import lax

CX = 4
CY = 8
CZ = 128
OUTER = 2
SWEEPS = 6
MSWEEPS = 2
CLASSES = 16
NX = 128
NY = 32
NZ = 256
NB_DEV = 512
SHARERS = 8
BSLOTS = 64
NODES = 131072
N_GRP = 2
N_GX = 32
N_GY = 4
DEVICES = 256


def brick_edges(key):
    return jax.random.uniform(jax.random.fold_in(key, 77), (3,), jnp.float32, 0.7, 1.4)


def corner_bits():
    index = jnp.arange(24, dtype=jnp.int32)
    corner = index % 8
    bits = jnp.stack([corner // 4 % 2, corner // 2 % 2, corner % 2])
    return (index // 8, bits)


def brick_integral(edges, bits, deriv_row, deriv_col):
    row_bits = bits[:, :, None]
    col_bits = bits[:, None, :]
    total = jnp.ones((24, 24), jnp.float32)
    for axis_k in range(3):
        length = edges[axis_k]
        alike = row_bits[axis_k] == col_bits[axis_k]
        stiff_one = jnp.where(alike, 1.0, -1.0) / length
        mass_one = length * jnp.where(alike, 2.0, 1.0) / 6.0
        grad_row = (2.0 * row_bits[axis_k].astype(jnp.float32) - 1.0) / 2.0
        grad_col = (2.0 * col_bits[axis_k].astype(jnp.float32) - 1.0) / 2.0
        on_row = deriv_row == axis_k
        on_col = deriv_col == axis_k
        factor = jnp.where(on_row & on_col, stiff_one, jnp.where(on_row, grad_row, jnp.where(on_col, grad_col, mass_one)))
        total = total * factor
    return total


def draw_stiff_lambda(key, part):
    edges = brick_edges(key)
    component, bits = corner_bits()
    comp_row = jnp.broadcast_to(component[:, None], (24, 24))
    comp_col = jnp.broadcast_to(component[None, :], (24, 24))
    return brick_integral(edges, bits, comp_row, comp_col)


def draw_stiff_mu(key, part):
    edges = brick_edges(key)
    component, bits = corner_bits()
    comp_row = jnp.broadcast_to(component[:, None], (24, 24))
    comp_col = jnp.broadcast_to(component[None, :], (24, 24))
    gradient_sum = jnp.zeros((24, 24), jnp.float32)
    for axis_k in range(3):
        fixed = jnp.full((24, 24), axis_k, jnp.int32)
        gradient_sum = gradient_sum + brick_integral(edges, bits, fixed, fixed)
    same = comp_row == comp_col
    return jnp.where(same, gradient_sum, 0.0) + brick_integral(edges, bits, comp_col, comp_row)


def draw_coupling_vec(key, part):
    edges = brick_edges(key)
    component, bits = corner_bits()
    own_bit = jnp.sum(jnp.where(jnp.arange(3)[:, None] == component[None, :], bits, 0), axis=0)
    own_edge = edges[component]
    return (2.0 * own_bit.astype(jnp.float32) - 1.0) / (4.0 * own_edge)


def touch_ends(values, own_key, least, high):
    shape = values.shape
    index_at = [jax.random.randint(jax.random.fold_in(own_key, axis), (), 0, shape[axis]) for axis in range(len(shape))]
    values = values.at[tuple(index_at)].set(least)
    longest = shape.index(max(shape))
    index_at[longest] = (index_at[longest] + 1) % shape[longest]
    return values.at[tuple(index_at)].set(high)


def level_of(rng, dims, shards, smallest, largest):
    level = 1.0
    for dim, shards_of in shards:
        draws = jax.random.uniform(jax.random.fold_in(jax.random.fold_in(rng, 6), dim), (shards_of,), jnp.float32, smallest / len(shards), largest / len(shards))
        level = level * jnp.repeat(jnp.exp(draws), dims[dim] // shards_of).reshape((-1,) + (1,) * (len(dims) - 1 - dim))
    return level


def gaussian(rng, extent, scale, limit, split=(), held_as=jnp.bfloat16):
    gain = level_of(rng, extent, split, -0.22, 0.18) if split else 1.0
    values = jax.random.normal(rng, extent, jnp.float32) * scale * gain
    return jnp.minimum(jnp.maximum(values, -limit), limit).astype(held_as)


def setup_inputs(seed: int = 0) -> dict:
    splits = jax.random.split(jax.random.key(seed), 15)
    pressure_start = gaussian(splits[0], (NX, NY, NZ), 1.0, 6.0, ((0, 32), (1, 4), (2, 2)), jnp.float32)
    source = gaussian(splits[1], (NX, NY, NZ), 1.0, 6.0, ((0, 32), (1, 4), (2, 2)), jnp.float32)
    storage = jnp.clip(jnp.exp(math.log(0.2) - 2.3025851 * jax.random.uniform(splits[2], (NX, NY, NZ), jnp.float32) ** level_of(splits[2], (NX, NY, NZ), ((0, 32), (1, 4), (2, 2)), -0.2, 0.2)), 0.02, 0.2)
    perm_class = touch_ends(jax.random.randint(splits[3], (NX, NY, NZ), 0, CLASSES), jax.random.fold_in(splits[3], 1), 0, CLASSES - 1).astype(jnp.int32)
    class_perm = jnp.clip(jnp.exp(jax.random.uniform(splits[4], (CLASSES,), jnp.float32, math.log(0.1), math.log(10.0))), 0.1, 10.0)
    block_route = jax.vmap(lambda own: jax.random.permutation(own, NB_DEV))(jax.random.split(splits[5], N_GX * SHARERS)).reshape((N_GX, SHARERS, NB_DEV)).astype(jnp.int32)
    displacement_start = gaussian(splits[6], (3, NODES), 0.5, 3.0, ((1, 256),), jnp.float32)
    load = gaussian(splits[7], (3, NODES), 1.0, 6.0, ((1, 256),), jnp.float32)
    support = jnp.clip(jnp.exp(math.log(2.0) - 2.3025851 * jax.random.uniform(splits[8], (3, NODES), jnp.float32) ** level_of(splits[8], (3, NODES), ((1, 256),), -0.2, 0.2)), 0.2, 2.0)
    lame_lambda = jnp.clip(jnp.exp(math.log(2.0) - 1.3862944 * jax.random.uniform(splits[9], (DEVICES, NB_DEV), jnp.float32) ** level_of(splits[9], (DEVICES, NB_DEV), ((0, 256),), -0.2, 0.2)), 0.5, 2.0)
    lame_mu = jnp.clip(jnp.exp(math.log(1.5) - 1.60943787 * jax.random.uniform(splits[10], (DEVICES, NB_DEV), jnp.float32) ** level_of(splits[10], (DEVICES, NB_DEV), ((0, 256),), -0.2, 0.2)), 0.3, 1.5)
    stiff_lambda = draw_stiff_lambda(jax.random.fold_in(splits[14], 71), 0)
    stiff_mu = draw_stiff_mu(jax.random.fold_in(splits[14], 71), 0)
    coupling_vec = draw_coupling_vec(jax.random.fold_in(splits[14], 71), 0)
    return {"pressure_start": pressure_start, "source": source, "storage": storage, "perm_class": perm_class, "class_perm": class_perm, "block_route": block_route, "displacement_start": displacement_start, "load": load, "support": support, "lame_lambda": lame_lambda, "lame_mu": lame_mu, "stiff_lambda": stiff_lambda, "stiff_mu": stiff_mu, "coupling_vec": coupling_vec}


stabilize = 0.5
biot_coef = 0.8
damping = 0.7


def harmonic(inside, outside):
    return 2.0 * inside * outside / (inside + outside)


def shifted_views(padded):
    return (padded[2:, 1:-1, 1:-1], padded[:-2, 1:-1, 1:-1], padded[1:-1, 2:, 1:-1],
            padded[1:-1, :-2, 1:-1], padded[1:-1, 1:-1, 2:], padded[1:-1, 1:-1, :-2])


def stencil_sum(padded, face_terms):
    beside = shifted_views(padded)
    summed = face_terms[0] * beside[0]
    for member in range(1, 6):
        summed = summed + face_terms[member] * beside[member]
    return summed


def reference(pressure_start, source, storage, perm_class, class_perm, block_route, displacement_start,
              load, support, lame_lambda, lame_mu, stiff_lambda, stiff_mu, coupling_vec):
    highest = lax.Precision.HIGHEST
    permeable = class_perm[perm_class]
    face_terms = tuple(harmonic(permeable, neighbor) for neighbor in shifted_views(jnp.pad(permeable, 1)))
    face_total = face_terms[0]
    for member in range(1, 6):
        face_total = face_total + face_terms[member]
    flow_diag = storage + stabilize + face_total
    fixed_rhs = source + storage * pressure_start
    half_x, half_y, half_z = CX // 2, CY // 2, CZ // 2
    wide_x, wide_y, wide_z = NX // 2, NY // 2, NZ // 2
    routes = block_route.reshape(N_GX, N_GRP, N_GY, N_GRP, N_GY, BSLOTS)
    elem_block = jnp.transpose(routes, (3, 0, 4, 1, 2, 5)).astype(jnp.int32)
    shape = elem_block.shape
    column_x = lax.broadcasted_iota(jnp.int32, shape, 1)
    source_z = lax.broadcasted_iota(jnp.int32, shape, 3)
    source_y = lax.broadcasted_iota(jnp.int32, shape, 4)
    glob_x = (column_x * half_x + elem_block // (half_y * half_z)).reshape(-1)
    glob_y = (source_y * half_y + (elem_block // half_z) % half_y).reshape(-1)
    glob_z = (source_z * half_z + elem_block % half_z).reshape(-1)
    block_index = (glob_x * wide_y + glob_y) * wide_z + glob_z
    corners = jnp.stack([((glob_x + corner // 4) * (wide_y + 1) + glob_y + (corner // 2) % 2) * (wide_z + 1)
                         + glob_z + corner % 2 for corner in range(8)])
    padded_count = (wide_x + 1) * (wide_y + 1) * (wide_z + 1)
    first_lame = lame_lambda.reshape(1, -1)
    second_lame = lame_mu.reshape(1, -1)

    def to_grid(values):
        grid = values.reshape(3, N_GRP, N_GX, N_GY, half_x, half_y, half_z)
        return jnp.transpose(grid, (0, 2, 4, 3, 5, 1, 6)).reshape(3, wide_x, wide_y, wide_z)

    def from_grid(grid):
        values = grid.reshape(3, N_GX, half_x, N_GY, half_y, N_GRP, half_z)
        return jnp.transpose(values, (0, 5, 1, 3, 2, 4, 6)).reshape(3, NODES)

    def corner_values(grid):
        flat = jnp.pad(grid, ((0, 0), (0, 1), (0, 1), (0, 1))).reshape(3, -1)
        return flat[:, corners].reshape(24, -1)

    def assemble(terms):
        flat = jnp.zeros((3, padded_count), jnp.float32).at[:, corners].add(terms.reshape(3, 8, -1))
        return flat.reshape(3, wide_x + 1, wide_y + 1, wide_z + 1)[:, :-1, :-1, :-1]

    owned_disp = to_grid(displacement_start)
    load_grid = to_grid(load)
    support_grid = to_grid(support)
    diag_terms = first_lame * jnp.diag(stiff_lambda)[:, None] + second_lame * jnp.diag(stiff_mu)[:, None]
    node_diag = support_grid + assemble(diag_terms)
    pressure = pressure_start
    strain_first = jnp.zeros_like(pressure_start)
    for outer_step in range(OUTER):
        corner_vals = corner_values(owned_disp)
        elem_strain = jnp.dot(coupling_vec, corner_vals, precision=highest)
        strain_blocks = jnp.zeros((wide_x * wide_y * wide_z,), jnp.float32).at[block_index].set(elem_strain)
        strain_blocks = strain_blocks.reshape(wide_x, wide_y, wide_z)
        strain = jnp.broadcast_to(strain_blocks[:, None, :, None, :, None],
                                  (wide_x, 2, wide_y, 2, wide_z, 2)).reshape(NX, NY, NZ)
        if outer_step == 0:
            strain_first = strain
        right_side = fixed_rhs + stabilize * pressure - biot_coef * (strain - strain_first)
        for sweep_step in range(SWEEPS):
            pressure = (right_side + stencil_sum(jnp.pad(pressure, 1), face_terms)) / flow_diag
        block_press = jnp.mean(pressure.reshape(wide_x, 2, wide_y, 2, wide_z, 2), axis=(1, 3, 5)).reshape(-1)
        elem_press = block_press[block_index]
        for sweep_step in range(MSWEEPS):
            if sweep_step > 0:
                corner_vals = corner_values(owned_disp)
            bulk_part = jnp.dot(stiff_lambda, corner_vals, precision=highest)
            shear_part = jnp.dot(stiff_mu, corner_vals, precision=highest)
            forces = first_lame * bulk_part + second_lame * shear_part
            elem_terms = biot_coef * elem_press[None, :] * coupling_vec[:, None] - forces
            residual = load_grid - support_grid * owned_disp + assemble(elem_terms)
            owned_disp = owned_disp + damping * residual / node_diag
    return pressure, from_grid(owned_disp)
```

```python
import jax
import jax.numpy as jnp
import numpy as np
from jax import lax
from jax.experimental import pallas as pl
from jax.experimental.pallas import tpu as pltpu
from jax.sharding import Mesh
from jax.sharding import PartitionSpec as P

SWEEPS = 6
CLASSES = 16
CHIPS = 16
PLANES = 14
NODES = 16

stabilize = 0.5
biot_coef = 0.8
damping = 0.7
tiny = 1e-30

f32 = jnp.float32
bf16 = jnp.bfloat16

VM = pl.BlockSpec(memory_space=pltpu.VMEM)
SM = pl.BlockSpec(memory_space=pltpu.SMEM)


def call(body, out_shapes, in_specs, scratch=()):
    return pl.pallas_call(
        body,
        out_shape=out_shapes,
        in_specs=in_specs,
        out_specs=jax.tree.map(lambda _: VM, out_shapes),
        scratch_shapes=list(scratch),
        compiler_params=pltpu.CompilerParams(vmem_limit_bytes=40 * 1024 * 1024),
    )


def lanes(shape):
    return lax.broadcasted_iota(jnp.int32, shape, 1)


def rows(shape):
    return lax.broadcasted_iota(jnp.int32, shape, 0)


def roll(x, shift, axis=1):
    shift = shift % x.shape[axis]
    return x if shift == 0 else pltpu.roll(x, shift, axis)


def three_parts(x):
    high = x.astype(bf16)
    rest = x - high.astype(f32)
    middle = rest.astype(bf16)
    return high, middle, (rest - middle.astype(f32)).astype(bf16)


def nt_dot(a, b):
    return lax.dot_general(a, b, (((1,), (1,)), ((), ())), preferred_element_type=f32)


def stage_kernel(classes, p0, src, sto, cls, disp, load, sup, lam, mu, cells, nodes, elems):
    for i in range(4):
        cells[i] = p0[i]
        cells[4 + i] = src[i]
        cells[8 + i] = sto[i]
        which = cls[i]
        perm = jnp.zeros((8, 128), f32)
        for member in range(CLASSES):
            perm = jnp.where(which == member, classes[member], perm)
        cells[12 + i] = perm
    nodes[...] = jnp.zeros((16, 512), f32)
    nodes[0:3] = disp[...]
    nodes[4:7] = load[...]
    nodes[8:11] = sup[...]
    low = lanes((1, 128)) < 64
    elems[...] = jnp.zeros((8, 8, 128), f32)
    for half in range(2):
        for y in range(4):
            index = half * 4 + y
            at = index // 2 * 128
            a = lam[0:1, at : at + 128]
            b = mu[0:1, at : at + 128]
            if index % 2 == 0:
                pair = jnp.where(low, a, roll(b, 64))
            else:
                pair = jnp.where(low, roll(a, 64), b)
            elems[y, half : half + 1] = pair
            elems[4 + y, half : half + 1] = pair


def pack_kernel(core, cells, cells_other, nodes, nodes_other, routed, routes, out, lame):
    first = core[0] == 0
    lane = lanes((8, 128))
    low = lane < 64
    lams = []
    mus = []
    for q in range(4):
        a = routed[2 * q]
        b = routed[2 * q + 1]
        lams.append(jnp.where(low, a, roll(b, 64)))
        mus.append(jnp.where(low, roll(a, 64), b))
    values = jnp.concatenate(
        three_parts(jnp.concatenate(lams, axis=1)) + three_parts(jnp.concatenate(mus, axis=1)), axis=0
    )
    block = rows((512, 512))
    for half in range(2):
        chosen = jnp.where(block == routes[half : half + 1, :], 1.0, 0.0).astype(bf16)
        got = nt_dot(values, chosen)
        lame[half] = got[0:8] + got[8:16] + got[16:24]
        lame[2 + half] = got[24:32] + got[32:40] + got[40:48]

    for pair in range(2):
        for i in range(4):
            tiles = []
            for field in (2 * pair, 2 * pair + 1):
                own = cells[4 * field + i]
                other = cells_other[4 * field + i]
                tiles.append((jnp.where(first, own, other), jnp.where(first, other, own)))
            for chip in range(CHIPS):
                start = 16 * chip - 24
                spot = lane % 64 + start
                in_low = (spot >= 0) & (spot < 128)
                in_high = (spot >= 128) & (spot < 256)
                found = []
                for member in range(2):
                    shift = 64 * member - start
                    win = jnp.zeros((8, 128), f32)
                    if start < 128:
                        win = jnp.where(in_low, roll(tiles[member][0], shift), win)
                    if start + 64 > 128:
                        win = jnp.where(in_high, roll(tiles[member][1], shift), win)
                    found.append(win)
                out[chip, 4 * pair + i] = jnp.where(low, found[0], found[1])

    sub = rows((8, 128))
    for i in range(2):
        for r in range(2):
            full = []
            for j in range(4):
                at = (i * 4 + j) // 2 * 128
                parts = []
                for half in range(2):
                    own = nodes[8 * r : 8 * r + 8, at : at + 128]
                    other = nodes_other[8 * r : 8 * r + 8, at : at + 128]
                    if half == 0:
                        tile = jnp.where(first, own, other)
                    else:
                        tile = jnp.where(first, other, own)
                    tile = jnp.where(sub == 7, lame[2 * r + half, half : half + 1, at : at + 128], tile)
                    parts.append(tile)
                if j % 2 == 0:
                    full.append(jnp.where(low, parts[0], roll(parts[1], 64)))
                else:
                    full.append(jnp.where(low, roll(parts[0], 64), parts[1]))
            for chip in range(CHIPS):
                start = 8 * chip - 12
                spot = lane % 32 + start
                tile = jnp.zeros((8, 128), f32)
                for j in range(4):
                    tile = jnp.where(lane // 32 == j, roll(full[j], 32 * j - start), tile)
                out[chip, 8 + 2 * i + r] = jnp.where((spot >= 0) & (spot < 128), tile, 0.0)


def low_mask(shape):
    return lanes(shape) < 64


def above(ref, x):
    return ref[x + 1] if x < PLANES - 1 else roll(ref[0], 64)


def below(ref, x):
    return ref[x - 1] if x > 0 else roll(ref[PLANES - 1], 64)


def window(core, places, then):
    for c in range(2):
        @pl.when(core[0] == c)
        def _():
            then(places[c])


def cell_coefs(start, source, storage, perm, coef, fixed, inverse):
    keep_top = rows((32, 128)) < 31
    for x in range(PLANES):
        p = perm[x]
        q = above(perm, x)
        coef[0, x] = 2.0 * p * q / jnp.maximum(p + q, tiny)
        q = roll(p, 31, 0)
        coef[2, x] = jnp.where(keep_top, 2.0 * p * q / jnp.maximum(p + q, tiny), 0.0)
        q = roll(p, 127)
        coef[4, x] = 2.0 * p * q / jnp.maximum(p + q, tiny)
    for x in range(PLANES):
        coef[1, x] = coef[0, x - 1] if x > 0 else roll(coef[0, PLANES - 1], 64)
        coef[3, x] = roll(coef[2, x], 1, 0)
        coef[5, x] = roll(coef[4, x], 1)
    for x in range(PLANES):
        total = coef[0, x] + coef[1, x] + coef[2, x] + coef[3, x] + coef[4, x] + coef[5, x]
        inv = jnp.where(storage[x] > 0.0, 1.0 / (storage[x] + stabilize + total), 0.0)
        inverse[x] = inv
        fixed[x] = source[x] + storage[x] * start[x]
        for face in range(6):
            coef[face, x] = coef[face, x] * inv


def one_sweep(src, dst, coef, rhs):
    for x in range(PLANES):
        p = src[x]
        total = rhs[x] + coef[0, x] * above(src, x) + coef[1, x] * below(src, x)
        total = total + coef[2, x] * roll(p, 31, 0) + coef[3, x] * roll(p, 1, 0)
        dst[x] = total + coef[4, x] * roll(p, 127) + coef[5, x] * roll(p, 1)


def sweeps(press, coef, rhs):
    def two(_, carry):
        one_sweep(press.at[0], press.at[1], coef, rhs)
        one_sweep(press.at[1], press.at[0], coef, rhs)
        return carry

    lax.fori_loop(0, SWEEPS // 2, two, 0)


def pair_matrix():
    cell = rows((128, 256))
    n = lanes((128, 256))
    hit = (cell // 2 % 32 == n % 32) & (cell // 64 == n // 128)
    return jnp.where(hit, 0.125, 0.0).astype(bf16)


def row_mask(shape):
    return lanes(shape) % 128 // 32 == rows(shape) % 8 // 2


def block_means(press, means):
    sums = jnp.concatenate([press[2 * q] + press[2 * q + 1] for q in range(7)], axis=0)
    matrix = pair_matrix()
    got = jnp.zeros((224, 256), f32)
    for part in three_parts(sums):
        got = got + jnp.dot(part, matrix, preferred_element_type=f32)
    got = jnp.where(row_mask((224, 256)), got, 0.0)
    for b in range(4, 11):
        piece = got[32 * (b % 7) : 32 * (b % 7) + 32, 128 * (b // 7) : 128 * (b // 7) + 128]
        for y in range(4):
            means[b, 0:1, 128 * y : 128 * y + 128] = jnp.sum(piece[8 * y : 8 * y + 8], axis=0, keepdims=True)


def last_row(shape):
    return lanes(shape) // 32 % 16 == 15


def corner_rolls(u):
    last = last_row(u.shape)
    return [
        u,
        roll(u, 511),
        jnp.where(last, 0.0, roll(u, 480)),
        jnp.where(last, 0.0, roll(u, 479)),
    ]


def assembled(here, under):
    summed = here[0:32] + under[32:64]
    last = last_row((8, 512))
    return (
        summed[0:8]
        + roll(summed[8:16], 1)
        + roll(jnp.where(last, 0.0, summed[16:24]), 32)
        + roll(jnp.where(last, 0.0, summed[24:32]), 33)
    )


def diag_of(lam, mu, sup, aux, safe, gain):
    depth = lanes((8, 512)) % 32
    inside = (depth >= 6) & (depth < 26)
    terms = {}
    for b in range(4, 11):
        terms[b] = aux[:, 1:2] * lam[b] + aux[:, 2:3] * mu[b]
        if b > 4:
            node_sup = sup[b]
            total = node_sup + assembled(terms[b], terms[b - 1])
            valid = inside & (node_sup > 0.0)
            safe[b] = jnp.where(valid, total, 1.0)
            gain[b] = jnp.where(valid, damping, 0.0)


def stiff_parts(stiff):
    high = stiff.astype(bf16)
    low = (stiff - high.astype(f32)).astype(bf16)
    return jnp.concatenate([high, high, low], axis=1)


def element_terms(matrix, coupling, v_here, v_next, lam, mu, press):
    vals = jnp.concatenate(v_here + v_next, axis=0)
    high = vals.astype(bf16)
    low = (vals - high.astype(f32)).astype(bf16)
    both = jnp.dot(matrix, jnp.concatenate([high, low, high], axis=0), preferred_element_type=f32)
    return coupling * (biot_coef * press) - (lam * both[0:64] + mu * both[64:128])


def displacements(u, lam, mu, load, sup, safe, gain, means, stiff, aux, moved):
    matrix = stiff_parts(stiff[...])
    coupling = aux[:, 0:1]

    def half(old, new, least, most):
        under = None
        v_here = corner_rolls(old[least - 1])
        for b in range(least - 1, most + 1):
            v_next = corner_rolls(old[b + 1])
            terms = element_terms(matrix, coupling, v_here, v_next, lam[b], mu[b], means[b])
            if b >= least:
                value = old[b]
                residual = load[b] - sup[b] * value + assembled(terms, under)
                new[b] = value + gain[b] * residual / safe[b]
            under = terms
            v_here = v_next

    half(u, moved.at[0], 5, 10)
    half(moved.at[0], moved.at[1], 6, 9)


def pack_mid(press, moved, out):
    low = low_mask((32, 128))
    pairs = [
        jnp.where(low, press[12], press[2]),
        jnp.where(low, press[13], press[3]),
        jnp.where(low, roll(press[0], 64), press[4]),
        jnp.where(low, roll(press[1], 64), press[5]),
    ]
    for y in range(4):
        for q in range(4):
            out[y, q] = pairs[q][8 * y : 8 * y + 8]
            out[y, 4 + q] = moved[1, 6 + q, :, 128 * y : 128 * y + 128]


def pack_last(press, moved, out):
    low = low_mask((32, 128))
    pairs = [
        jnp.where(low, press[12], roll(press[13], 64)),
        jnp.where(low, roll(press[0], 64), press[1]),
        jnp.where(low, roll(press[2], 64), press[3]),
        jnp.where(low, roll(press[4], 64), press[5]),
    ]
    for x in range(2):
        for y in range(4):
            for i in range(2):
                out[4 * x + y, i] = pairs[2 * x + i][8 * y : 8 * y + 8]
                out[4 * x + y, 2 + i] = moved[1, 6 + 2 * x + i, :, 128 * y : 128 * y + 128]


def first_kernel(
    core, grid, halo, share, stiff, aux,
    mid, coef, fixed, inverse, u, lam, mu, load, sup, safe, gain,
    press, storage, perm, rhs, means, moved,
):
    low = low_mask((32, 128))

    def unpack(units):
        def tile(cell, at):
            ref, unit = units[cell // 4]
            return ref[4 * unit : 4 * unit + 4, at + cell % 4].reshape(32, 128)

        for x in range(PLANES):
            a = tile(x, 0)
            b = tile(x + PLANES, 0)
            press[0, x] = jnp.where(low, a, roll(b, 64))
            rhs[x] = jnp.where(low, roll(a, 64), b)
            a = tile(x, 4)
            b = tile(x + PLANES, 4)
            storage[x] = jnp.where(low, a, roll(b, 64))
            perm[x] = jnp.where(low, roll(a, 64), b)
        sub = rows((8, 128))
        for n in range(NODES):
            ref, unit = units[n // 2]
            for y in range(4):
                at = slice(128 * y, 128 * y + 128)
                tile_a = ref[4 * unit + y, 8 + 2 * (n % 2)]
                u[n, :, at] = jnp.where(sub < 3, tile_a, 0.0)
                if 4 <= n <= 10:
                    tile_b = ref[4 * unit + y, 9 + 2 * (n % 2)]
                    load[n, :, at] = jnp.where(sub < 3, pltpu.roll(tile_a, 4, 0), 0.0)
                    sup[n, :, at] = jnp.where(sub < 3, tile_b, 0.0)
                    lam[n, :, at] = tile_a[7:8]
                    mu[n, :, at] = tile_b[7:8]

    places = [
        [(halo, 0), (halo, 1), (halo, 2), (grid, 0), (grid, 1), (grid, 2), (grid, 3), (share, 0)],
        [(share, 0), (grid, 0), (grid, 1), (grid, 2), (grid, 3), (halo, 0), (halo, 1), (halo, 2)],
    ]
    window(core, places, unpack)
    cell_coefs(press.at[0], rhs, storage, perm, coef, fixed, inverse)
    for x in range(PLANES):
        rhs[x] = (fixed[x] + stabilize * press[0, x]) * inverse[x]
    sweeps(press, coef, rhs)
    block_means(press.at[0], means)
    diag_of(lam, mu, sup, aux, safe, gain)
    displacements(u, lam, mu, load, sup, safe, gain, means, stiff, aux, moved)
    pack_mid(press.at[0], moved, mid)


def second_kernel(
    core, own, partner, halo, far, across, stiff, aux,
    coef, fixed, inverse, start, lam, mu, load, sup, safe, gain,
    last, press, rhs, means, u, strain, moved,
):
    low = low_mask((32, 128))

    def unpack(units):
        def piece(cell, want_low):
            k = cell + 4
            ref, k = units[k // 8], k % 8
            value = ref[:, k % 4].reshape(32, 128)
            return value if (k < 4) == want_low else roll(value, 64)

        for x in range(PLANES):
            press[0, x] = jnp.where(low, piece(x, True), piece(x + PLANES, False))
        for n in range(NODES):
            k = n + 2
            ref = units[k // 4]
            for y in range(4):
                u[n, :, 128 * y : 128 * y + 128] = ref[y, 4 + k % 4]

    window(core, [[far, halo, own, partner, across], [across, partner, own, halo, far]], unpack)

    strain[...] = jnp.zeros((PLANES, 1, 512), f32)
    last_y = last_row((8, 512))
    here = u[1] - start[1]
    for b in range(1, 14):
        following = u[b + 1] - start[b + 1]
        parts = [
            aux[8 * a : 8 * a + 8, 0:1] * here + aux[32 + 8 * a : 40 + 8 * a, 0:1] * following
            for a in range(4)
        ]
        total = (
            parts[0]
            + roll(parts[1], 511)
            + jnp.where(last_y, 0.0, roll(parts[2], 480) + roll(parts[3], 479))
        )
        strain[b] = jnp.sum(total, axis=0, keepdims=True)
        here = following
    mask = row_mask((8, 128))
    spread = []
    for q in range(7):
        for y in range(4):
            at = slice(128 * y, 128 * y + 128)
            spread.append(
                jnp.concatenate(
                    [jnp.where(mask, strain[q, :, at], 0.0), jnp.where(mask, strain[7 + q, :, at], 0.0)],
                    axis=1,
                )
            )
    matrix = pair_matrix()
    got = jnp.zeros((224, 128), f32)
    for part in three_parts(jnp.concatenate(spread, axis=0)):
        got = got + nt_dot(part, matrix)
    for x in range(PLANES):
        change = got[32 * (x // 2) : 32 * (x // 2) + 32]
        right = fixed[x] + stabilize * press[0, x] - (8.0 * biot_coef) * change
        rhs[x] = right * inverse[x]
    sweeps(press, coef, rhs)
    block_means(press.at[0], means)
    displacements(u, lam, mu, load, sup, safe, gain, means, stiff, aux, moved)
    pack_last(press.at[0], moved, last)


def unpack_kernel(core, got, pressure, disp, held):
    lane = lanes((8, 128))
    base = core[0] * 8
    for i in range(4):
        total = jnp.zeros((8, 128), f32)
        for s in range(8):
            tile = got[base + s, i // 2]
            total = jnp.where(lane // 16 == s, roll(tile, 16 * s - 24 - 64 * (i % 2)), total)
        pressure[i] = total
    for i in range(2):
        for pair in range(2):
            total = jnp.zeros((8, 128), f32)
            for s in range(8):
                tile = got[base + s, 2 + i]
                for side in range(2):
                    shift = 64 * side + 8 * s - 32 * (2 * pair + side) - 12
                    total = jnp.where(lane // 8 == 8 * side + s, roll(tile, shift), total)
            held[:, 128 * (2 * i + pair) : 128 * (2 * i + pair) + 128] = total
    disp[...] = held[0:3]


def corner_major(stiff):
    grid = stiff.reshape(3, 8, 3, 8).transpose(1, 0, 3, 2)
    return jnp.pad(grid, ((0, 0), (0, 5), (0, 0), (0, 5))).reshape(64, 64)


def corner_column(vec):
    return jnp.pad(vec.reshape(3, 8).T, ((0, 0), (0, 5))).reshape(64)


def shape(*dims):
    return jax.ShapeDtypeStruct(dims, f32)


def shards(
    pressure_start, source, storage, perm_class, class_perm, block_route, displacement_start,
    load, support, lame_lambda, lame_mu, stiff_lambda, stiff_mu, coupling_vec,
):
    core = lax.axis_index("grp")
    core_arg = jnp.full((1,), core, jnp.int32)
    swap = [(0, 1), (1, 0)]

    cells, nodes, elems = call(
        stage_kernel,
        (shape(16, 8, 128), shape(16, 512), shape(8, 8, 128)),
        [SM] + [VM] * 9,
    )(class_perm, pressure_start, source, storage, perm_class, displacement_start, load, support,
      lame_lambda, lame_mu)
    routed = lax.all_to_all(elems, ("grp", "gy"), 0, 0, tiled=True)
    cells_other = lax.ppermute(cells, "grp", swap)
    nodes_other = lax.ppermute(nodes, "grp", swap)
    routes = lax.dynamic_index_in_dim(
        block_route[0].reshape(2, 4, 512), lax.axis_index("gy"), 1, keepdims=False
    )
    packed = call(
        pack_kernel, shape(16, 12, 8, 128), [SM] + [VM] * 6, [pltpu.VMEM((4, 8, 512), f32)]
    )(core_arg, cells, cells_other, nodes, nodes_other, routed, routes)
    grid = lax.all_to_all(packed, ("gx", "gy"), 0, 0, tiled=True)

    chain = [((0, z), (1, z - 1)) for z in range(1, 8)] + [((1, z - 1), (0, z)) for z in range(1, 8)]
    pairs = [(a[0] * 8 + a[1], b[0] * 8 + b[1]) for b, a in chain]
    halo = lax.ppermute(lax.dynamic_slice_in_dim(grid, 4 * core, 12, 0), ("grp", "gz"), pairs)
    share = lax.ppermute(lax.dynamic_slice_in_dim(halo, 8 * (1 - core), 4, 0), "grp", swap)

    stiff = jnp.concatenate([corner_major(stiff_lambda), corner_major(stiff_mu)], axis=0)
    columns = [corner_column(coupling_vec), corner_column(jnp.diag(stiff_lambda)), corner_column(jnp.diag(stiff_mu))]
    aux = jnp.pad(jnp.stack(columns, axis=1), ((0, 0), (0, 125)))

    kept = (
        shape(6, PLANES, 32, 128), shape(PLANES, 32, 128), shape(PLANES, 32, 128),
        shape(NODES, 8, 512), shape(11, 1, 512), shape(11, 1, 512), shape(11, 8, 512),
        shape(11, 8, 512), shape(11, 8, 512), shape(11, 8, 512),
    )
    mid, *statics = call(
        first_kernel,
        (shape(4, 8, 8, 128),) + kept,
        [SM] + [VM] * 5,
        [
            pltpu.VMEM((2, PLANES, 32, 128), f32),
            pltpu.VMEM((PLANES, 32, 128), f32),
            pltpu.VMEM((PLANES, 32, 128), f32),
            pltpu.VMEM((PLANES, 32, 128), f32),
            pltpu.VMEM((PLANES, 1, 512), f32),
            pltpu.VMEM((2, NODES, 8, 512), f32),
        ],
    )(core_arg, grid, halo, share, stiff, aux)

    partner = lax.ppermute(mid, "grp", swap)
    moved = lax.ppermute(jnp.stack([mid, partner]), ("grp", "gz"), pairs)
    near, far = moved[0], moved[1]
    across = lax.ppermute(near, "grp", swap)
    last = call(
        second_kernel,
        shape(8, 4, 8, 128),
        [SM] + [VM] * 17,
        [
            pltpu.VMEM((2, PLANES, 32, 128), f32),
            pltpu.VMEM((PLANES, 32, 128), f32),
            pltpu.VMEM((PLANES, 1, 512), f32),
            pltpu.VMEM((NODES, 8, 512), f32),
            pltpu.VMEM((PLANES, 1, 512), f32),
            pltpu.VMEM((2, NODES, 8, 512), f32),
        ],
    )(core_arg, mid, partner, near, far, across, stiff, aux, *statics)

    other = lax.ppermute(last, "grp", swap)
    whole = jnp.concatenate([jnp.where(core == 0, last, other), jnp.where(core == 0, other, last)], axis=0)
    back = lax.all_to_all(whole, ("gx", "gy"), 0, 0, tiled=True)
    return call(
        unpack_kernel,
        (shape(4, 8, 128), shape(3, 512)),
        [SM, VM],
        [pltpu.VMEM((8, 512), f32)],
    )(core_arg, back)


def solution(mesh):
    fine = Mesh(np.asarray(mesh.devices).reshape(2, 8, 4, 4), ("grp", "gz", "gx", "gy"))
    cell = P(("gz", "gx"), "gy", "grp")
    node = P(None, ("grp", "gz", "gx", "gy"))
    elem = P(("grp", "gz", "gx", "gy"), None)
    return jax.shard_map(
        shards,
        mesh=fine,
        in_specs=(
            cell, cell, cell, cell, P(), P(("gz", "gx"), None, None), node, node, node, elem, elem,
            P(), P(), P(),
        ),
        out_specs=(cell, node),
        check_vma=False,
    )
```

```python
import jax
import jax.numpy as jnp
import numpy as np
from jax import lax
from jax.experimental import pallas as pl
from jax.experimental.pallas import tpu as pltpu
from jax.sharding import Mesh
from jax.sharding import PartitionSpec as P

SWEEPS = 6
CLASSES = 16
CHIPS = 16
PLANES = 16
NODES = 16
TILES = 13

stabilize = 0.5
biot_coef = 0.8
damping = 0.7
tiny = 1e-30

f32 = jnp.float32
bf16 = jnp.bfloat16

VM = pl.BlockSpec(memory_space=pltpu.VMEM)
SM = pl.BlockSpec(memory_space=pltpu.SMEM)


def call(body, out_shapes, in_specs, scratch=(), budget=40 * 1024 * 1024):
    return pl.pallas_call(
        body,
        out_shape=out_shapes,
        in_specs=in_specs,
        out_specs=jax.tree.map(lambda _: VM, out_shapes),
        scratch_shapes=list(scratch),
        compiler_params=pltpu.CompilerParams(vmem_limit_bytes=budget),
    )


def lanes(shape):
    return lax.broadcasted_iota(jnp.int32, shape, 1)


def rows(shape):
    return lax.broadcasted_iota(jnp.int32, shape, 0)


def roll(x, shift, axis=1):
    shift = shift % x.shape[axis]
    return x if shift == 0 else pltpu.roll(x, shift, axis)


def three_parts(x):
    high = x.astype(bf16)
    rest = x - high.astype(f32)
    middle = rest.astype(bf16)
    return high, middle, (rest - middle.astype(f32)).astype(bf16)


def nt_dot(a, b):
    return lax.dot_general(a, b, (((1,), (1,)), ((), ())), preferred_element_type=f32)


def stage_kernel(perms, p0, src, sto, cls, disp, load, sup, lam, mu, cells, nodes, held, small, pair, classes, sems):
    copies = [
        pltpu.make_async_copy(perms, classes, sems.at[9]),
        pltpu.make_async_copy(p0, cells.at[0:4], sems.at[0]),
        pltpu.make_async_copy(src, cells.at[4:8], sems.at[1]),
        pltpu.make_async_copy(sto, cells.at[8:12], sems.at[2]),
        pltpu.make_async_copy(cls, held, sems.at[3]),
        pltpu.make_async_copy(disp, small.at[0], sems.at[4]),
        pltpu.make_async_copy(load, small.at[1], sems.at[5]),
        pltpu.make_async_copy(sup, small.at[2], sems.at[6]),
        pltpu.make_async_copy(lam, pair.at[0], sems.at[7]),
        pltpu.make_async_copy(mu, pair.at[1], sems.at[8]),
    ]
    for copy in copies:
        copy.start()
    nodes[...] = jnp.zeros((16, 512), f32)
    for copy in copies:
        copy.wait()
    for i in range(4):
        which = held[i]
        perm = jnp.zeros((8, 128), f32)
        for member in range(CLASSES):
            perm = jnp.where(which == member, classes[member], perm)
        cells[12 + i] = perm
    nodes[0:3] = small[0]
    nodes[3:4] = pair[0]
    nodes[4:7] = small[1]
    nodes[7:8] = pair[1]
    nodes[8:11] = small[2]


def pack_kernel(core, cells, cells_other, nodes, nodes_other, routes, out):
    first = core[0] == 0
    lane = lanes((8, 128))
    low = lane < 64
    sub = rows((8, 128))

    placed = jnp.zeros((192, 128), f32)
    device = lanes((1, 512)) // 64
    for half in range(2):
        block = routes[half : half + 1, :]
        row = block // 64 % 4 * 8 + block // 256 * 4 + device % 4
        depth = device // 4 * 64 + block % 64
        at_row = rows((32, 512)) == row
        at_depth = jnp.where(rows((128, 512)) == depth, 1.0, 0.0).astype(bf16)
        spread = []
        for source in (3, 7):
            own = nodes[source : source + 1, :]
            other = nodes_other[source : source + 1, :]
            value = jnp.where(first, own, other) if half == 0 else jnp.where(first, other, own)
            for part in three_parts(value):
                spread.append(jnp.where(at_row, part.astype(f32), 0.0))
        placed = placed + nt_dot(jnp.concatenate(spread, axis=0).astype(bf16), at_depth)
    grids = [placed[96 * v : 96 * v + 32] + placed[96 * v + 32 : 96 * v + 64] + placed[96 * v + 64 : 96 * v + 96] for v in range(2)]

    for pair in range(2):
        for i in range(4):
            tiles = []
            for field in (2 * pair, 2 * pair + 1):
                own = cells[4 * field + i]
                other = cells_other[4 * field + i]
                tiles.append((jnp.where(first, own, other), jnp.where(first, other, own)))
            for chip in range(CHIPS):
                start = 16 * chip - 24
                spot = lane % 64 + start
                in_low = (spot >= 0) & (spot < 128)
                in_high = (spot >= 128) & (spot < 256)
                found = []
                for member in range(2):
                    shift = 64 * member - start
                    win = jnp.zeros((8, 128), f32)
                    if start < 128:
                        win = jnp.where(in_low, roll(tiles[member][0], shift), win)
                    if start + 64 > 128:
                        win = jnp.where(in_high, roll(tiles[member][1], shift), win)
                    found.append(win)
                out[chip, 4 * pair + i] = jnp.where(low, found[0], found[1])

    def full_depth(i, r):
        full = []
        for j in range(4):
            at = (i * 4 + j) // 2 * 128
            own = nodes[8 * r : 8 * r + 8, at : at + 128]
            other = nodes_other[8 * r : 8 * r + 8, at : at + 128]
            near = jnp.where(first, own, other)
            deep = jnp.where(first, other, own)
            if j % 2 == 0:
                full.append(jnp.where(low, near, roll(deep, 64)))
            else:
                full.append(jnp.where(low, roll(near, 64), deep))
        return full

    supports = [jnp.where(sub < 4, a, pltpu.roll(b, 4, 0)) for a, b in zip(full_depth(0, 1), full_depth(1, 1))]
    members = [full_depth(0, 0), full_depth(1, 0), supports]
    members += [[grid[8 * j : 8 * j + 8] for j in range(4)] for grid in grids]
    for at, full in enumerate(members):
        for chip in range(CHIPS):
            start = 8 * chip - 12
            spot = lane % 32 + start
            tile = jnp.zeros((8, 128), f32)
            for j in range(4):
                tile = jnp.where(lane // 32 == j, roll(full[j], 32 * j - start), tile)
            out[chip, 8 + at] = jnp.where((spot >= 0) & (spot < 128), tile, 0.0)


def low_mask(shape):
    return lanes(shape) < 64


def above(ref, x):
    return ref[x + 1] if x < PLANES - 1 else roll(ref[0], 64)


def below(ref, x):
    return ref[x - 1] if x > 0 else roll(ref[PLANES - 1], 64)


def window(core, places, then):
    for c in range(2):
        @pl.when(core[0] == c)
        def _():
            then(places[c])


def cell_coefs(start, source, storage, perm, coef, fixed, inverse):
    keep_top = rows((32, 128)) < 31
    for x in range(PLANES):
        p = perm[x]
        q = above(perm, x)
        coef[0, x] = 2.0 * p * q / jnp.maximum(p + q, tiny)
        q = roll(p, 31, 0)
        coef[2, x] = jnp.where(keep_top, 2.0 * p * q / jnp.maximum(p + q, tiny), 0.0)
        q = roll(p, 127)
        coef[4, x] = 2.0 * p * q / jnp.maximum(p + q, tiny)
    for x in range(PLANES):
        coef[1, x] = coef[0, x - 1] if x > 0 else roll(coef[0, PLANES - 1], 64)
        coef[3, x] = roll(coef[2, x], 1, 0)
        coef[5, x] = roll(coef[4, x], 1)
    for x in range(PLANES):
        total = coef[0, x] + coef[1, x] + coef[2, x] + coef[3, x] + coef[4, x] + coef[5, x]
        inv = jnp.where(storage[x] > 0.0, 1.0 / (storage[x] + stabilize + total), 0.0)
        inverse[x] = inv
        fixed[x] = source[x] + storage[x] * start[x]
        for face in range(6):
            coef[face, x] = coef[face, x] * inv


def one_sweep(src, dst, coef, rhs):
    for x in range(PLANES):
        p = src[x]
        total = rhs[x] + coef[0, x] * above(src, x) + coef[1, x] * below(src, x)
        total = total + coef[2, x] * roll(p, 31, 0) + coef[3, x] * roll(p, 1, 0)
        dst[x] = total + coef[4, x] * roll(p, 127) + coef[5, x] * roll(p, 1)


def sweeps(press, coef, rhs):
    def two(_, carry):
        one_sweep(press.at[0], press.at[1], coef, rhs)
        one_sweep(press.at[1], press.at[0], coef, rhs)
        return carry

    lax.fori_loop(0, SWEEPS // 2, two, 0)


def pair_matrix():
    cell = rows((128, 256))
    n = lanes((128, 256))
    hit = (cell // 2 % 32 == n % 32) & (cell // 64 == n // 128)
    return jnp.where(hit, 0.125, 0.0).astype(bf16)


def row_mask(shape):
    return lanes(shape) % 128 // 32 == rows(shape) % 8 // 2


def block_means(press, means):
    sums = jnp.concatenate([press[2 * q] + press[2 * q + 1] for q in range(8)], axis=0)
    matrix = pair_matrix()
    got = jnp.zeros((256, 256), f32)
    for part in three_parts(sums):
        got = got + jnp.dot(part, matrix, preferred_element_type=f32)
    got = jnp.where(row_mask((256, 256)), got, 0.0)
    for b in range(3, 12):
        piece = got[32 * (b % 8) : 32 * (b % 8) + 32, 128 * (b // 8) : 128 * (b // 8) + 128]
        for y in range(4):
            means[b, 0:1, 128 * y : 128 * y + 128] = jnp.sum(piece[8 * y : 8 * y + 8], axis=0, keepdims=True)


def last_row(shape):
    return lanes(shape) // 32 % 16 == 15


def corner_rolls(u):
    last = last_row(u.shape)
    return [
        u,
        roll(u, 511),
        jnp.where(last, 0.0, roll(u, 480)),
        jnp.where(last, 0.0, roll(u, 479)),
    ]


def assembled(here, under):
    summed = here[0:32] + under[32:64]
    last = last_row((8, 512))
    return (
        summed[0:8]
        + roll(summed[8:16], 1)
        + roll(jnp.where(last, 0.0, summed[16:24]), 32)
        + roll(jnp.where(last, 0.0, summed[24:32]), 33)
    )


def diag_of(lam, mu, sup, aux, safe, gain):
    depth = lanes((8, 512)) % 32
    inside = (depth >= 6) & (depth < 26)
    terms = {}
    for b in range(3, 12):
        terms[b] = aux[:, 1:2] * lam[b] + aux[:, 2:3] * mu[b]
        if b > 3:
            node_sup = sup[b]
            total = node_sup + assembled(terms[b], terms[b - 1])
            valid = inside & (node_sup > 0.0)
            safe[b] = jnp.where(valid, total, 1.0)
            gain[b] = jnp.where(valid, damping, 0.0)


def stiff_parts(stiff):
    high = stiff.astype(bf16)
    low = (stiff - high.astype(f32)).astype(bf16)
    return jnp.concatenate([high, high, low], axis=1)


def element_terms(matrix, coupling, v_here, v_next, lam, mu, press):
    vals = jnp.concatenate(v_here + v_next, axis=0)
    high = vals.astype(bf16)
    low = (vals - high.astype(f32)).astype(bf16)
    both = jnp.dot(matrix, jnp.concatenate([high, low, high], axis=0), preferred_element_type=f32)
    return coupling * (biot_coef * press) - (lam * both[0:64] + mu * both[64:128])


def displacements(u, lam, mu, load, sup, safe, gain, means, stiff, aux, moved, least, most):
    matrix = stiff_parts(stiff[...])
    coupling = aux[:, 0:1]

    def half(old, new, least, most):
        under = None
        v_here = corner_rolls(old[least - 1])
        for b in range(least - 1, most + 1):
            v_next = corner_rolls(old[b + 1])
            terms = element_terms(matrix, coupling, v_here, v_next, lam[b], mu[b], means[b])
            if b >= least:
                value = old[b]
                residual = load[b] - sup[b] * value + assembled(terms, under)
                new[b] = value + gain[b] * residual / safe[b]
            under = terms
            v_here = v_next

    half(u, moved.at[0], least - 1, most + 1)
    half(moved.at[0], moved.at[1], least, most)


def pack_mid(core, press, moved, out):
    low = low_mask((32, 128))
    pairs = [jnp.where(low, press[12 + q], press[q]) for q in range(4)]
    extra = jnp.where(low, press[10], roll(press[11], 64))
    node = jnp.where(core[0] == 0, moved[1, 10], moved[1, 5])
    for y in range(4):
        for q in range(4):
            out[y, q] = pairs[q][8 * y : 8 * y + 8]
            out[y, 4 + q] = moved[1, 6 + q, :, 128 * y : 128 * y + 128]
        out[y, 8] = extra[8 * y : 8 * y + 8]
        out[y, 9] = node[:, 128 * y : 128 * y + 128]


def pack_last(press, moved, out):
    lane = lanes((32, 128))
    for x in range(2):
        cells = jnp.zeros((32, 128), f32)
        for i in range(4):
            if x == 0:
                tile = roll(press[12 + i], 16 * i - 24)
            else:
                tile = roll(press[i], 16 * i - 88)
            cells = jnp.where(lane // 16 == i, tile, cells)
        for y in range(4):
            total = cells[8 * y : 8 * y + 8]
            for i in range(2):
                tile = moved[1, 6 + 2 * x + i, :, 128 * y : 128 * y + 128]
                for j in range(4):
                    total = jnp.where(lane[0:8] // 8 == 8 + 4 * i + j, roll(tile, 52 + 32 * i - 24 * j), total)
            out[4 * x + y] = total


def first_kernel(
    core, ok, grid, halo, share, stiff, aux,
    mid, coef, fixed, inverse, u, lam, mu, load, sup, safe, gain,
    press, storage, perm, rhs, means, moved,
):
    low = low_mask((32, 128))

    def unpack(units):
        def read(unit, y, at):
            ref, index, flag = units[unit]
            value = ref[4 * index + y, at] if y is not None else ref[4 * index : 4 * index + 4, at]
            return value if flag is None else value * ok[flag]

        def tile(cell, at):
            return read(cell // 4, None, at + cell % 4).reshape(32, 128)

        for x in range(PLANES):
            a = tile(x, 0)
            b = tile(x + PLANES, 0)
            press[0, x] = jnp.where(low, a, roll(b, 64))
            rhs[x] = jnp.where(low, roll(a, 64), b)
            a = tile(x, 4)
            b = tile(x + PLANES, 4)
            storage[x] = jnp.where(low, a, roll(b, 64))
            perm[x] = jnp.where(low, roll(a, 64), b)
        sub = rows((8, 128))
        for unit in range(8):
            for y in range(4):
                at = slice(128 * y, 128 * y + 128)
                support = read(unit, y, 10)
                for i in range(2):
                    n = 2 * unit + i
                    tile_a = read(unit, y, 8 + i)
                    u[n, :, at] = jnp.where(sub < 3, tile_a, 0.0)
                    if 4 <= n <= 11:
                        load[n, :, at] = jnp.where(sub < 3, pltpu.roll(tile_a, 4, 0), 0.0)
                        tile_b = support if i == 0 else pltpu.roll(support, 4, 0)
                        sup[n, :, at] = jnp.where(sub < 3, tile_b, 0.0)
            if 1 <= unit <= 5:
                for at, param in ((11, lam), (12, mu)):
                    total = read(unit, 0, at) + read(unit, 1, at) + read(unit, 2, at) + read(unit, 3, at)
                    for i in range(2):
                        for y in range(4):
                            row = 4 * i + y
                            param[2 * unit + i, :, 128 * y : 128 * y + 128] = total[row : row + 1]

    below = [(halo, 0, 0), (halo, 1, 0), (halo, 2, 0)]
    plane = [(grid, 0, None), (grid, 1, None), (grid, 2, None), (grid, 3, None)]
    beside = [(share, 0, 1)]
    window(core, [below + plane + beside, beside + plane + below], unpack)
    cell_coefs(press.at[0], rhs, storage, perm, coef, fixed, inverse)
    for x in range(PLANES):
        rhs[x] = (fixed[x] + stabilize * press[0, x]) * inverse[x]
    sweeps(press, coef, rhs)
    block_means(press.at[0], means)
    diag_of(lam, mu, sup, aux, safe, gain)
    displacements(u, lam, mu, load, sup, safe, gain, means, stiff, aux, moved, 5, 10)
    pack_mid(core, press.at[0], moved, mid)


def second_kernel(
    core, ok, own, partner, near, across, stiff, aux,
    coef, fixed, inverse, start, lam, mu, load, sup, safe, gain,
    last, press, rhs, means, u, strain, moved,
):
    low = low_mask((32, 128))

    def unpack(runs, extra):
        def piece(cell, want_low):
            if cell in extra["cells"]:
                ref, q, is_low = extra["cells"][cell]
            elif 4 <= cell < 28:
                k = (cell - 4) % 8
                ref, q, is_low = runs[(cell - 4) // 8][0], k % 4, k < 4
            else:
                return jnp.zeros((32, 128), f32)
            value = ref[:, q].reshape(32, 128)
            return value if is_low == want_low else roll(value, 64)

        for x in range(PLANES):
            press[0, x] = jnp.where(low, piece(x, True), piece(x + PLANES, False))
        for n in range(NODES):
            if n in extra["nodes"]:
                ref, q, flag = extra["nodes"][n]
            elif 2 <= n < 14:
                (ref, flag), q = runs[(n - 2) // 4], 4 + (n - 2) % 4
            else:
                u[n] = jnp.zeros((8, 512), f32)
                continue
            for y in range(4):
                value = ref[y, q]
                u[n, :, 128 * y : 128 * y + 128] = value if flag is None else value * ok[flag]

    @pl.when(core[0] == 0)
    def _():
        unpack(
            [(near, 0), (own, None), (partner, None)],
            {"cells": {2: (near, 8, True), 3: (near, 8, False)}, "nodes": {1: (near, 9, 0), 14: (across, 4, 1)}},
        )

    @pl.when(core[0] == 1)
    def _():
        unpack(
            [(partner, None), (own, None), (near, 0)],
            {"cells": {2: (across, 2, False), 3: (across, 3, False)}, "nodes": {1: (across, 7, 1), 14: (near, 9, 0)}},
        )

    strain[...] = jnp.zeros((PLANES, 1, 512), f32)
    last_y = last_row((8, 512))
    here = u[1] - start[1]
    for b in range(1, 14):
        following = u[b + 1] - start[b + 1]
        parts = [
            aux[8 * a : 8 * a + 8, 0:1] * here + aux[32 + 8 * a : 40 + 8 * a, 0:1] * following
            for a in range(4)
        ]
        total = (
            parts[0]
            + roll(parts[1], 511)
            + jnp.where(last_y, 0.0, roll(parts[2], 480) + roll(parts[3], 479))
        )
        strain[b] = jnp.sum(total, axis=0, keepdims=True)
        here = following
    mask = row_mask((8, 128))
    spread = []
    for q in range(8):
        for y in range(4):
            at = slice(128 * y, 128 * y + 128)
            spread.append(
                jnp.concatenate(
                    [jnp.where(mask, strain[q, :, at], 0.0), jnp.where(mask, strain[8 + q, :, at], 0.0)],
                    axis=1,
                )
            )
    matrix = pair_matrix()
    got = jnp.zeros((256, 128), f32)
    for part in three_parts(jnp.concatenate(spread, axis=0)):
        got = got + nt_dot(part, matrix)
    for x in range(PLANES):
        change = got[32 * (x // 2) : 32 * (x // 2) + 32]
        right = fixed[x] + stabilize * press[0, x] - (8.0 * biot_coef) * change
        rhs[x] = right * inverse[x]
    sweeps(press, coef, rhs)
    block_means(press.at[0], means)
    displacements(u, lam, mu, load, sup, safe, gain, means, stiff, aux, moved, 6, 9)
    pack_last(press.at[0], moved, last)


def unpack_kernel(core, got, pressure, disp, held):
    lane = lanes((8, 128))
    base = core[0] * 8
    tiles = [got[base + s] for s in range(8)]
    for i in range(4):
        total = jnp.zeros((8, 128), f32)
        for s in range(8):
            total = jnp.where(lane // 16 == s, roll(tiles[s], 16 * s - 16 * i), total)
        pressure[i] = total
    for i in range(2):
        for pair in range(2):
            total = jnp.zeros((8, 128), f32)
            for s in range(8):
                for side in range(2):
                    shift = 64 * side + 8 * s - 64 - 32 * i - 8 * (2 * pair + side)
                    total = jnp.where(lane // 8 == 8 * side + s, roll(tiles[s], shift), total)
            held[:, 128 * (2 * i + pair) : 128 * (2 * i + pair) + 128] = total
    disp[...] = held[0:3]


def corner_major(stiff):
    grid = stiff.reshape(3, 8, 3, 8).transpose(1, 0, 3, 2)
    return jnp.pad(grid, ((0, 0), (0, 5), (0, 0), (0, 5))).reshape(64, 64)


def corner_column(vec):
    return jnp.pad(vec.reshape(3, 8).T, ((0, 0), (0, 5))).reshape(64)


def shape(*dims):
    return jax.ShapeDtypeStruct(dims, f32)


def shards(
    pressure_start, source, storage, perm_class, class_perm, block_route, displacement_start,
    load, support, lame_lambda, lame_mu, stiff_lambda, stiff_mu, coupling_vec,
):
    core = lax.axis_index("grp")
    layer = lax.axis_index("gz")
    core_arg = jnp.full((1,), core, jnp.int32)
    has_below, has_above = layer > 0, layer < 7
    ok = jnp.stack(
        [jnp.where(core == 0, has_below, has_above), jnp.where(core == 0, has_above, has_below)]
    ).astype(f32)
    swap = [(0, 1), (1, 0)]

    cells, nodes = call(
        stage_kernel,
        (shape(16, 8, 128), shape(16, 512)),
        [pl.BlockSpec(memory_space=pltpu.HBM)] * 10,
        [
            pltpu.VMEM((4, 8, 128), jnp.int32),
            pltpu.VMEM((3, 3, 512), f32),
            pltpu.VMEM((2, 1, 512), f32),
            pltpu.SMEM((CLASSES,), f32),
            pltpu.SemaphoreType.DMA((10,)),
        ],
        64 * 1024 * 1024 - 65536,
    )(class_perm, pressure_start, source, storage, perm_class, displacement_start, load, support,
      lame_lambda, lame_mu)
    cells_other = lax.ppermute(cells, "grp", swap)
    nodes_other = lax.ppermute(nodes, "grp", swap)
    routes = lax.dynamic_index_in_dim(
        block_route[0].reshape(8, 2, 4, 64), lax.axis_index("gy"), 2, keepdims=False
    ).transpose(1, 0, 2).reshape(2, 512)
    packed = call(pack_kernel, shape(16, TILES, 8, 128), [SM] + [VM] * 5)(
        core_arg, cells, cells_other, nodes, nodes_other, routes
    )
    grid = lax.all_to_all(packed, ("gx", "gy"), 0, 0, tiled=True)

    ring = [(8 + z, (z + 1) % 8) for z in range(8)] + [(z, 8 + (z - 1) % 8) for z in range(8)]
    halo = lax.ppermute(lax.dynamic_slice_in_dim(grid, 4 * core, 12, 0), ("grp", "gz"), ring)
    share = lax.ppermute(lax.dynamic_slice_in_dim(halo, 8 * (1 - core), 4, 0), "grp", swap)

    stiff = jnp.concatenate([corner_major(stiff_lambda), corner_major(stiff_mu)], axis=0)
    columns = [corner_column(coupling_vec), corner_column(jnp.diag(stiff_lambda)), corner_column(jnp.diag(stiff_mu))]
    aux = jnp.pad(jnp.stack(columns, axis=1), ((0, 0), (0, 125)))

    kept = (
        shape(6, PLANES, 32, 128), shape(PLANES, 32, 128), shape(PLANES, 32, 128),
        shape(NODES, 8, 512), shape(12, 1, 512), shape(12, 1, 512), shape(12, 8, 512),
        shape(12, 8, 512), shape(12, 8, 512), shape(12, 8, 512),
    )
    mid, *statics = call(
        first_kernel,
        (shape(4, 10, 8, 128),) + kept,
        [SM, SM] + [VM] * 5,
        [
            pltpu.VMEM((2, PLANES, 32, 128), f32),
            pltpu.VMEM((PLANES, 32, 128), f32),
            pltpu.VMEM((PLANES, 32, 128), f32),
            pltpu.VMEM((PLANES, 32, 128), f32),
            pltpu.VMEM((PLANES, 1, 512), f32),
            pltpu.VMEM((2, NODES, 8, 512), f32),
        ],
    )(core_arg, ok, grid, halo, share, stiff, aux)

    near = lax.ppermute(mid, ("grp", "gz"), ring)
    partner = lax.ppermute(mid, "grp", swap)
    across = lax.ppermute(near, "grp", swap)
    last = call(
        second_kernel,
        shape(8, 8, 128),
        [SM, SM] + [VM] * 16,
        [
            pltpu.VMEM((2, PLANES, 32, 128), f32),
            pltpu.VMEM((PLANES, 32, 128), f32),
            pltpu.VMEM((PLANES, 1, 512), f32),
            pltpu.VMEM((NODES, 8, 512), f32),
            pltpu.VMEM((PLANES, 1, 512), f32),
            pltpu.VMEM((2, NODES, 8, 512), f32),
        ],
    )(core_arg, ok, mid, partner, near, across, stiff, aux, *statics)

    other = lax.ppermute(last, "grp", swap)
    whole = jnp.concatenate([jnp.where(core == 0, last, other), jnp.where(core == 0, other, last)], axis=0)
    back = lax.all_to_all(whole, ("gx", "gy"), 0, 0, tiled=True)
    return call(
        unpack_kernel,
        (shape(4, 8, 128), shape(3, 512)),
        [SM, VM],
        [pltpu.VMEM((8, 512), f32)],
    )(core_arg, back)


def solution(mesh):
    fine = Mesh(np.asarray(mesh.devices).reshape(2, 8, 4, 4), ("grp", "gz", "gx", "gy"))
    cell = P(("gz", "gx"), "gy", "grp")
    node = P(None, ("grp", "gz", "gx", "gy"))
    elem = P(("grp", "gz", "gx", "gy"), None)
    return jax.shard_map(
        shards,
        mesh=fine,
        in_specs=(
            cell, cell, cell, cell, P(), P(("gz", "gx"), None, None), node, node, node, elem, elem,
            P(), P(), P(),
        ),
        out_specs=(cell, node),
        check_vma=False,
    )
```

```python
import jax
import jax.numpy as jnp
import numpy as np
from jax import lax
from jax.experimental import pallas as pl
from jax.experimental.pallas import tpu as pltpu
from jax.sharding import Mesh
from jax.sharding import PartitionSpec as P

SWEEPS = 6
CLASSES = 16
CHIPS = 16
PLANES = 16
NODES = 16
TILES = 13
EARLY = 5
FAR = (2, 3, 6, 7, 8, 9)

stabilize = 0.5
biot_coef = 0.8
damping = 0.7
tiny = 1e-30

f32 = jnp.float32
bf16 = jnp.bfloat16

VM = pl.BlockSpec(memory_space=pltpu.VMEM)
SM = pl.BlockSpec(memory_space=pltpu.SMEM)
HB = pl.BlockSpec(memory_space=pltpu.HBM)
WHOLE = 64 * 1024 * 1024 - 65536


def call(body, out_shapes, in_specs, scratch=(), budget=40 * 1024 * 1024):
    return pl.pallas_call(
        body,
        out_shape=out_shapes,
        in_specs=in_specs,
        out_specs=jax.tree.map(lambda _: VM, out_shapes),
        scratch_shapes=list(scratch),
        compiler_params=pltpu.CompilerParams(vmem_limit_bytes=budget),
    )


def lanes(shape):
    return lax.broadcasted_iota(jnp.int32, shape, 1)


def rows(shape):
    return lax.broadcasted_iota(jnp.int32, shape, 0)


def roll(x, shift, axis=1):
    shift = shift % x.shape[axis]
    return x if shift == 0 else pltpu.roll(x, shift, axis)


def three_parts(x):
    high = x.astype(bf16)
    rest = x - high.astype(f32)
    middle = rest.astype(bf16)
    return high, middle, (rest - middle.astype(f32)).astype(bf16)


def nt_dot(a, b):
    return lax.dot_general(a, b, (((1,), (1,)), ((), ())), preferred_element_type=f32)


def stage_kernel(perms, p0, src, sto, cls, disp, load, sup, lam, mu, cells, nodes, held, small, pair, classes, sems):
    copies = [
        pltpu.make_async_copy(perms, classes, sems.at[9]),
        pltpu.make_async_copy(p0, cells.at[0:4], sems.at[0]),
        pltpu.make_async_copy(src, cells.at[4:8], sems.at[1]),
        pltpu.make_async_copy(sto, cells.at[8:12], sems.at[2]),
        pltpu.make_async_copy(cls, held, sems.at[3]),
        pltpu.make_async_copy(disp, small.at[0], sems.at[4]),
        pltpu.make_async_copy(load, small.at[1], sems.at[5]),
        pltpu.make_async_copy(sup, small.at[2], sems.at[6]),
        pltpu.make_async_copy(lam, pair.at[0], sems.at[7]),
        pltpu.make_async_copy(mu, pair.at[1], sems.at[8]),
    ]
    for copy in copies:
        copy.start()
    nodes[...] = jnp.zeros((16, 512), f32)
    for copy in copies:
        copy.wait()
    for i in range(4):
        which = held[i]
        perm = jnp.zeros((8, 128), f32)
        for member in range(CLASSES):
            perm = jnp.where(which == member, classes[member], perm)
        cells[12 + i] = perm
    nodes[0:3] = small[0]
    nodes[3:4] = pair[0]
    nodes[4:7] = small[1]
    nodes[7:8] = pair[1]
    nodes[8:11] = small[2]


def pack_kernel(core, across, a, b, c, d, e, out, cells, cells_other, nodes, nodes_other, routes, sems):
    pairs = [(a, cells), (b, cells_other), (c, nodes), (d, nodes_other), (e, routes)]
    copies = [pltpu.make_async_copy(src, dst, sems.at[n]) for n, (src, dst) in enumerate(pairs)]
    for copy in copies:
        copy.start()
    for copy in copies:
        copy.wait()
    first = core[0] == 0
    lane = lanes((8, 128))
    low = lane < 64
    sub = rows((8, 128))

    placed = jnp.zeros((192, 128), f32)
    device = lanes((1, 512)) // 64
    for half in range(2):
        mine = jnp.zeros((8, 128), jnp.int32)
        for y in range(4):
            at = 256 * half + y // 2 * 128
            mine = jnp.where(across[0] == y, roll(routes[0, :, at : at + 128], 64 * (y % 2)), mine)
        block = jnp.concatenate(
            [jnp.where(low[0:1], mine[2 * m : 2 * m + 1], roll(mine[2 * m + 1 : 2 * m + 2], 64)) for m in range(4)],
            axis=1,
        )
        row = block // 64 % 4 * 8 + block // 256 * 4 + device % 4
        depth = device // 4 * 64 + block % 64
        at_row = rows((32, 512)) == row
        at_depth = jnp.where(rows((128, 512)) == depth, 1.0, 0.0).astype(bf16)
        spread = []
        for source in (3, 7):
            own = nodes[source : source + 1, :]
            other = nodes_other[source : source + 1, :]
            value = jnp.where(first, own, other) if half == 0 else jnp.where(first, other, own)
            for part in three_parts(value):
                spread.append(jnp.where(at_row, part.astype(f32), 0.0))
        placed = placed + nt_dot(jnp.concatenate(spread, axis=0).astype(bf16), at_depth)
    grids = [placed[96 * v : 96 * v + 32] + placed[96 * v + 32 : 96 * v + 64] + placed[96 * v + 64 : 96 * v + 96] for v in range(2)]

    for pair in range(2):
        for i in range(4):
            tiles = []
            for field in (2 * pair, 2 * pair + 1):
                own = cells[4 * field + i]
                other = cells_other[4 * field + i]
                tiles.append((jnp.where(first, own, other), jnp.where(first, other, own)))
            for chip in range(CHIPS):
                start = 16 * chip - 24
                spot = lane % 64 + start
                in_low = (spot >= 0) & (spot < 128)
                in_high = (spot >= 128) & (spot < 256)
                found = []
                for member in range(2):
                    shift = 64 * member - start
                    win = jnp.zeros((8, 128), f32)
                    if start < 128:
                        win = jnp.where(in_low, roll(tiles[member][0], shift), win)
                    if start + 64 > 128:
                        win = jnp.where(in_high, roll(tiles[member][1], shift), win)
                    found.append(win)
                out[chip, 4 * pair + i] = jnp.where(low, found[0], found[1])

    def full_depth(i, r):
        full = []
        for j in range(4):
            at = (i * 4 + j) // 2 * 128
            own = nodes[8 * r : 8 * r + 8, at : at + 128]
            other = nodes_other[8 * r : 8 * r + 8, at : at + 128]
            near = jnp.where(first, own, other)
            deep = jnp.where(first, other, own)
            if j % 2 == 0:
                full.append(jnp.where(low, near, roll(deep, 64)))
            else:
                full.append(jnp.where(low, roll(near, 64), deep))
        return full

    supports = [jnp.where(sub < 4, a, pltpu.roll(b, 4, 0)) for a, b in zip(full_depth(0, 1), full_depth(1, 1))]
    members = [full_depth(0, 0), full_depth(1, 0), supports]
    members += [[grid[8 * j : 8 * j + 8] for j in range(4)] for grid in grids]
    for at, full in enumerate(members):
        for chip in range(CHIPS):
            start = 8 * chip - 12
            spot = lane % 32 + start
            tile = jnp.zeros((8, 128), f32)
            for j in range(4):
                tile = jnp.where(lane // 32 == j, roll(full[j], 32 * j - start), tile)
            out[chip, 8 + at] = jnp.where((spot >= 0) & (spot < 128), tile, 0.0)


def low_mask(shape):
    return lanes(shape) < 64


def window(core, places, then):
    for c in range(2):
        @pl.when(core[0] == c)
        def _():
            then(places[c])


def face(p, q):
    return 2.0 * p * q / jnp.maximum(p + q, tiny)


def cell_coefs(least, most, start, source, storage, perm, coef, fixed, inverse):
    keep_top = rows((32, 128)) < 31
    outer = face(perm(least - 1), perm(least)) if least else jnp.zeros((32, 128), f32)
    for x in range(least, most):
        p = perm(x)
        inner = face(p, perm(x + 1) if x < PLANES - 1 else roll(p, 64))
        up = jnp.where(keep_top, face(p, roll(p, 31, 0)), 0.0)
        deep = face(p, roll(p, 127))
        coef[0, x - least] = inner
        coef[1, x - least] = up
        coef[2, x - least] = deep
        total = inner + outer + up + roll(up, 1, 0) + deep + roll(deep, 1)
        outer = inner
        store = storage(x)
        inverse[x - least] = jnp.where(store > 0.0, 1.0 / (store + stabilize + total), 0.0)
        fixed[x - least] = source(x) + store * start(x)


def both(early, late):
    return lambda x: early[x] if x < EARLY else late[x - EARLY]


def both_faces(early, late):
    return lambda way, x: early[way, x] if x < EARLY else late[way, x - EARLY]


def one_sweep(src, dst, coef, rhs, inverse, least):
    outer = coef(0, least - 1) * src[least - 1]
    p = src[least]
    for x in range(least, PLANES):
        q = src[x + 1] if x < PLANES - 1 else roll(p, 64)
        inner, up, deep = coef(0, x), coef(1, x), coef(2, x)
        total = rhs[x] + inner * q + outer
        total = total + up * roll(p, 31, 0) + roll(up * p, 1, 0)
        total = total + deep * roll(p, 127) + roll(deep * p, 1)
        dst[x] = total * inverse(x)
        outer = inner * p
        p = q


def sweeps(press, coef, rhs, inverse, first):
    for n in range(SWEEPS):
        one_sweep(press.at[n % 2], press.at[1 - n % 2], coef, rhs, inverse, first + n)


def pair_matrix():
    cell = rows((128, 256))
    n = lanes((128, 256))
    hit = (cell // 2 % 32 == n % 32) & (cell // 64 == n // 128)
    return jnp.where(hit, 0.125, 0.0).astype(bf16)


def row_mask(shape):
    return lanes(shape) % 128 // 32 == rows(shape) % 8 // 2


def block_means(press, means, least, most):
    sums = jnp.concatenate([press[2 * q] + press[2 * q + 1] for q in range(3, 8)], axis=0)
    matrix = pair_matrix()
    got = jnp.zeros((160, 256), f32)
    for part in three_parts(sums):
        got = got + jnp.dot(part, matrix, preferred_element_type=f32)
    got = jnp.where(row_mask((160, 256)), got, 0.0)
    for b in range(least, most + 1):
        q, side = (b, 0) if b < 8 else (15 - b, 128)
        piece = got[32 * q - 96 : 32 * q - 64, side : side + 128]
        for y in range(4):
            means[b, 0:1, 128 * y : 128 * y + 128] = jnp.sum(piece[8 * y : 8 * y + 8], axis=0, keepdims=True)


def last_row(shape):
    return lanes(shape) // 32 % 16 == 15


def corner_rolls(u):
    last = last_row(u.shape)
    return [
        u,
        roll(u, 511),
        jnp.where(last, 0.0, roll(u, 480)),
        jnp.where(last, 0.0, roll(u, 479)),
    ]


def assembled(here, under):
    summed = here[0:32] + under[32:64]
    last = last_row((8, 512))
    return (
        summed[0:8]
        + roll(summed[8:16], 1)
        + roll(jnp.where(last, 0.0, summed[16:24]), 32)
        + roll(jnp.where(last, 0.0, summed[24:32]), 33)
    )


def diag_of(lam, mu, sup, aux, safe, gain):
    depth = lanes((8, 512)) % 32
    inside = (depth >= 6) & (depth < 26)
    terms = {}
    for b in range(3, 12):
        terms[b] = aux[:, 1:2] * lam[b] + aux[:, 2:3] * mu[b]
        if b > 3:
            node_sup = sup[b]
            total = node_sup + assembled(terms[b], terms[b - 1])
            valid = inside & (node_sup > 0.0)
            safe[b] = jnp.where(valid, total, 1.0)
            gain[b] = jnp.where(valid, damping, 0.0)


def stiff_parts(stiff):
    high = stiff.astype(bf16)
    low = (stiff - high.astype(f32)).astype(bf16)
    return jnp.concatenate([high, high, low], axis=1)


def element_terms(matrix, coupling, v_here, v_next, lam, mu, press):
    vals = jnp.concatenate(v_here + v_next, axis=0)
    high = vals.astype(bf16)
    low = (vals - high.astype(f32)).astype(bf16)
    both = jnp.dot(matrix, jnp.concatenate([high, low, high], axis=0), preferred_element_type=f32)
    return coupling * (biot_coef * press) - (lam * both[0:64] + mu * both[64:128])


def displacements(u, lam, mu, load, sup, safe, gain, means, stiff, aux, moved, least, most):
    matrix = stiff_parts(stiff[...])
    coupling = aux[:, 0:1]

    def half(old, new, least, most):
        under = None
        v_here = corner_rolls(old[least - 1])
        for b in range(least - 1, most + 1):
            v_next = corner_rolls(old[b + 1])
            terms = element_terms(matrix, coupling, v_here, v_next, lam[b], mu[b], means[b])
            if b >= least:
                value = old[b]
                residual = load[b] - sup[b] * value + assembled(terms, under)
                new[b] = value + gain[b] * residual / safe[b]
            under = terms
            v_here = v_next

    half(u, moved.at[0], least - 1, most + 1)
    half(moved.at[0], moved.at[1], least, most)


def pack_mid(core, press, moved, out):
    low = low_mask((32, 128))
    upper = rows((8, 512)) < 4
    extra = jnp.where(low, press[10], roll(press[11], 64))
    node = jnp.where(core[0] == 0, moved[1, 10], moved[1, 5])
    pairs = [(moved[1, 6], moved[1, 7]), (moved[1, 8], moved[1, 9])]
    held = [jnp.where(upper, a, roll(b, 4, 0)) for a, b in pairs] + [node]
    for y in range(4):
        for q in range(4):
            out[y, q] = press[12 + q, 8 * y : 8 * y + 8]
        out[y, 4] = extra[8 * y : 8 * y + 8]
        for q in range(3):
            out[y, 5 + q] = held[q][:, 128 * y : 128 * y + 128]


def pack_last(press, moved, out):
    lane = lanes((32, 128))
    for x in range(2):
        cells = jnp.zeros((32, 128), f32)
        for i in range(4):
            if x == 0:
                tile = roll(press[12 + i], 16 * i - 24)
            else:
                tile = roll(press[15 - i], 16 * i - 88)
            cells = jnp.where(lane // 16 == i, tile, cells)
        for y in range(4):
            total = cells[8 * y : 8 * y + 8]
            for i in range(2):
                tile = moved[1, 6 + 2 * x + i, :, 128 * y : 128 * y + 128]
                for j in range(4):
                    total = jnp.where(lane[0:8] // 8 == 8 + 4 * i + j, roll(tile, 52 + 32 * i - 24 * j), total)
            out[4 * x + y] = total


def inside_flags(core, layer):
    below = jnp.where(layer[0] > 0, 1.0, 0.0)
    above = jnp.where(layer[0] < 7, 1.0, 0.0)
    first = core[0] == 0
    return jnp.where(first, below, above), jnp.where(first, above, below)


def units_of(grid, halo, share, ok):
    def plane(x):
        return lambda y, at: grid[4 * x + y, at]

    def near(y, at):
        return halo[13 * y + at] * ok[0]

    def middle(y, at):
        return halo[52 + 10 * y + at] * ok[0] if at < 10 else jnp.zeros((8, 128), f32)

    def far(y, at):
        if at not in FAR:
            return jnp.zeros((8, 128), f32)
        return halo[92 + 6 * y + FAR.index(at)] * ok[0]

    def beside(y, at):
        return jnp.zeros((8, 128), f32) if share is None else share[13 * y + at] * ok[1]

    inside = [plane(x) for x in range(4)]
    return [[far, middle, near] + inside + [beside], [beside] + inside + [near, middle, far]]


def unpack_cells(units, planes, press, source, storage, perm):
    low = low_mask((32, 128))

    def tile(cell, at):
        return jnp.concatenate([units[cell // 4](y, at + cell % 4) for y in range(4)], axis=0)

    for x in planes:
        a = tile(x, 0)
        b = tile(31 - x, 0)
        press(x)[...] = jnp.where(low, a, roll(b, 64))
        source(x)[...] = jnp.where(low, roll(a, 64), b)
        a = tile(x, 4)
        b = tile(31 - x, 4)
        storage(x)[...] = jnp.where(low, a, roll(b, 64))
        perm(x)[...] = jnp.where(low, roll(a, 64), b)


def prepare_kernel(
    core, layer, grid, halo, aux,
    start, edge, coef, fixed, inverse, u, lam, mu, load, sup, safe, gain,
    source, storage, perm,
):
    ok = inside_flags(core, layer)
    def unpack(units):
        unpack_cells(
            units, range(4, PLANES), lambda x: start.at[x - 4], lambda x: source.at[x],
            lambda x: storage.at[x], lambda x: perm.at[x],
        )
        sub = rows((8, 128))
        for unit in range(8):
            for y in range(4):
                at = slice(128 * y, 128 * y + 128)
                for i in range(2):
                    n = 2 * unit + i
                    tile_a = units[unit](y, 8 + i)
                    u[n, :, at] = jnp.where(sub < 3, tile_a, 0.0)
                    if 4 <= n <= 11:
                        load[n, :, at] = jnp.where(sub < 3, pltpu.roll(tile_a, 4, 0), 0.0)
                        tile_b = units[unit](y, 10)
                        if i == 1:
                            tile_b = pltpu.roll(tile_b, 4, 0)
                        sup[n, :, at] = jnp.where(sub < 3, tile_b, 0.0)
            if 1 <= unit <= 5:
                for at, param in ((11, lam), (12, mu)):
                    total = units[unit](0, at) + units[unit](1, at) + units[unit](2, at) + units[unit](3, at)
                    for i in range(2):
                        for y in range(4):
                            row = 4 * i + y
                            param[2 * unit + i, :, 128 * y : 128 * y + 128] = total[row : row + 1]

    window(core, units_of(grid, halo, None, ok), unpack)
    cell_coefs(
        EARLY, PLANES, lambda x: start[x - 4], lambda x: source[x], lambda x: storage[x],
        lambda x: perm[x], coef, fixed, inverse,
    )
    edge[0] = perm[4]
    edge[1] = perm[5]
    edge[2] = source[4]
    edge[3] = storage[4]
    diag_of(lam, mu, sup, aux, safe, gain)


def first_kernel(
    core, layer, halo, share, stiff, aux,
    start, edge, coef_late, fixed_late, inverse_late, u, lam, mu, load, sup, safe, gain,
    mid, coef_early, fixed_early, inverse_early, beside,
    press, source, storage, perm, rhs, means, moved,
):
    ok = inside_flags(core, layer)
    sub = rows((8, 128))

    def unpack(units):
        unpack_cells(
            units, range(4), lambda x: press.at[0, x], lambda x: source.at[x],
            lambda x: storage.at[x], lambda x: perm.at[x],
        )

    window(core, units_of(None, halo, share, ok), unpack)
    for y in range(4):
        for i in range(2):
            tile = share[13 * y + 8 + i] * ok[1]
            beside[i, :, 128 * y : 128 * y + 128] = jnp.where(sub < 3, tile, 0.0)
    for x in range(4, PLANES):
        press[0, x] = start[x - 4]
    cell_coefs(
        0, EARLY, lambda x: press[0, x],
        lambda x: source[x] if x < 4 else edge[2], lambda x: storage[x] if x < 4 else edge[3],
        lambda x: perm[x] if x < 4 else edge[x - 4], coef_early, fixed_early, inverse_early,
    )
    fixed = both(fixed_early, fixed_late)
    for x in range(PLANES):
        rhs[x] = fixed(x) + stabilize * press[0, x]
    sweeps(press, both_faces(coef_early, coef_late), rhs, both(inverse_early, inverse_late), 1)
    block_means(press.at[0], means, 3, 11)
    displacements(u, lam, mu, load, sup, safe, gain, means, stiff, aux, moved, 5, 10)
    pack_mid(core, press.at[0], moved, mid)


def node_of(ref, k, y):
    value = ref[y, 5 + k // 2]
    return jnp.where(rows((8, 128)) < 4, roll(value, 4, 0) if k % 2 else value, 0.0)


def strain_rows(aux, nodes, blocks, strain):
    last_y = last_row((8, 512))
    column = [jnp.broadcast_to(aux[8 * a : 8 * a + 8, 0:1], (8, 512)) for a in range(8)]
    for b in blocks:
        here, following = nodes(b), nodes(b + 1)
        parts = [column[a] * here + column[4 + a] * following for a in range(4)]
        total = (
            parts[0]
            + roll(parts[1], 511)
            + jnp.where(last_y, 0.0, roll(parts[2] + roll(parts[3], 511), 480))
        )
        strain[b] = jnp.sum(total, axis=0, keepdims=True)


def right_sides(strain, groups, press, fixed, rhs):
    mask = row_mask((8, 128))
    spread = []
    for q in groups:
        for y in range(4):
            at = slice(128 * y, 128 * y + 128)
            pair = [jnp.where(mask, strain[q, :, at], 0.0), jnp.where(mask, strain[15 - q, :, at], 0.0)]
            spread.append(jnp.concatenate(pair, axis=1))
    matrix = pair_matrix()
    got = jnp.zeros((32 * len(groups), 128), f32)
    for part in three_parts(jnp.concatenate(spread, axis=0)):
        got = got + nt_dot(part, matrix)
    for n, q in enumerate(groups):
        change = got[32 * n : 32 * n + 32]
        for x in (2 * q, 2 * q + 1):
            rhs[x] = fixed(x) + stabilize * press[x] - (8.0 * biot_coef) * change


def resume_kernel(core, layer, own, partner, near, aux, start, fixed_late, press, u, rhs, strain, moved):
    ok = inside_flags(core, layer)
    low = low_mask((32, 128))

    def unpack(runs, extra_cells, extra_node):
        def piece(cell, want_low):
            if cell in extra_cells:
                ref, q, is_low = near, 4, cell == 2
            elif 4 <= cell < 28:
                k = (cell - 4) % 8
                ref, q, is_low = runs[(cell - 4) // 8][0], min(k, 7 - k), k < 4
            else:
                return jnp.zeros((32, 128), f32)
            value = ref[:, q].reshape(32, 128)
            return value if is_low == want_low else roll(value, 64)

        for x in range(2, PLANES):
            press[x] = jnp.where(low, piece(x, True), piece(31 - x, False))
        for n in range(1, 15):
            if n == extra_node:
                ref, k, flag = near, 4, 0
            elif 2 <= n < 14:
                (ref, flag), k = runs[(n - 2) // 4], (n - 2) % 4
            else:
                u[n] = jnp.zeros((8, 512), f32)
                continue
            for y in range(4):
                value = node_of(ref, k, y)
                u[n, :, 128 * y : 128 * y + 128] = value if flag is None else value * ok[flag]

    @pl.when(core[0] == 0)
    def _():
        unpack([(near, 0), (own, None), (partner, None)], (2, 3), 1)

    @pl.when(core[0] == 1)
    def _():
        unpack([(partner, None), (own, None), (near, 0)], (), 14)

    for n in range(3, 14):
        moved[n] = u[n] - start[n]
    strain_rows(aux, lambda n: moved[n], range(3, 13), strain)
    right_sides(strain, range(3, 8), press, lambda x: fixed_late[x - EARLY], rhs)


def second_kernel(
    core, layer, across, stiff, aux, held, u, rhs_late,
    coef_late, fixed_late, inverse_late, start, lam, mu, load, sup, safe, gain,
    coef_early, fixed_early, inverse_early, beside,
    last, press, rhs, means, nodes, strain, moved,
):
    ok = inside_flags(core, layer)
    low = low_mask((32, 128))
    first = core[0] == 0
    for x in range(2, PLANES):
        press[0, x] = held[x]
    for x in range(6, PLANES):
        rhs[x] = rhs_late[x]
    for n in range(2, 14):
        nodes[n] = u[n]

    for x, q in ((2, 1), (3, 0)):
        turned = roll(across[:, q].reshape(32, 128), 64)
        press[0, x] = jnp.where(low & jnp.logical_not(first), turned, held[x])
    for y in range(4):
        at = slice(128 * y, 128 * y + 128)
        nodes[1, :, at] = jnp.where(first, u[1, :, at], node_of(across, 3, y) * ok[1])
        nodes[14, :, at] = jnp.where(first, node_of(across, 0, y) * ok[1], u[14, :, at])
    for n in (2, 3, 13):
        moved[0, n] = nodes[n] - start[n]
    moved[0, 1] = nodes[1] - jnp.where(first, start[1], beside[1])
    moved[0, 14] = nodes[14] - jnp.where(first, beside[0], start[14])
    strain[14] = jnp.zeros((1, 512), f32)
    strain_rows(aux, lambda n: moved[0, n], (1, 2, 13), strain)
    right_sides(strain, (1, 2), press.at[0], both(fixed_early, fixed_late), rhs)
    sweeps(press, both_faces(coef_early, coef_late), rhs, both(inverse_early, inverse_late), 3)
    block_means(press.at[0], means, 4, 10)
    displacements(nodes, lam, mu, load, sup, safe, gain, means, stiff, aux, moved, 6, 9)
    pack_last(press.at[0], moved, last)


def unpack_kernel(core, got, pressure, disp, held):
    lane = lanes((8, 128))
    base = core[0] * 8
    tiles = [got[base + s] for s in range(8)]
    for i in range(4):
        total = jnp.zeros((8, 128), f32)
        for s in range(8):
            total = jnp.where(lane // 16 == s, roll(tiles[s], 16 * s - 16 * i), total)
        pressure[i] = total
    for i in range(2):
        for pair in range(2):
            total = jnp.zeros((8, 128), f32)
            for s in range(8):
                for side in range(2):
                    shift = 64 * side + 8 * s - 64 - 32 * i - 8 * (2 * pair + side)
                    total = jnp.where(lane // 8 == 8 * side + s, roll(tiles[s], shift), total)
            held[:, 128 * (2 * i + pair) : 128 * (2 * i + pair) + 128] = total
    disp[...] = held[0:3]


def corner_major(stiff):
    grid = stiff.reshape(3, 8, 3, 8).transpose(1, 0, 3, 2)
    return jnp.pad(grid, ((0, 0), (0, 5), (0, 0), (0, 5))).reshape(64, 64)


def corner_column(vec):
    return jnp.pad(vec.reshape(3, 8).T, ((0, 0), (0, 5))).reshape(64)


def pick_far(tiles):
    return jnp.concatenate([tiles[:, 2:4], tiles[:, 6:10]], axis=1)


def shape(*dims):
    return jax.ShapeDtypeStruct(dims, f32)


def shards(
    pressure_start, source, storage, perm_class, class_perm, block_route, displacement_start,
    load, support, lame_lambda, lame_mu, stiff_lambda, stiff_mu, coupling_vec,
):
    core = lax.axis_index("grp")
    layer = lax.axis_index("gz")
    core_arg = jnp.full((1,), core, jnp.int32)
    row_arg = jnp.full((1,), lax.axis_index("gy"), jnp.int32)
    layer_arg = jnp.full((1,), layer, jnp.int32)
    swap = [(0, 1), (1, 0)]

    cells, nodes = call(
        stage_kernel,
        (shape(16, 8, 128), shape(16, 512)),
        [HB] * 10,
        [
            pltpu.VMEM((4, 8, 128), jnp.int32),
            pltpu.VMEM((3, 3, 512), f32),
            pltpu.VMEM((2, 1, 512), f32),
            pltpu.SMEM((CLASSES,), f32),
            pltpu.SemaphoreType.DMA((10,)),
        ],
        WHOLE,
    )(class_perm, pressure_start, source, storage, perm_class, displacement_start, load, support,
      lame_lambda, lame_mu)
    cells_other = lax.ppermute(cells, "grp", swap)
    nodes_other = lax.ppermute(nodes, "grp", swap)
    packed = call(
        pack_kernel,
        shape(16, TILES, 8, 128),
        [SM, SM] + [HB] * 5,
        [
            pltpu.VMEM((16, 8, 128), f32),
            pltpu.VMEM((16, 8, 128), f32),
            pltpu.VMEM((16, 512), f32),
            pltpu.VMEM((16, 512), f32),
            pltpu.VMEM((1, 8, 512), jnp.int32),
            pltpu.SemaphoreType.DMA((5,)),
        ],
        WHOLE,
    )(core_arg, row_arg, cells, cells_other, nodes, nodes_other, block_route)
    grid = lax.all_to_all(packed, ("gx", "gy"), 0, 0, tiled=True)

    ring = [(8 + z, (z + 1) % 8) for z in range(8)] + [(z, 8 + (z - 1) % 8) for z in range(8)]
    sent = [
        lax.dynamic_slice_in_dim(grid, 12 * core, 4, 0),
        lax.dynamic_slice_in_dim(grid, 4 + 4 * core, 4, 0)[:, :10],
        pick_far(lax.dynamic_slice_in_dim(grid, 8 - 4 * core, 4, 0)),
    ]
    sent = jnp.concatenate([part.reshape(-1, 8, 128) for part in sent], axis=0)
    halo = lax.ppermute(sent, ("grp", "gz"), ring)
    share = lax.ppermute(halo[:52], "grp", swap)

    stiff = jnp.concatenate([corner_major(stiff_lambda), corner_major(stiff_mu)], axis=0)
    columns = [corner_column(coupling_vec), corner_column(jnp.diag(stiff_lambda)), corner_column(jnp.diag(stiff_mu))]
    aux = jnp.pad(jnp.stack(columns, axis=1), ((0, 0), (0, 125)))

    late = PLANES - EARLY
    statics = call(
        prepare_kernel,
        (
            shape(PLANES - 4, 32, 128), shape(4, 32, 128),
            shape(3, late, 32, 128), shape(late, 32, 128), shape(late, 32, 128),
            shape(NODES, 8, 512), shape(12, 1, 512), shape(12, 1, 512), shape(12, 8, 512),
            shape(12, 8, 512), shape(12, 8, 512), shape(12, 8, 512),
        ),
        [SM, SM] + [VM] * 3,
        [pltpu.VMEM((PLANES, 32, 128), f32)] * 3,
    )(core_arg, layer_arg, grid, halo, aux)
    mid, *early = call(
        first_kernel,
        (
            shape(4, 8, 8, 128), shape(3, EARLY, 32, 128), shape(EARLY, 32, 128),
            shape(EARLY, 32, 128), shape(2, 8, 512),
        ),
        [SM, SM] + [VM] * 16,
        [
            pltpu.VMEM((2, PLANES, 32, 128), f32),
            pltpu.VMEM((4, 32, 128), f32),
            pltpu.VMEM((4, 32, 128), f32),
            pltpu.VMEM((4, 32, 128), f32),
            pltpu.VMEM((PLANES, 32, 128), f32),
            pltpu.VMEM((PLANES, 1, 512), f32),
            pltpu.VMEM((2, NODES, 8, 512), f32),
        ],
    )(core_arg, layer_arg, halo, share, stiff, aux, *statics)

    near = lax.ppermute(mid, ("grp", "gz"), ring)
    partner = lax.ppermute(mid, "grp", swap)
    across = lax.ppermute(near, "grp", swap)
    resumed = call(
        resume_kernel,
        (shape(PLANES, 32, 128), shape(NODES, 8, 512), shape(PLANES, 32, 128)),
        [SM, SM] + [VM] * 6,
        [pltpu.VMEM((PLANES, 1, 512), f32), pltpu.VMEM((NODES, 8, 512), f32)],
    )(core_arg, layer_arg, mid, partner, near, aux, statics[5], statics[3])
    last = call(
        second_kernel,
        shape(8, 8, 128),
        [SM, SM] + [VM] * 20,
        [
            pltpu.VMEM((2, PLANES, 32, 128), f32),
            pltpu.VMEM((PLANES, 32, 128), f32),
            pltpu.VMEM((PLANES, 1, 512), f32),
            pltpu.VMEM((NODES, 8, 512), f32),
            pltpu.VMEM((PLANES, 1, 512), f32),
            pltpu.VMEM((2, NODES, 8, 512), f32),
        ],
    )(core_arg, layer_arg, across, stiff, aux, *resumed, *statics[2:], *early)

    other = lax.ppermute(last, "grp", swap)
    whole = jnp.concatenate([jnp.where(core == 0, last, other), jnp.where(core == 0, other, last)], axis=0)
    back = lax.all_to_all(whole, ("gx", "gy"), 0, 0, tiled=True)
    return call(
        unpack_kernel,
        (shape(4, 8, 128), shape(3, 512)),
        [SM, VM],
        [pltpu.VMEM((8, 512), f32)],
    )(core_arg, back)


def solution(mesh):
    fine = Mesh(np.asarray(mesh.devices).reshape(2, 8, 4, 4), ("grp", "gz", "gx", "gy"))
    cell = P(("gz", "gx"), "gy", "grp")
    node = P(None, ("grp", "gz", "gx", "gy"))
    elem = P(("grp", "gz", "gx", "gy"), None)
    return jax.shard_map(
        shards,
        mesh=fine,
        in_specs=(
            cell, cell, cell, cell, P(), P(("gz", "gx"), None, None), node, node, node, elem, elem,
            P(), P(), P(),
        ),
        out_specs=(cell, node),
        check_vma=False,
    )
```

```python
import jax
import jax.numpy as jnp
import numpy as np
from jax import lax
from jax.experimental import pallas as pl
from jax.experimental.pallas import tpu as pltpu
from jax.sharding import Mesh
from jax.sharding import PartitionSpec as P

SWEEPS = 6
CLASSES = 16
CHIPS = 16
PLANES = 16
NODES = 16
TILES = 13
EARLY = 5
FAR = (2, 3, 6, 7, 8, 9)

stabilize = 0.5
biot_coef = 0.8
damping = 0.7
tiny = 1e-30

f32 = jnp.float32
bf16 = jnp.bfloat16

VM = pl.BlockSpec(memory_space=pltpu.VMEM)
SM = pl.BlockSpec(memory_space=pltpu.SMEM)
HB = pl.BlockSpec(memory_space=pltpu.HBM)
WHOLE = 64 * 1024 * 1024 - 65536


def call(body, out_shapes, in_specs, scratch=(), budget=40 * 1024 * 1024, out_spec=VM):
    return pl.pallas_call(
        body,
        out_shape=out_shapes,
        in_specs=in_specs,
        out_specs=jax.tree.map(lambda _: out_spec, out_shapes),
        scratch_shapes=list(scratch),
        compiler_params=pltpu.CompilerParams(vmem_limit_bytes=budget),
    )


def lanes(shape):
    return lax.broadcasted_iota(jnp.int32, shape, 1)


def rows(shape):
    return lax.broadcasted_iota(jnp.int32, shape, 0)


def roll(x, shift, axis=1):
    shift = shift % x.shape[axis]
    return x if shift == 0 else pltpu.roll(x, shift, axis)


def three_parts(x):
    high = x.astype(bf16)
    rest = x - high.astype(f32)
    middle = rest.astype(bf16)
    return high, middle, (rest - middle.astype(f32)).astype(bf16)


def nt_dot(a, b):
    return lax.dot_general(a, b, (((1,), (1,)), ((), ())), preferred_element_type=f32)


def stage_kernel(perms, p0, src, sto, cls, disp, load, sup, lam, mu, cells, nodes, held, small, pair, classes, sems):
    copies = [
        pltpu.make_async_copy(perms, classes, sems.at[9]),
        pltpu.make_async_copy(p0, cells.at[0:4], sems.at[0]),
        pltpu.make_async_copy(src, cells.at[4:8], sems.at[1]),
        pltpu.make_async_copy(sto, cells.at[8:12], sems.at[2]),
        pltpu.make_async_copy(cls, held, sems.at[3]),
        pltpu.make_async_copy(disp, small.at[0], sems.at[4]),
        pltpu.make_async_copy(load, small.at[1], sems.at[5]),
        pltpu.make_async_copy(sup, small.at[2], sems.at[6]),
        pltpu.make_async_copy(lam, pair.at[0], sems.at[7]),
        pltpu.make_async_copy(mu, pair.at[1], sems.at[8]),
    ]
    for copy in copies:
        copy.start()
    nodes[...] = jnp.zeros((16, 512), f32)
    for copy in copies:
        copy.wait()
    for i in range(4):
        which = held[i]
        perm = jnp.zeros((8, 128), f32)
        for member in range(CLASSES):
            perm = jnp.where(which == member, classes[member], perm)
        cells[12 + i] = perm
    nodes[0:3] = small[0]
    nodes[3:4] = pair[0]
    nodes[4:7] = small[1]
    nodes[7:8] = pair[1]
    nodes[8:11] = small[2]


def pack_kernel(core, across, layer, a, b, c, d, e, packed, cells, cells_other, nodes, nodes_other, routes, out, sems, done):
    pairs = [(a, cells), (b, cells_other), (c, nodes), (d, nodes_other), (e, routes)]
    copies = [pltpu.make_async_copy(src, dst, sems.at[n]) for n, (src, dst) in enumerate(pairs)]
    for copy in copies:
        copy.start()
    for copy in copies:
        copy.wait()
    sent = []

    def send(at):
        sent.append(pltpu.make_async_copy(out.at[:, at], packed.at[:, at], done.at[at]))
        sent[-1].start()

    first = core[0] == 0
    lane = lanes((8, 128))
    low = lane < 64
    sub = rows((8, 128))

    placed = jnp.zeros((192, 128), f32)
    device = lanes((1, 512)) // 64
    for half in range(2):
        mine = jnp.zeros((8, 128), jnp.int32)
        for y in range(4):
            at = 256 * half + y // 2 * 128
            mine = jnp.where(across[0] == y, roll(routes[0, :, at : at + 128], 64 * (y % 2)), mine)
        block = jnp.concatenate(
            [jnp.where(low[0:1], mine[2 * m : 2 * m + 1], roll(mine[2 * m + 1 : 2 * m + 2], 64)) for m in range(4)],
            axis=1,
        )
        row = block // 64 % 4 * 8 + block // 256 * 4 + device % 4
        depth = device // 4 * 64 + block % 64
        at_row = rows((32, 512)) == row
        at_depth = jnp.where(rows((128, 512)) == depth, 1.0, 0.0).astype(bf16)
        spread = []
        for source in (3, 7):
            own = nodes[source : source + 1, :]
            other = nodes_other[source : source + 1, :]
            value = jnp.where(first, own, other) if half == 0 else jnp.where(first, other, own)
            for part in three_parts(value):
                spread.append(jnp.where(at_row, part.astype(f32), 0.0))
        placed = placed + nt_dot(jnp.concatenate(spread, axis=0).astype(bf16), at_depth)
    grids = [placed[96 * v : 96 * v + 32] + placed[96 * v + 32 : 96 * v + 64] + placed[96 * v + 64 : 96 * v + 96] for v in range(2)]

    for pair in range(2):
        for i in range(4):
            tiles = []
            for field in (2 * pair, 2 * pair + 1):
                own = cells[4 * field + i]
                other = cells_other[4 * field + i]
                tiles.append((jnp.where(first, own, other), jnp.where(first, other, own)))
            for chip in range(CHIPS):
                start = 16 * chip - 24
                spot = lane % 64 + start
                in_low = (spot >= 0) & (spot < 128)
                in_high = (spot >= 128) & (spot < 256)
                found = []
                for member in range(2):
                    shift = 64 * member - start
                    win = jnp.zeros((8, 128), f32)
                    if start < 128:
                        win = jnp.where(in_low, roll(tiles[member][0], shift), win)
                    if start + 64 > 128:
                        win = jnp.where(in_high, roll(tiles[member][1], shift), win)
                    found.append(win)
                out[chip, 4 * pair + i] = jnp.where(low, found[0], found[1])
            send(4 * pair + i)

    def full_depth(i, r):
        full = []
        for j in range(4):
            at = (i * 4 + j) // 2 * 128
            own = nodes[8 * r : 8 * r + 8, at : at + 128]
            other = nodes_other[8 * r : 8 * r + 8, at : at + 128]
            near = jnp.where(first, own, other)
            deep = jnp.where(first, other, own)
            if j % 2 == 0:
                full.append(jnp.where(low, near, roll(deep, 64)))
            else:
                full.append(jnp.where(low, roll(near, 64), deep))
        return full

    supports = [jnp.where(sub < 4, a, pltpu.roll(b, 4, 0)) for a, b in zip(full_depth(0, 1), full_depth(1, 1))]
    members = [full_depth(0, 0), full_depth(1, 0), supports]
    members += [[grid[8 * j : 8 * j + 8] for j in range(4)] for grid in grids]
    for at, full in enumerate(members):
        for chip in range(CHIPS):
            start = 8 * chip - 12
            spot = lane % 32 + start
            tile = jnp.zeros((8, 128), f32)
            for j in range(4):
                tile = jnp.where(lane // 32 == j, roll(full[j], 32 * j - start), tile)
            out[chip, 8 + at] = jnp.where((spot >= 0) & (spot < 128), tile, 0.0)
        send(8 + at)
    for copy in sent:
        copy.wait()


def low_mask(shape):
    return lanes(shape) < 64


def window(core, places, then):
    for c in range(2):
        @pl.when(core[0] == c)
        def _():
            then(places[c])


def face(p, q):
    return 2.0 * p * q / jnp.maximum(p + q, tiny)


def cell_coefs(least, most, start, source, storage, perm, coef, fixed, inverse):
    keep_top = rows((32, 128)) < 31
    outer = face(perm(least - 1), perm(least)) if least else jnp.zeros((32, 128), f32)
    for x in range(least, most):
        p = perm(x)
        inner = face(p, perm(x + 1) if x < PLANES - 1 else roll(p, 64))
        up = jnp.where(keep_top, face(p, roll(p, 31, 0)), 0.0)
        deep = face(p, roll(p, 127))
        coef[0, x - least] = inner
        coef[1, x - least] = up
        coef[2, x - least] = deep
        total = inner + outer + up + roll(up, 1, 0) + deep + roll(deep, 1)
        outer = inner
        store = storage(x)
        inverse[x - least] = jnp.where(store > 0.0, 1.0 / (store + stabilize + total), 0.0)
        fixed[x - least] = source(x) + store * start(x)


def both(early, late):
    return lambda x: early[x] if x < EARLY else late[x - EARLY]


def both_faces(early, late):
    return lambda way, x: early[way, x] if x < EARLY else late[way, x - EARLY]


def one_sweep(src, dst, coef, rhs, inverse, least):
    outer = coef(0, least - 1) * src[least - 1]
    p = src[least]
    for x in range(least, PLANES):
        q = src[x + 1] if x < PLANES - 1 else roll(p, 64)
        inner, up, deep = coef(0, x), coef(1, x), coef(2, x)
        total = rhs[x] + inner * q + outer
        total = total + up * roll(p, 31, 0) + roll(up * p, 1, 0)
        total = total + deep * roll(p, 127) + roll(deep * p, 1)
        dst[x] = total * inverse(x)
        outer = inner * p
        p = q


def sweeps(press, coef, rhs, inverse, first):
    for n in range(SWEEPS):
        one_sweep(press.at[n % 2], press.at[1 - n % 2], coef, rhs, inverse, first + n)


def pair_matrix():
    cell = rows((128, 256))
    n = lanes((128, 256))
    hit = (cell // 2 % 32 == n % 32) & (cell // 64 == n // 128)
    return jnp.where(hit, 0.125, 0.0).astype(bf16)


def row_mask(shape):
    return lanes(shape) % 128 // 32 == rows(shape) % 8 // 2


def block_means(press, means, least, most):
    sums = jnp.concatenate([press[2 * q] + press[2 * q + 1] for q in range(3, 8)], axis=0)
    matrix = pair_matrix()
    got = jnp.zeros((160, 256), f32)
    for part in three_parts(sums):
        got = got + jnp.dot(part, matrix, preferred_element_type=f32)
    got = jnp.where(row_mask((160, 256)), got, 0.0)
    for b in range(least, most + 1):
        q, side = (b, 0) if b < 8 else (15 - b, 128)
        piece = got[32 * q - 96 : 32 * q - 64, side : side + 128]
        for y in range(4):
            means[b, 0:1, 128 * y : 128 * y + 128] = jnp.sum(piece[8 * y : 8 * y + 8], axis=0, keepdims=True)


def last_row(shape):
    return lanes(shape) // 32 % 16 == 15


def corner_rolls(u):
    last = last_row(u.shape)
    return [
        u,
        roll(u, 511),
        jnp.where(last, 0.0, roll(u, 480)),
        jnp.where(last, 0.0, roll(u, 479)),
    ]


def assembled(here, under):
    summed = [here[8 * j : 8 * j + 8] + roll(under[8 * j : 8 * j + 8], 4, 0) for j in range(4)]
    last = last_row((8, 512))
    return (
        summed[0]
        + roll(summed[1], 1)
        + roll(jnp.where(last, 0.0, summed[2] + roll(summed[3], 1)), 32)
    )


def diag_of(lam, mu, sup, aux, safe, gain):
    depth = lanes((8, 512)) % 32
    inside = (depth >= 6) & (depth < 26)
    terms = {}
    for b in range(3, 12):
        terms[b] = aux[:, 1:2] * lam[b] + aux[:, 2:3] * mu[b]
        if b > 3:
            node_sup = sup[b]
            total = node_sup + assembled(terms[b], terms[b - 1])
            valid = inside & (node_sup > 0.0)
            safe[b] = jnp.where(valid, total, 1.0)
            gain[b] = jnp.where(valid, damping, 0.0)


def stiff_parts(stiff):
    high = stiff.astype(bf16)
    low = (stiff - high.astype(f32)).astype(bf16)
    return jnp.concatenate([high, high, low], axis=1)


def element_terms(matrix, coupling, v_here, v_next, lam, mu, press):
    vals = jnp.concatenate([a + roll(b, 4, 0) for a, b in zip(v_here, v_next)], axis=0)
    high = vals.astype(bf16)
    low = (vals - high.astype(f32)).astype(bf16)
    both = jnp.dot(matrix, jnp.concatenate([high, low, high], axis=0), preferred_element_type=f32)
    return coupling * (biot_coef * press) - (lam * both[0:32] + mu * both[32:64])


def displacements(u, lam, mu, load, sup, safe, gain, means, stiff, aux, moved, least, most):
    matrix = stiff_parts(stiff[...])
    coupling = aux[:, 0:1]

    def half(old, new, least, most):
        under = None
        v_here = corner_rolls(old[least - 1])
        for b in range(least - 1, most + 1):
            v_next = corner_rolls(old[b + 1])
            terms = element_terms(matrix, coupling, v_here, v_next, lam[b], mu[b], means[b])
            if b >= least:
                value = old[b]
                residual = load[b] - sup[b] * value + assembled(terms, under)
                new[b] = value + gain[b] * residual / safe[b]
            under = terms
            v_here = v_next

    half(u, moved.at[0], least - 1, most + 1)
    half(moved.at[0], moved.at[1], least, most)


def pack_mid(core, press, moved, out):
    low = low_mask((32, 128))
    upper = rows((8, 512)) < 4
    extra = jnp.where(low, press[10], roll(press[11], 64))
    node = jnp.where(core[0] == 0, moved[1, 10], moved[1, 5])
    pairs = [(moved[1, 6], moved[1, 7]), (moved[1, 8], moved[1, 9])]
    held = [jnp.where(upper, a, roll(b, 4, 0)) for a, b in pairs] + [node]
    for y in range(4):
        for q in range(4):
            out[y, q] = press[12 + q, 8 * y : 8 * y + 8]
        out[y, 4] = extra[8 * y : 8 * y + 8]
        for q in range(3):
            out[y, 5 + q] = held[q][:, 128 * y : 128 * y + 128]


def pack_last(press, moved, out):
    lane = lanes((32, 128))
    for x in range(2):
        cells = jnp.zeros((32, 128), f32)
        for i in range(4):
            if x == 0:
                tile = roll(press[12 + i], 16 * i - 24)
            else:
                tile = roll(press[15 - i], 16 * i - 88)
            cells = jnp.where(lane // 16 == i, tile, cells)
        for y in range(4):
            total = cells[8 * y : 8 * y + 8]
            for i in range(2):
                tile = moved[1, 6 + 2 * x + i, :, 128 * y : 128 * y + 128]
                for j in range(4):
                    total = jnp.where(lane[0:8] // 8 == 8 + 4 * i + j, roll(tile, 52 + 32 * i - 24 * j), total)
            out[4 * x + y] = total


def inside_flags(core, layer):
    below = jnp.where(layer[0] > 0, 1.0, 0.0)
    above = jnp.where(layer[0] < 7, 1.0, 0.0)
    first = core[0] == 0
    return jnp.where(first, below, above), jnp.where(first, above, below)


def units_of(grid, halo, share, ok):
    def plane(x):
        return lambda y, at: grid[4 * x + y, at]

    def near(y, at):
        return halo[13 * y + at] * ok[0]

    def middle(y, at):
        return halo[52 + 10 * y + at] * ok[0] if at < 10 else jnp.zeros((8, 128), f32)

    def far(y, at):
        if at not in FAR:
            return jnp.zeros((8, 128), f32)
        at = 92 + 2 * y + at - 2 if at < 4 else 100 + 4 * y + at - 6
        return halo[at] * ok[0]

    def beside(y, at):
        return jnp.zeros((8, 128), f32) if share is None else share[13 * y + at] * ok[1]

    inside = [plane(x) for x in range(4)]
    return [[far, middle, near] + inside + [beside], [beside] + inside + [near, middle, far]]


def unpack_cells(units, planes, press, source, storage, perm):
    low = low_mask((32, 128))

    def tile(cell, at):
        return jnp.concatenate([units[cell // 4](y, at + cell % 4) for y in range(4)], axis=0)

    for x in planes:
        a = tile(x, 0)
        b = tile(31 - x, 0)
        press(x)[...] = jnp.where(low, a, roll(b, 64))
        source(x)[...] = jnp.where(low, roll(a, 64), b)
        a = tile(x, 4)
        b = tile(31 - x, 4)
        storage(x)[...] = jnp.where(low, a, roll(b, 64))
        perm(x)[...] = jnp.where(low, roll(a, 64), b)


def prepare_kernel(
    core, layer, grid, halo, aux,
    start, edge, coef, fixed, inverse, u, lam, mu, load, sup, safe, gain,
    source, storage, perm,
):
    ok = inside_flags(core, layer)
    def unpack(units):
        unpack_cells(
            units, range(4, PLANES), lambda x: start.at[x - 4], lambda x: source.at[x],
            lambda x: storage.at[x], lambda x: perm.at[x],
        )
        sub = rows((8, 128))
        for unit in range(8):
            for y in range(4):
                at = slice(128 * y, 128 * y + 128)
                for i in range(2):
                    n = 2 * unit + i
                    tile_a = units[unit](y, 8 + i)
                    u[n, :, at] = jnp.where(sub < 3, tile_a, 0.0)
                    if 4 <= n <= 11:
                        load[n, :, at] = jnp.where(sub < 3, pltpu.roll(tile_a, 4, 0), 0.0)
                        tile_b = units[unit](y, 10)
                        if i == 1:
                            tile_b = pltpu.roll(tile_b, 4, 0)
                        sup[n, :, at] = jnp.where(sub < 3, tile_b, 0.0)
            if 1 <= unit <= 5:
                for at, param in ((11, lam), (12, mu)):
                    total = units[unit](0, at) + units[unit](1, at) + units[unit](2, at) + units[unit](3, at)
                    for i in range(2):
                        for y in range(4):
                            row = 4 * i + y
                            param[2 * unit + i, :, 128 * y : 128 * y + 128] = total[row : row + 1]

    window(core, units_of(grid, halo, None, ok), unpack)
    cell_coefs(
        EARLY, PLANES, lambda x: start[x - 4], lambda x: source[x], lambda x: storage[x],
        lambda x: perm[x], coef, fixed, inverse,
    )
    edge[0] = perm[4]
    edge[1] = perm[5]
    edge[2] = source[4]
    edge[3] = storage[4]
    diag_of(lam, mu, sup, aux, safe, gain)


def first_kernel(
    core, layer, halo, share, stiff, aux,
    start, edge, coef_late, fixed_late, inverse_late, u, lam, mu, load, sup, safe, gain,
    mid, coef_early, fixed_early, inverse_early, beside,
    press, source, storage, perm, rhs, means, moved,
):
    ok = inside_flags(core, layer)
    sub = rows((8, 128))

    def unpack(units):
        unpack_cells(
            units, range(4), lambda x: press.at[0, x], lambda x: source.at[x],
            lambda x: storage.at[x], lambda x: perm.at[x],
        )

    window(core, units_of(None, halo, share, ok), unpack)
    for y in range(4):
        for i in range(2):
            tile = share[13 * y + 8 + i] * ok[1]
            beside[i, :, 128 * y : 128 * y + 128] = jnp.where(sub < 3, tile, 0.0)
    for x in range(4, PLANES):
        press[0, x] = start[x - 4]
    cell_coefs(
        0, EARLY, lambda x: press[0, x],
        lambda x: source[x] if x < 4 else edge[2], lambda x: storage[x] if x < 4 else edge[3],
        lambda x: perm[x] if x < 4 else edge[x - 4], coef_early, fixed_early, inverse_early,
    )
    fixed = both(fixed_early, fixed_late)
    for x in range(PLANES):
        rhs[x] = fixed(x) + stabilize * press[0, x]
    sweeps(press, both_faces(coef_early, coef_late), rhs, both(inverse_early, inverse_late), 1)
    block_means(press.at[0], means, 3, 11)
    displacements(u, lam, mu, load, sup, safe, gain, means, stiff, aux, moved, 5, 10)
    pack_mid(core, press.at[0], moved, mid)


def node_of(ref, k, y):
    value = ref[y, 5 + k // 2]
    return jnp.where(rows((8, 128)) < 4, roll(value, 4, 0) if k % 2 else value, 0.0)


def strain_rows(aux, nodes, blocks, strain):
    last_y = last_row((8, 512))
    column = [jnp.broadcast_to(aux[8 * j : 8 * j + 8, 0:1], (8, 512)) for j in range(4)]
    for b in blocks:
        pair = nodes(b) + roll(nodes(b + 1), 4, 0)
        parts = [column[j] * pair for j in range(4)]
        total = (
            parts[0]
            + roll(parts[1], 511)
            + jnp.where(last_y, 0.0, roll(parts[2] + roll(parts[3], 511), 480))
        )
        strain[b] = jnp.sum(total, axis=0, keepdims=True)


def right_sides(strain, groups, press, fixed, rhs):
    mask = row_mask((8, 128))
    spread = []
    for q in groups:
        for y in range(4):
            at = slice(128 * y, 128 * y + 128)
            pair = [jnp.where(mask, strain[q, :, at], 0.0), jnp.where(mask, strain[15 - q, :, at], 0.0)]
            spread.append(jnp.concatenate(pair, axis=1))
    matrix = pair_matrix()
    got = jnp.zeros((32 * len(groups), 128), f32)
    for part in three_parts(jnp.concatenate(spread, axis=0)):
        got = got + nt_dot(part, matrix)
    for n, q in enumerate(groups):
        change = got[32 * n : 32 * n + 32]
        for x in (2 * q, 2 * q + 1):
            rhs[x] = fixed(x) + stabilize * press[x] - (8.0 * biot_coef) * change


def resume_kernel(core, layer, own, partner, near, aux, start, fixed_late, press, u, rhs, strain, moved):
    ok = inside_flags(core, layer)
    low = low_mask((32, 128))

    def unpack(runs, extra_cells, extra_node):
        def piece(cell, want_low):
            if cell in extra_cells:
                ref, q, is_low = near, 4, cell == 2
            elif 4 <= cell < 28:
                k = (cell - 4) % 8
                ref, q, is_low = runs[(cell - 4) // 8][0], min(k, 7 - k), k < 4
            else:
                return jnp.zeros((32, 128), f32)
            value = ref[:, q].reshape(32, 128)
            return value if is_low == want_low else roll(value, 64)

        for x in range(2, PLANES):
            press[x] = jnp.where(low, piece(x, True), piece(31 - x, False))
        for n in range(1, 15):
            if n == extra_node:
                ref, k, flag = near, 4, 0
            elif 2 <= n < 14:
                (ref, flag), k = runs[(n - 2) // 4], (n - 2) % 4
            else:
                u[n] = jnp.zeros((8, 512), f32)
                continue
            for y in range(4):
                value = node_of(ref, k, y)
                u[n, :, 128 * y : 128 * y + 128] = value if flag is None else value * ok[flag]

    @pl.when(core[0] == 0)
    def _():
        unpack([(near, 0), (own, None), (partner, None)], (2, 3), 1)

    @pl.when(core[0] == 1)
    def _():
        unpack([(partner, None), (own, None), (near, 0)], (), 14)

    for n in range(3, 14):
        moved[n] = u[n] - start[n]
    strain_rows(aux, lambda n: moved[n], range(3, 13), strain)
    right_sides(strain, range(3, 8), press, lambda x: fixed_late[x - EARLY], rhs)


def second_kernel(
    core, layer, across, stiff, aux, held, u, rhs_late,
    coef_late, fixed_late, inverse_late, start, lam, mu, load, sup, safe, gain,
    coef_early, fixed_early, inverse_early, beside,
    last, press, rhs, means, nodes, strain, moved,
):
    ok = inside_flags(core, layer)
    low = low_mask((32, 128))
    first = core[0] == 0
    for x in range(2, PLANES):
        press[0, x] = held[x]
    for x in range(6, PLANES):
        rhs[x] = rhs_late[x]
    for n in range(2, 14):
        nodes[n] = u[n]

    for x, q in ((2, 1), (3, 0)):
        turned = roll(across[:, q].reshape(32, 128), 64)
        press[0, x] = jnp.where(low & jnp.logical_not(first), turned, held[x])
    for y in range(4):
        at = slice(128 * y, 128 * y + 128)
        nodes[1, :, at] = jnp.where(first, u[1, :, at], node_of(across, 3, y) * ok[1])
        nodes[14, :, at] = jnp.where(first, node_of(across, 0, y) * ok[1], u[14, :, at])
    for n in (2, 3, 13):
        moved[0, n] = nodes[n] - start[n]
    moved[0, 1] = nodes[1] - jnp.where(first, start[1], beside[1])
    moved[0, 14] = nodes[14] - jnp.where(first, beside[0], start[14])
    strain[14] = jnp.zeros((1, 512), f32)
    strain_rows(aux, lambda n: moved[0, n], (1, 2, 13), strain)
    right_sides(strain, (1, 2), press.at[0], both(fixed_early, fixed_late), rhs)
    sweeps(press, both_faces(coef_early, coef_late), rhs, both(inverse_early, inverse_late), 3)
    block_means(press.at[0], means, 4, 10)
    displacements(nodes, lam, mu, load, sup, safe, gain, means, stiff, aux, moved, 6, 9)
    pack_last(press.at[0], moved, last)


def unpack_kernel(core, got, pressure, disp, held):
    lane = lanes((8, 128))
    base = core[0] * 8
    tiles = [got[base + s] for s in range(8)]
    for i in range(4):
        total = jnp.zeros((8, 128), f32)
        for s in range(8):
            total = jnp.where(lane // 16 == s, roll(tiles[s], 16 * s - 16 * i), total)
        pressure[i] = total
    for i in range(2):
        for pair in range(2):
            total = jnp.zeros((8, 128), f32)
            for s in range(8):
                for side in range(2):
                    shift = 64 * side + 8 * s - 64 - 32 * i - 8 * (2 * pair + side)
                    total = jnp.where(lane // 8 == 8 * side + s, roll(tiles[s], shift), total)
            held[:, 128 * (2 * i + pair) : 128 * (2 * i + pair) + 128] = total
    disp[...] = held[0:3]


def corner_major(stiff):
    grid = stiff.reshape(3, 2, 4, 3, 2, 4).transpose(2, 1, 0, 5, 4, 3)
    return jnp.pad(grid, ((0, 0), (0, 0), (0, 1), (0, 0), (0, 0), (0, 1))).reshape(32, 32)


def corner_column(vec):
    return jnp.pad(vec.reshape(3, 2, 4).transpose(2, 1, 0), ((0, 0), (0, 0), (0, 1))).reshape(32)


def shape(*dims):
    return jax.ShapeDtypeStruct(dims, f32)


def shards(
    pressure_start, source, storage, perm_class, class_perm, block_route, displacement_start,
    load, support, lame_lambda, lame_mu, stiff_lambda, stiff_mu, coupling_vec,
):
    core = lax.axis_index("grp")
    core_arg = jnp.full((1,), core, jnp.int32)
    row_arg = jnp.full((1,), lax.axis_index("gy"), jnp.int32)
    layer = lax.axis_index("gz")
    layer_arg = jnp.full((1,), layer, jnp.int32)
    swap = [(0, 1), (1, 0)]

    cells, nodes = call(
        stage_kernel,
        (shape(16, 8, 128), shape(16, 512)),
        [HB] * 10,
        [
            pltpu.VMEM((4, 8, 128), jnp.int32),
            pltpu.VMEM((3, 3, 512), f32),
            pltpu.VMEM((2, 1, 512), f32),
            pltpu.SMEM((CLASSES,), f32),
            pltpu.SemaphoreType.DMA((10,)),
        ],
        WHOLE,
    )(class_perm, pressure_start, source, storage, perm_class, displacement_start, load, support,
      lame_lambda, lame_mu)
    cells_other = lax.ppermute(cells, "grp", swap)
    nodes_other = lax.ppermute(nodes, "grp", swap)
    packed = call(
        pack_kernel,
        shape(16, TILES, 8, 128),
        [SM, SM, SM] + [HB] * 5,
        [
            pltpu.VMEM((16, 8, 128), f32),
            pltpu.VMEM((16, 8, 128), f32),
            pltpu.VMEM((16, 512), f32),
            pltpu.VMEM((16, 512), f32),
            pltpu.VMEM((1, 8, 512), jnp.int32),
            pltpu.VMEM((16, TILES, 8, 128), f32),
            pltpu.SemaphoreType.DMA((5,)),
            pltpu.SemaphoreType.DMA((TILES,)),
        ],
        WHOLE,
        HB,
    )(core_arg, row_arg, layer_arg, cells, cells_other, nodes, nodes_other, block_route)
    grid = lax.all_to_all(packed, ("gx", "gy"), 0, 0, tiled=True)
    grid, core, layer, stiff_lambda, stiff_mu, coupling_vec = lax.optimization_barrier(
        (grid, core, layer, stiff_lambda, stiff_mu, coupling_vec)
    )
    core_arg = jnp.full((1,), core, jnp.int32)
    layer_arg = jnp.full((1,), layer, jnp.int32)

    ring = [(8 + z, (z + 1) % 8) for z in range(8)] + [(z, 8 + (z - 1) % 8) for z in range(8)]
    first = core == 0
    sent = [
        jnp.where(first, grid[0:4], grid[12:16]),
        jnp.where(first, grid[4:8, :10], grid[8:12, :10]),
        jnp.where(first, grid[8:12, 2:4], grid[4:8, 2:4]),
        jnp.where(first, grid[8:12, 6:10], grid[4:8, 6:10]),
    ]
    sent = jnp.concatenate([part.reshape(-1, 8, 128) for part in sent], axis=0)
    halo = lax.ppermute(sent, ("grp", "gz"), ring)
    share = lax.ppermute(halo[:52], "grp", swap)

    stiff = jnp.concatenate([corner_major(stiff_lambda), corner_major(stiff_mu)], axis=0)
    columns = [corner_column(coupling_vec), corner_column(jnp.diag(stiff_lambda)), corner_column(jnp.diag(stiff_mu))]
    aux = jnp.pad(jnp.stack(columns, axis=1), ((0, 0), (0, 125)))

    late = PLANES - EARLY
    statics = call(
        prepare_kernel,
        (
            shape(PLANES - 4, 32, 128), shape(4, 32, 128),
            shape(3, late, 32, 128), shape(late, 32, 128), shape(late, 32, 128),
            shape(NODES, 8, 512), shape(12, 1, 512), shape(12, 1, 512), shape(12, 8, 512),
            shape(12, 8, 512), shape(12, 8, 512), shape(12, 8, 512),
        ),
        [SM, SM] + [VM] * 3,
        [pltpu.VMEM((PLANES, 32, 128), f32)] * 3,
    )(core_arg, layer_arg, grid, halo, aux)
    mid, *early = call(
        first_kernel,
        (
            shape(4, 8, 8, 128), shape(3, EARLY, 32, 128), shape(EARLY, 32, 128),
            shape(EARLY, 32, 128), shape(2, 8, 512),
        ),
        [SM, SM] + [VM] * 16,
        [
            pltpu.VMEM((2, PLANES, 32, 128), f32),
            pltpu.VMEM((4, 32, 128), f32),
            pltpu.VMEM((4, 32, 128), f32),
            pltpu.VMEM((4, 32, 128), f32),
            pltpu.VMEM((PLANES, 32, 128), f32),
            pltpu.VMEM((PLANES, 1, 512), f32),
            pltpu.VMEM((2, NODES, 8, 512), f32),
        ],
    )(core_arg, layer_arg, halo, share, stiff, aux, *statics)

    near = lax.ppermute(mid, ("grp", "gz"), ring)
    partner = lax.ppermute(mid, "grp", swap)
    across = lax.ppermute(near, "grp", swap)
    resumed = call(
        resume_kernel,
        (shape(PLANES, 32, 128), shape(NODES, 8, 512), shape(PLANES, 32, 128)),
        [SM, SM] + [VM] * 6,
        [pltpu.VMEM((PLANES, 1, 512), f32), pltpu.VMEM((NODES, 8, 512), f32)],
    )(core_arg, layer_arg, mid, partner, near, aux, statics[5], statics[3])
    last = call(
        second_kernel,
        shape(8, 8, 128),
        [SM, SM] + [VM] * 20,
        [
            pltpu.VMEM((2, PLANES, 32, 128), f32),
            pltpu.VMEM((PLANES, 32, 128), f32),
            pltpu.VMEM((PLANES, 1, 512), f32),
            pltpu.VMEM((NODES, 8, 512), f32),
            pltpu.VMEM((PLANES, 1, 512), f32),
            pltpu.VMEM((2, NODES, 8, 512), f32),
        ],
    )(core_arg, layer_arg, across, stiff, aux, *resumed, *statics[2:], *early)

    other = lax.ppermute(last, "grp", swap)
    whole = jnp.concatenate([jnp.where(core == 0, last, other), jnp.where(core == 0, other, last)], axis=0)
    back = lax.all_to_all(whole, ("gx", "gy"), 0, 0, tiled=True)
    return call(
        unpack_kernel,
        (shape(4, 8, 128), shape(3, 512)),
        [SM, VM],
        [pltpu.VMEM((8, 512), f32)],
    )(core_arg, back)


def solution(mesh):
    fine = Mesh(np.asarray(mesh.devices).reshape(2, 8, 4, 4), ("grp", "gz", "gx", "gy"))
    cell = P(("gz", "gx"), "gy", "grp")
    node = P(None, ("grp", "gz", "gx", "gy"))
    elem = P(("grp", "gz", "gx", "gy"), None)
    return jax.shard_map(
        shards,
        mesh=fine,
        in_specs=(
            cell, cell, cell, cell, P(), P(("gz", "gx"), None, None), node, node, node, elem, elem,
            P(), P(), P(),
        ),
        out_specs=(cell, node),
        check_vma=False,
    )
```

```python
import jax
import jax.numpy as jnp
import numpy as np
from jax import lax
from jax.experimental import pallas as pl
from jax.experimental.pallas import tpu as pltpu
from jax.sharding import Mesh
from jax.sharding import PartitionSpec as P

SWEEPS = 6
CLASSES = 16
CHIPS = 16
PLANES = 16
NODES = 16
TILES = 13
EARLY = 5
FAR = (2, 3, 6, 7, 8, 9)

stabilize = 0.5
biot_coef = 0.8
damping = 0.7
tiny = 1e-30

f32 = jnp.float32
bf16 = jnp.bfloat16

VM = pl.BlockSpec(memory_space=pltpu.VMEM)
SM = pl.BlockSpec(memory_space=pltpu.SMEM)
HB = pl.BlockSpec(memory_space=pltpu.HBM)
WHOLE = 64 * 1024 * 1024 - 65536


def call(body, out_shapes, in_specs, scratch=(), budget=40 * 1024 * 1024, out_spec=VM):
    return pl.pallas_call(
        body,
        out_shape=out_shapes,
        in_specs=in_specs,
        out_specs=jax.tree.map(lambda _: out_spec, out_shapes),
        scratch_shapes=list(scratch),
        compiler_params=pltpu.CompilerParams(vmem_limit_bytes=budget),
    )


def lanes(shape):
    return lax.broadcasted_iota(jnp.int32, shape, 1)


def rows(shape):
    return lax.broadcasted_iota(jnp.int32, shape, 0)


def roll(x, shift, axis=1):
    shift = shift % x.shape[axis]
    return x if shift == 0 else pltpu.roll(x, shift, axis)


def three_parts(x):
    high = x.astype(bf16)
    rest = x - high.astype(f32)
    middle = rest.astype(bf16)
    return high, middle, (rest - middle.astype(f32)).astype(bf16)


def nt_dot(a, b):
    return lax.dot_general(a, b, (((1,), (1,)), ((), ())), preferred_element_type=f32)


def pack_kernel(
    core, across, layer, perms, p0, src, sto, cls, disp, load, sup, lam, mu, blocks,
    packed, cells, nodes, routes, held, small, pair, classes, out, sems, done,
):
    copies = [
        pltpu.make_async_copy(perms, classes, sems.at[0]),
        pltpu.make_async_copy(cls, held, sems.at[1]),
        pltpu.make_async_copy(p0, cells.at[0:4], sems.at[2]),
        pltpu.make_async_copy(src, cells.at[4:8], sems.at[3]),
        pltpu.make_async_copy(sto, cells.at[8:12], sems.at[4]),
        pltpu.make_async_copy(disp, small.at[0], sems.at[5]),
        pltpu.make_async_copy(load, small.at[1], sems.at[6]),
        pltpu.make_async_copy(sup, small.at[2], sems.at[7]),
        pltpu.make_async_copy(lam, pair.at[0], sems.at[8]),
        pltpu.make_async_copy(mu, pair.at[1], sems.at[9]),
        pltpu.make_async_copy(blocks, routes, sems.at[10]),
    ]
    for copy in copies:
        copy.start()
    nodes[...] = jnp.zeros((16, 512), f32)
    for copy in copies:
        copy.wait()
    for i in range(4):
        which = held[i]
        perm = jnp.zeros((8, 128), f32)
        for member in range(CLASSES):
            perm = jnp.where(which == member, classes[member], perm)
        cells[12 + i] = perm
    nodes[0:3] = small[0]
    nodes[4:7] = small[1]
    nodes[8:11] = small[2]
    sent = []

    def send(at):
        sent.append(pltpu.make_async_copy(out.at[:, at], packed.at[:, at], done.at[at]))
        sent[-1].start()

    first = core[0] == 0
    lane = lanes((8, 128))
    low = lane < 64
    sub = rows((8, 128))

    device = lanes((1, 512)) // 64
    mine = jnp.zeros((8, 128), jnp.int32)
    for k in range(8):
        at = k // 2 * 128
        here = (core[0] == k // 4) & (across[0] == k % 4)
        mine = jnp.where(here, roll(routes[0, :, at : at + 128], 64 * (k % 2)), mine)
    block = jnp.concatenate(
        [jnp.where(low[0:1], mine[2 * m : 2 * m + 1], roll(mine[2 * m + 1 : 2 * m + 2], 64)) for m in range(4)],
        axis=1,
    )
    row = block // 64 % 4 * 8 + block // 256 * 4 + device % 4
    depth = device // 4 * 64 + block % 64
    at_row = rows((32, 512)) == row
    at_depth = jnp.where(rows((128, 512)) == depth, 1.0, 0.0).astype(bf16)
    spread = [
        jnp.where(at_row, part.astype(f32), 0.0) for v in range(2) for part in three_parts(pair[v])
    ]
    placed = nt_dot(jnp.concatenate(spread, axis=0).astype(bf16), at_depth)
    grids = [placed[96 * v : 96 * v + 32] + placed[96 * v + 32 : 96 * v + 64] + placed[96 * v + 64 : 96 * v + 96] for v in range(2)]

    for pair in range(2):
        for i in range(4):
            tiles = []
            for field in (2 * pair, 2 * pair + 1):
                own = cells[4 * field + i]
                tiles.append((jnp.where(first, own, 0.0), jnp.where(first, 0.0, own)))
            for chip in range(CHIPS):
                start = 16 * chip - 24
                spot = lane % 64 + start
                in_low = (spot >= 0) & (spot < 128)
                in_high = (spot >= 128) & (spot < 256)
                found = []
                for member in range(2):
                    shift = 64 * member - start
                    win = jnp.zeros((8, 128), f32)
                    if start < 128:
                        win = jnp.where(in_low, roll(tiles[member][0], shift), win)
                    if start + 64 > 128:
                        win = jnp.where(in_high, roll(tiles[member][1], shift), win)
                    found.append(win)
                out[chip, 4 * pair + i] = jnp.where(low, found[0], found[1])
            send(4 * pair + i)

    def full_depth(i, r):
        full = []
        for j in range(4):
            at = (i * 4 + j) // 2 * 128
            own = nodes[8 * r : 8 * r + 8, at : at + 128]
            near = jnp.where(first, own, 0.0)
            deep = jnp.where(first, 0.0, own)
            if j % 2 == 0:
                full.append(jnp.where(low, near, roll(deep, 64)))
            else:
                full.append(jnp.where(low, roll(near, 64), deep))
        return full

    supports = [jnp.where(sub < 4, a, pltpu.roll(b, 4, 0)) for a, b in zip(full_depth(0, 1), full_depth(1, 1))]
    members = [full_depth(0, 0), full_depth(1, 0), supports]
    members += [[grid[8 * j : 8 * j + 8] for j in range(4)] for grid in grids]
    for at, full in enumerate(members):
        for chip in range(CHIPS):
            start = 8 * chip - 12
            spot = lane % 32 + start
            tile = jnp.zeros((8, 128), f32)
            for j in range(4):
                tile = jnp.where(lane // 32 == j, roll(full[j], 32 * j - start), tile)
            out[chip, 8 + at] = jnp.where((spot >= 0) & (spot < 128), tile, 0.0)
        send(8 + at)
    for copy in sent:
        copy.wait()


def low_mask(shape):
    return lanes(shape) < 64


def window(core, places, then):
    for c in range(2):
        @pl.when(core[0] == c)
        def _():
            then(places[c])


def face(p, q):
    return 2.0 * p * q / jnp.maximum(p + q, tiny)


def cell_coefs(least, most, start, source, storage, perm, coef, fixed, inverse):
    keep_top = rows((32, 128)) < 31
    outer = face(perm(least - 1), perm(least)) if least else jnp.zeros((32, 128), f32)
    for x in range(least, most):
        p = perm(x)
        inner = face(p, perm(x + 1) if x < PLANES - 1 else roll(p, 64))
        up = jnp.where(keep_top, face(p, roll(p, 31, 0)), 0.0)
        deep = face(p, roll(p, 127))
        coef[0, x - least] = inner
        coef[1, x - least] = up
        coef[2, x - least] = deep
        total = inner + outer + up + roll(up, 1, 0) + deep + roll(deep, 1)
        outer = inner
        store = storage(x)
        inverse[x - least] = jnp.where(store > 0.0, 1.0 / (store + stabilize + total), 0.0)
        fixed[x - least] = source(x) + store * start(x)


def both(early, late):
    return lambda x: early[x] if x < EARLY else late[x - EARLY]


def both_faces(early, late):
    return lambda way, x: early[way, x] if x < EARLY else late[way, x - EARLY]


def one_sweep(src, dst, coef, rhs, inverse, least):
    outer = coef(0, least - 1) * src[least - 1]
    p = src[least]
    for x in range(least, PLANES):
        q = src[x + 1] if x < PLANES - 1 else roll(p, 64)
        inner, up, deep = coef(0, x), coef(1, x), coef(2, x)
        total = rhs[x] + inner * q + outer
        total = total + up * roll(p, 31, 0) + roll(up * p, 1, 0)
        total = total + deep * roll(p, 127) + roll(deep * p, 1)
        dst[x] = total * inverse(x)
        outer = inner * p
        p = q


def sweeps(press, coef, rhs, inverse, first):
    for n in range(SWEEPS):
        one_sweep(press.at[n % 2], press.at[1 - n % 2], coef, rhs, inverse, first + n)


def pair_matrix():
    cell = rows((128, 256))
    n = lanes((128, 256))
    hit = (cell // 2 % 32 == n % 32) & (cell // 64 == n // 128)
    return jnp.where(hit, 0.125, 0.0).astype(bf16)


def row_mask(shape):
    return lanes(shape) % 128 // 32 == rows(shape) % 8 // 2


def block_means(press, means, least, most):
    sums = jnp.concatenate([press[2 * q] + press[2 * q + 1] for q in range(3, 8)], axis=0)
    matrix = pair_matrix()
    got = jnp.zeros((160, 256), f32)
    for part in three_parts(sums):
        got = got + jnp.dot(part, matrix, preferred_element_type=f32)
    got = jnp.where(row_mask((160, 256)), got, 0.0)
    for b in range(least, most + 1):
        q, side = (b, 0) if b < 8 else (15 - b, 128)
        piece = got[32 * q - 96 : 32 * q - 64, side : side + 128]
        for y in range(4):
            means[b, 0:1, 128 * y : 128 * y + 128] = jnp.sum(piece[8 * y : 8 * y + 8], axis=0, keepdims=True)


def last_row(shape):
    return lanes(shape) // 32 % 16 == 15


def corner_rolls(u):
    last = last_row(u.shape)
    return [
        u,
        roll(u, 511),
        jnp.where(last, 0.0, roll(u, 480)),
        jnp.where(last, 0.0, roll(u, 479)),
    ]


def assembled(here, under):
    summed = [here[8 * j : 8 * j + 8] + roll(under[8 * j : 8 * j + 8], 4, 0) for j in range(4)]
    last = last_row((8, 512))
    return (
        summed[0]
        + roll(summed[1], 1)
        + roll(jnp.where(last, 0.0, summed[2] + roll(summed[3], 1)), 32)
    )


def diag_of(lam, mu, sup, aux, safe, gain):
    depth = lanes((8, 512)) % 32
    inside = (depth >= 6) & (depth < 26)
    terms = {}
    for b in range(3, 12):
        terms[b] = aux[:, 1:2] * lam[b] + aux[:, 2:3] * mu[b]
        if b > 3:
            node_sup = sup[b]
            total = node_sup + assembled(terms[b], terms[b - 1])
            valid = inside & (node_sup > 0.0)
            safe[b] = jnp.where(valid, total, 1.0)
            gain[b] = jnp.where(valid, damping, 0.0)


def stiff_parts(stiff):
    high = stiff.astype(bf16)
    low = (stiff - high.astype(f32)).astype(bf16)
    return jnp.concatenate([high, high, low], axis=1)


def element_terms(matrix, coupling, v_here, v_next, lam, mu, press):
    vals = jnp.concatenate([a + roll(b, 4, 0) for a, b in zip(v_here, v_next)], axis=0)
    high = vals.astype(bf16)
    low = (vals - high.astype(f32)).astype(bf16)
    both = jnp.dot(matrix, jnp.concatenate([high, low, high], axis=0), preferred_element_type=f32)
    return coupling * (biot_coef * press) - (lam * both[0:32] + mu * both[32:64])


def displacements(u, lam, mu, load, sup, safe, gain, means, stiff, aux, moved, least, most):
    matrix = stiff_parts(stiff[...])
    coupling = aux[:, 0:1]

    def half(old, new, least, most):
        under = None
        v_here = corner_rolls(old[least - 1])
        for b in range(least - 1, most + 1):
            v_next = corner_rolls(old[b + 1])
            terms = element_terms(matrix, coupling, v_here, v_next, lam[b], mu[b], means[b])
            if b >= least:
                value = old[b]
                residual = load[b] - sup[b] * value + assembled(terms, under)
                new[b] = value + gain[b] * residual / safe[b]
            under = terms
            v_here = v_next

    half(u, moved.at[0], least - 1, most + 1)
    half(moved.at[0], moved.at[1], least, most)


def pack_mid(core, press, moved, out):
    low = low_mask((32, 128))
    upper = rows((8, 512)) < 4
    extra = jnp.where(low, press[10], roll(press[11], 64))
    node = jnp.where(core[0] == 0, moved[1, 10], moved[1, 5])
    pairs = [(moved[1, 6], moved[1, 7]), (moved[1, 8], moved[1, 9])]
    held = [jnp.where(upper, a, roll(b, 4, 0)) for a, b in pairs] + [node]
    for y in range(4):
        for q in range(4):
            out[y, q] = press[12 + q, 8 * y : 8 * y + 8]
        out[y, 4] = extra[8 * y : 8 * y + 8]
        for q in range(3):
            out[y, 5 + q] = held[q][:, 128 * y : 128 * y + 128]


def pack_last(press, moved, out):
    lane = lanes((32, 128))
    for x in range(2):
        cells = jnp.zeros((32, 128), f32)
        for i in range(4):
            if x == 0:
                tile = roll(press[12 + i], 16 * i - 24)
            else:
                tile = roll(press[15 - i], 16 * i - 88)
            cells = jnp.where(lane // 16 == i, tile, cells)
        for y in range(4):
            total = cells[8 * y : 8 * y + 8]
            for i in range(2):
                tile = moved[1, 6 + 2 * x + i, :, 128 * y : 128 * y + 128]
                for j in range(4):
                    total = jnp.where(lane[0:8] // 8 == 8 + 4 * i + j, roll(tile, 52 + 32 * i - 24 * j), total)
            out[4 * x + y] = total


def inside_flags(core, layer):
    below = jnp.where(layer[0] > 0, 1.0, 0.0)
    above = jnp.where(layer[0] < 7, 1.0, 0.0)
    first = core[0] == 0
    return jnp.where(first, below, above), jnp.where(first, above, below)


def units_of(grid, halo, share, ok):
    def plane(x):
        return lambda y, at: grid[4 * x + y, at]

    def near(y, at):
        return halo[13 * y + at] * ok[0]

    def middle(y, at):
        return halo[52 + 10 * y + at] * ok[0] if at < 10 else jnp.zeros((8, 128), f32)

    def far(y, at):
        if at not in FAR:
            return jnp.zeros((8, 128), f32)
        at = 92 + 2 * y + at - 2 if at < 4 else 100 + 4 * y + at - 6
        return halo[at] * ok[0]

    def beside(y, at):
        return jnp.zeros((8, 128), f32) if share is None else share[13 * y + at] * ok[1]

    inside = [plane(x) for x in range(4)]
    return [[far, middle, near] + inside + [beside], [beside] + inside + [near, middle, far]]


def unpack_cells(units, planes, press, source, storage, perm):
    low = low_mask((32, 128))

    def tile(cell, at):
        return jnp.concatenate([units[cell // 4](y, at + cell % 4) for y in range(4)], axis=0)

    for x in planes:
        a = tile(x, 0)
        b = tile(31 - x, 0)
        press(x)[...] = jnp.where(low, a, roll(b, 64))
        source(x)[...] = jnp.where(low, roll(a, 64), b)
        a = tile(x, 4)
        b = tile(31 - x, 4)
        storage(x)[...] = jnp.where(low, a, roll(b, 64))
        perm(x)[...] = jnp.where(low, roll(a, 64), b)


def prepare_kernel(
    core, layer, grid, halo, aux,
    start, edge, coef, fixed, inverse, u, lam, mu, load, sup, safe, gain,
    source, storage, perm,
):
    ok = inside_flags(core, layer)
    def unpack(units):
        unpack_cells(
            units, range(4, PLANES), lambda x: start.at[x - 4], lambda x: source.at[x],
            lambda x: storage.at[x], lambda x: perm.at[x],
        )
        sub = rows((8, 128))
        for unit in range(8):
            for y in range(4):
                at = slice(128 * y, 128 * y + 128)
                for i in range(2):
                    n = 2 * unit + i
                    tile_a = units[unit](y, 8 + i)
                    u[n, :, at] = jnp.where(sub < 3, tile_a, 0.0)
                    if 4 <= n <= 11:
                        load[n, :, at] = jnp.where(sub < 3, pltpu.roll(tile_a, 4, 0), 0.0)
                        tile_b = units[unit](y, 10)
                        if i == 1:
                            tile_b = pltpu.roll(tile_b, 4, 0)
                        sup[n, :, at] = jnp.where(sub < 3, tile_b, 0.0)
            if 1 <= unit <= 5:
                for at, param in ((11, lam), (12, mu)):
                    total = units[unit](0, at) + units[unit](1, at) + units[unit](2, at) + units[unit](3, at)
                    for i in range(2):
                        for y in range(4):
                            row = 4 * i + y
                            param[2 * unit + i, :, 128 * y : 128 * y + 128] = total[row : row + 1]

    window(core, units_of(grid, halo, None, ok), unpack)
    cell_coefs(
        EARLY, PLANES, lambda x: start[x - 4], lambda x: source[x], lambda x: storage[x],
        lambda x: perm[x], coef, fixed, inverse,
    )
    edge[0] = perm[4]
    edge[1] = perm[5]
    edge[2] = source[4]
    edge[3] = storage[4]
    diag_of(lam, mu, sup, aux, safe, gain)


def first_kernel(
    core, layer, halo, share, stiff, aux,
    start, edge, coef_late, fixed_late, inverse_late, u, lam, mu, load, sup, safe, gain,
    mid, coef_early, fixed_early, inverse_early, beside,
    press, source, storage, perm, rhs, means, moved,
):
    ok = inside_flags(core, layer)
    sub = rows((8, 128))

    def unpack(units):
        unpack_cells(
            units, range(4), lambda x: press.at[0, x], lambda x: source.at[x],
            lambda x: storage.at[x], lambda x: perm.at[x],
        )

    window(core, units_of(None, halo, share, ok), unpack)
    for y in range(4):
        for i in range(2):
            tile = share[13 * y + 8 + i] * ok[1]
            beside[i, :, 128 * y : 128 * y + 128] = jnp.where(sub < 3, tile, 0.0)
    for x in range(4, PLANES):
        press[0, x] = start[x - 4]
    cell_coefs(
        0, EARLY, lambda x: press[0, x],
        lambda x: source[x] if x < 4 else edge[2], lambda x: storage[x] if x < 4 else edge[3],
        lambda x: perm[x] if x < 4 else edge[x - 4], coef_early, fixed_early, inverse_early,
    )
    fixed = both(fixed_early, fixed_late)
    for x in range(PLANES):
        rhs[x] = fixed(x) + stabilize * press[0, x]
    sweeps(press, both_faces(coef_early, coef_late), rhs, both(inverse_early, inverse_late), 1)
    block_means(press.at[0], means, 3, 11)
    displacements(u, lam, mu, load, sup, safe, gain, means, stiff, aux, moved, 5, 10)
    pack_mid(core, press.at[0], moved, mid)


def node_of(ref, k, y):
    value = ref[y, 5 + k // 2]
    return jnp.where(rows((8, 128)) < 4, roll(value, 4, 0) if k % 2 else value, 0.0)


def strain_rows(aux, nodes, blocks, strain):
    last_y = last_row((8, 512))
    column = [jnp.broadcast_to(aux[8 * j : 8 * j + 8, 0:1], (8, 512)) for j in range(4)]
    for b in blocks:
        pair = nodes(b) + roll(nodes(b + 1), 4, 0)
        parts = [column[j] * pair for j in range(4)]
        total = (
            parts[0]
            + roll(parts[1], 511)
            + jnp.where(last_y, 0.0, roll(parts[2] + roll(parts[3], 511), 480))
        )
        strain[b] = jnp.sum(total, axis=0, keepdims=True)


def right_sides(strain, groups, press, fixed, rhs):
    mask = row_mask((8, 128))
    spread = []
    for q in groups:
        for y in range(4):
            at = slice(128 * y, 128 * y + 128)
            pair = [jnp.where(mask, strain[q, :, at], 0.0), jnp.where(mask, strain[15 - q, :, at], 0.0)]
            spread.append(jnp.concatenate(pair, axis=1))
    matrix = pair_matrix()
    got = jnp.zeros((32 * len(groups), 128), f32)
    for part in three_parts(jnp.concatenate(spread, axis=0)):
        got = got + nt_dot(part, matrix)
    for n, q in enumerate(groups):
        change = got[32 * n : 32 * n + 32]
        for x in (2 * q, 2 * q + 1):
            rhs[x] = fixed(x) + stabilize * press[x] - (8.0 * biot_coef) * change


def resume_kernel(core, layer, own, partner, near, aux, start, fixed_late, press, u, rhs, strain, moved):
    ok = inside_flags(core, layer)
    low = low_mask((32, 128))

    def unpack(runs, extra_cells, extra_node):
        def piece(cell, want_low):
            if cell in extra_cells:
                ref, q, is_low = near, 4, cell == 2
            elif 4 <= cell < 28:
                k = (cell - 4) % 8
                ref, q, is_low = runs[(cell - 4) // 8][0], min(k, 7 - k), k < 4
            else:
                return jnp.zeros((32, 128), f32)
            value = ref[:, q].reshape(32, 128)
            return value if is_low == want_low else roll(value, 64)

        for x in range(2, PLANES):
            press[x] = jnp.where(low, piece(x, True), piece(31 - x, False))
        for n in range(1, 15):
            if n == extra_node:
                ref, k, flag = near, 4, 0
            elif 2 <= n < 14:
                (ref, flag), k = runs[(n - 2) // 4], (n - 2) % 4
            else:
                u[n] = jnp.zeros((8, 512), f32)
                continue
            for y in range(4):
                value = node_of(ref, k, y)
                u[n, :, 128 * y : 128 * y + 128] = value if flag is None else value * ok[flag]

    @pl.when(core[0] == 0)
    def _():
        unpack([(near, 0), (own, None), (partner, None)], (2, 3), 1)

    @pl.when(core[0] == 1)
    def _():
        unpack([(partner, None), (own, None), (near, 0)], (), 14)

    for n in range(3, 14):
        moved[n] = u[n] - start[n]
    strain_rows(aux, lambda n: moved[n], range(3, 13), strain)
    right_sides(strain, range(3, 8), press, lambda x: fixed_late[x - EARLY], rhs)


def second_kernel(
    core, layer, across, stiff, aux, held, u, rhs_late,
    coef_late, fixed_late, inverse_late, start, lam, mu, load, sup, safe, gain,
    coef_early, fixed_early, inverse_early, beside,
    last, press, rhs, means, nodes, strain, moved,
):
    ok = inside_flags(core, layer)
    low = low_mask((32, 128))
    first = core[0] == 0
    for x in range(2, PLANES):
        press[0, x] = held[x]
    for x in range(6, PLANES):
        rhs[x] = rhs_late[x]
    for n in range(2, 14):
        nodes[n] = u[n]

    for x, q in ((2, 1), (3, 0)):
        turned = roll(across[:, q].reshape(32, 128), 64)
        press[0, x] = jnp.where(low & jnp.logical_not(first), turned, held[x])
    for y in range(4):
        at = slice(128 * y, 128 * y + 128)
        nodes[1, :, at] = jnp.where(first, u[1, :, at], node_of(across, 3, y) * ok[1])
        nodes[14, :, at] = jnp.where(first, node_of(across, 0, y) * ok[1], u[14, :, at])
    for n in (2, 3, 13):
        moved[0, n] = nodes[n] - start[n]
    moved[0, 1] = nodes[1] - jnp.where(first, start[1], beside[1])
    moved[0, 14] = nodes[14] - jnp.where(first, beside[0], start[14])
    strain[14] = jnp.zeros((1, 512), f32)
    strain_rows(aux, lambda n: moved[0, n], (1, 2, 13), strain)
    right_sides(strain, (1, 2), press.at[0], both(fixed_early, fixed_late), rhs)
    sweeps(press, both_faces(coef_early, coef_late), rhs, both(inverse_early, inverse_late), 3)
    block_means(press.at[0], means, 4, 10)
    displacements(nodes, lam, mu, load, sup, safe, gain, means, stiff, aux, moved, 6, 9)
    pack_last(press.at[0], moved, last)


def unpack_kernel(core, got, pressure, disp, held):
    lane = lanes((8, 128))
    base = core[0] * 8
    tiles = [got[base + s] for s in range(8)]
    for i in range(4):
        total = jnp.zeros((8, 128), f32)
        for s in range(8):
            total = jnp.where(lane // 16 == s, roll(tiles[s], 16 * s - 16 * i), total)
        pressure[i] = total
    for i in range(2):
        for pair in range(2):
            total = jnp.zeros((8, 128), f32)
            for s in range(8):
                for side in range(2):
                    shift = 64 * side + 8 * s - 64 - 32 * i - 8 * (2 * pair + side)
                    total = jnp.where(lane // 8 == 8 * side + s, roll(tiles[s], shift), total)
            held[:, 128 * (2 * i + pair) : 128 * (2 * i + pair) + 128] = total
    disp[...] = held[0:3]


def corner_major(stiff):
    grid = stiff.reshape(3, 2, 4, 3, 2, 4).transpose(2, 1, 0, 5, 4, 3)
    return jnp.pad(grid, ((0, 0), (0, 0), (0, 1), (0, 0), (0, 0), (0, 1))).reshape(32, 32)


def corner_column(vec):
    return jnp.pad(vec.reshape(3, 2, 4).transpose(2, 1, 0), ((0, 0), (0, 0), (0, 1))).reshape(32)


def shape(*dims):
    return jax.ShapeDtypeStruct(dims, f32)


def shards(
    pressure_start, source, storage, perm_class, class_perm, block_route, displacement_start,
    load, support, lame_lambda, lame_mu, stiff_lambda, stiff_mu, coupling_vec,
):
    core = lax.axis_index("grp")
    core_arg = jnp.full((1,), core, jnp.int32)
    row_arg = jnp.full((1,), lax.axis_index("gy"), jnp.int32)
    layer = lax.axis_index("gz")
    layer_arg = jnp.full((1,), layer, jnp.int32)
    swap = [(0, 1), (1, 0)]

    packed = call(
        pack_kernel,
        shape(16, TILES, 8, 128),
        [SM, SM, SM] + [HB] * 11,
        [
            pltpu.VMEM((16, 8, 128), f32),
            pltpu.VMEM((16, 512), f32),
            pltpu.VMEM((1, 8, 512), jnp.int32),
            pltpu.VMEM((4, 8, 128), jnp.int32),
            pltpu.VMEM((3, 3, 512), f32),
            pltpu.VMEM((2, 1, 512), f32),
            pltpu.SMEM((CLASSES,), f32),
            pltpu.VMEM((16, TILES, 8, 128), f32),
            pltpu.SemaphoreType.DMA((11,)),
            pltpu.SemaphoreType.DMA((TILES,)),
        ],
        WHOLE,
        HB,
    )(core_arg, row_arg, layer_arg, class_perm, pressure_start, source, storage, perm_class,
      displacement_start, load, support, lame_lambda, lame_mu, block_route)
    grid = lax.all_to_all(packed, ("gx", "gy"), 0, 0, tiled=True)
    grid, core, layer, stiff_lambda, stiff_mu, coupling_vec = lax.optimization_barrier(
        (grid, core, layer, stiff_lambda, stiff_mu, coupling_vec)
    )
    core_arg = jnp.full((1,), core, jnp.int32)
    layer_arg = jnp.full((1,), layer, jnp.int32)

    ring = [(8 + z, (z + 1) % 8) for z in range(8)] + [(z, 8 + (z - 1) % 8) for z in range(8)]
    grid = grid + lax.ppermute(grid, "grp", swap)
    first = core == 0
    sent = [
        jnp.where(first, grid[0:4], grid[12:16]),
        jnp.where(first, grid[4:8, :10], grid[8:12, :10]),
        jnp.where(first, grid[8:12, 2:4], grid[4:8, 2:4]),
        jnp.where(first, grid[8:12, 6:10], grid[4:8, 6:10]),
    ]
    sent = jnp.concatenate([part.reshape(-1, 8, 128) for part in sent], axis=0)
    halo = lax.ppermute(sent, ("grp", "gz"), ring)
    share = lax.ppermute(halo[:52], "grp", swap)

    stiff = jnp.concatenate([corner_major(stiff_lambda), corner_major(stiff_mu)], axis=0)
    columns = [corner_column(coupling_vec), corner_column(jnp.diag(stiff_lambda)), corner_column(jnp.diag(stiff_mu))]
    aux = jnp.pad(jnp.stack(columns, axis=1), ((0, 0), (0, 125)))

    late = PLANES - EARLY
    statics = call(
        prepare_kernel,
        (
            shape(PLANES - 4, 32, 128), shape(4, 32, 128),
            shape(3, late, 32, 128), shape(late, 32, 128), shape(late, 32, 128),
            shape(NODES, 8, 512), shape(12, 1, 512), shape(12, 1, 512), shape(12, 8, 512),
            shape(12, 8, 512), shape(12, 8, 512), shape(12, 8, 512),
        ),
        [SM, SM] + [VM] * 3,
        [pltpu.VMEM((PLANES, 32, 128), f32)] * 3,
    )(core_arg, layer_arg, grid, halo, aux)
    mid, *early = call(
        first_kernel,
        (
            shape(4, 8, 8, 128), shape(3, EARLY, 32, 128), shape(EARLY, 32, 128),
            shape(EARLY, 32, 128), shape(2, 8, 512),
        ),
        [SM, SM] + [VM] * 16,
        [
            pltpu.VMEM((2, PLANES, 32, 128), f32),
            pltpu.VMEM((4, 32, 128), f32),
            pltpu.VMEM((4, 32, 128), f32),
            pltpu.VMEM((4, 32, 128), f32),
            pltpu.VMEM((PLANES, 32, 128), f32),
            pltpu.VMEM((PLANES, 1, 512), f32),
            pltpu.VMEM((2, NODES, 8, 512), f32),
        ],
    )(core_arg, layer_arg, halo, share, stiff, aux, *statics)

    near = lax.ppermute(mid, ("grp", "gz"), ring)
    partner = lax.ppermute(mid, "grp", swap)
    across = lax.ppermute(near, "grp", swap)
    resumed = call(
        resume_kernel,
        (shape(PLANES, 32, 128), shape(NODES, 8, 512), shape(PLANES, 32, 128)),
        [SM, SM] + [VM] * 6,
        [pltpu.VMEM((PLANES, 1, 512), f32), pltpu.VMEM((NODES, 8, 512), f32)],
    )(core_arg, layer_arg, mid, partner, near, aux, statics[5], statics[3])
    last = call(
        second_kernel,
        shape(8, 8, 128),
        [SM, SM] + [VM] * 20,
        [
            pltpu.VMEM((2, PLANES, 32, 128), f32),
            pltpu.VMEM((PLANES, 32, 128), f32),
            pltpu.VMEM((PLANES, 1, 512), f32),
            pltpu.VMEM((NODES, 8, 512), f32),
            pltpu.VMEM((PLANES, 1, 512), f32),
            pltpu.VMEM((2, NODES, 8, 512), f32),
        ],
    )(core_arg, layer_arg, across, stiff, aux, *resumed, *statics[2:], *early)

    other = lax.ppermute(last, "grp", swap)
    whole = jnp.concatenate([jnp.where(core == 0, last, other), jnp.where(core == 0, other, last)], axis=0)
    back = lax.all_to_all(whole, ("gx", "gy"), 0, 0, tiled=True)
    return call(
        unpack_kernel,
        (shape(4, 8, 128), shape(3, 512)),
        [SM, VM],
        [pltpu.VMEM((8, 512), f32)],
    )(core_arg, back)


def solution(mesh):
    fine = Mesh(np.asarray(mesh.devices).reshape(2, 8, 4, 4), ("grp", "gz", "gx", "gy"))
    cell = P(("gz", "gx"), "gy", "grp")
    node = P(None, ("grp", "gz", "gx", "gy"))
    elem = P(("grp", "gz", "gx", "gy"), None)
    return jax.shard_map(
        shards,
        mesh=fine,
        in_specs=(
            cell, cell, cell, cell, P(), P(("gz", "gx"), None, None), node, node, node, elem, elem,
            P(), P(), P(),
        ),
        out_specs=(cell, node),
        check_vma=False,
    )
```

```python
import jax
import jax.numpy as jnp
import numpy as np
from jax import lax
from jax.experimental import pallas as pl
from jax.experimental.pallas import tpu as pltpu
from jax.sharding import Mesh
from jax.sharding import PartitionSpec as P

SWEEPS = 6
CLASSES = 16
CHIPS = 16
PLANES = 16
NODES = 16
TILES = 13
EARLY = 5
FAR = (2, 3, 6, 7, 8)

stabilize = 0.5
biot_coef = 0.8
damping = 0.7
tiny = 1e-30

f32 = jnp.float32
bf16 = jnp.bfloat16

VM = pl.BlockSpec(memory_space=pltpu.VMEM)
SM = pl.BlockSpec(memory_space=pltpu.SMEM)
HB = pl.BlockSpec(memory_space=pltpu.HBM)
WHOLE = 64 * 1024 * 1024 - 65536


def call(body, out_shapes, in_specs, scratch=(), budget=40 * 1024 * 1024, out_spec=VM):
    return pl.pallas_call(
        body,
        out_shape=out_shapes,
        in_specs=in_specs,
        out_specs=jax.tree.map(lambda _: out_spec, out_shapes),
        scratch_shapes=list(scratch),
        compiler_params=pltpu.CompilerParams(vmem_limit_bytes=budget),
    )


def lanes(shape):
    return lax.broadcasted_iota(jnp.int32, shape, 1)


def rows(shape):
    return lax.broadcasted_iota(jnp.int32, shape, 0)


def roll(x, shift, axis=1):
    shift = shift % x.shape[axis]
    return x if shift == 0 else pltpu.roll(x, shift, axis)


def three_parts(x):
    high = x.astype(bf16)
    rest = x - high.astype(f32)
    middle = rest.astype(bf16)
    return high, middle, (rest - middle.astype(f32)).astype(bf16)


def nt_dot(a, b):
    return lax.dot_general(a, b, (((1,), (1,)), ((), ())), preferred_element_type=f32)


def pack_kernel(
    core, across, layer, perms, p0, src, sto, cls, disp, load, sup, lam, mu, blocks,
    packed, cells, nodes, routes, held, small, pair, classes, out, sems, done,
):
    copies = [
        pltpu.make_async_copy(perms, classes, sems.at[0]),
        pltpu.make_async_copy(cls, held, sems.at[1]),
        pltpu.make_async_copy(p0, cells.at[0:4], sems.at[2]),
        pltpu.make_async_copy(src, cells.at[4:8], sems.at[3]),
        pltpu.make_async_copy(sto, cells.at[8:12], sems.at[4]),
        pltpu.make_async_copy(disp, small.at[0], sems.at[5]),
        pltpu.make_async_copy(load, small.at[1], sems.at[6]),
        pltpu.make_async_copy(sup, small.at[2], sems.at[7]),
        pltpu.make_async_copy(lam, pair.at[0], sems.at[8]),
        pltpu.make_async_copy(mu, pair.at[1], sems.at[9]),
        pltpu.make_async_copy(blocks, routes, sems.at[10]),
    ]
    for copy in copies:
        copy.start()
    nodes[...] = jnp.zeros((24, 512), f32)
    for copy in copies:
        copy.wait()
    for i in range(4):
        which = held[i]
        perm = jnp.zeros((8, 128), f32)
        for member in range(CLASSES):
            perm = jnp.where(which == member, classes[member], perm)
        cells[12 + i] = perm
    nodes[0:3] = small[0]
    nodes[8:11] = small[1]
    nodes[16:19] = small[2]
    sent = []

    def send(at):
        sent.append(pltpu.make_async_copy(out.at[:, at], packed.at[:, at], done.at[at]))
        sent[-1].start()

    first = core[0] == 0
    lane = lanes((8, 128))
    low = lane < 64
    sub = rows((8, 128))

    device = lanes((1, 512)) // 64
    mine = jnp.zeros((8, 128), jnp.int32)
    for k in range(8):
        at = k // 2 * 128
        here = (core[0] == k // 4) & (across[0] == k % 4)
        mine = jnp.where(here, roll(routes[0, :, at : at + 128], 64 * (k % 2)), mine)
    block = jnp.concatenate(
        [jnp.where(low[0:1], mine[2 * m : 2 * m + 1], roll(mine[2 * m + 1 : 2 * m + 2], 64)) for m in range(4)],
        axis=1,
    )
    row = block // 64 % 4 * 8 + block // 256 * 4 + device % 4
    depth = device // 4 * 64 + block % 64
    at_row = rows((32, 512)) == row
    at_depth = jnp.where(rows((128, 512)) == depth, 1.0, 0.0).astype(bf16)
    spread = [
        jnp.where(at_row, part.astype(f32), 0.0) for v in range(2) for part in three_parts(pair[v])
    ]
    placed = nt_dot(jnp.concatenate(spread, axis=0).astype(bf16), at_depth)
    grids = [placed[96 * v : 96 * v + 32] + placed[96 * v + 32 : 96 * v + 64] + placed[96 * v + 64 : 96 * v + 96] for v in range(2)]

    for pair in range(2):
        for i in range(4):
            tiles = []
            for field in (2 * pair, 2 * pair + 1):
                own = cells[4 * field + i]
                tiles.append((jnp.where(first, own, 0.0), jnp.where(first, 0.0, own)))
            for chip in range(CHIPS):
                start = 16 * chip - 24
                spot = lane % 64 + start
                in_low = (spot >= 0) & (spot < 128)
                in_high = (spot >= 128) & (spot < 256)
                found = []
                for member in range(2):
                    shift = 64 * member - start
                    win = jnp.zeros((8, 128), f32)
                    if start < 128:
                        win = jnp.where(in_low, roll(tiles[member][0], shift), win)
                    if start + 64 > 128:
                        win = jnp.where(in_high, roll(tiles[member][1], shift), win)
                    found.append(win)
                out[chip, 4 * pair + i] = jnp.where(low, found[0], found[1])
            send(4 * pair + i)

    def full_depth(i, r):
        full = []
        for j in range(4):
            at = (i * 4 + j) // 2 * 128
            own = nodes[8 * r : 8 * r + 8, at : at + 128]
            near = jnp.where(first, own, 0.0)
            deep = jnp.where(first, 0.0, own)
            if j % 2 == 0:
                full.append(jnp.where(low, near, roll(deep, 64)))
            else:
                full.append(jnp.where(low, roll(near, 64), deep))
        return full

    members = [
        [jnp.where(sub < 4, a, pltpu.roll(b, 4, 0)) for a, b in zip(full_depth(0, r), full_depth(1, r))]
        for r in range(3)
    ]
    members += [[grid[8 * j : 8 * j + 8] for j in range(4)] for grid in grids]
    for at, full in enumerate(members):
        for chip in range(CHIPS):
            start = 8 * chip - 12
            spot = lane % 32 + start
            tile = jnp.zeros((8, 128), f32)
            for j in range(4):
                tile = jnp.where(lane // 32 == j, roll(full[j], 32 * j - start), tile)
            out[chip, 8 + at] = jnp.where((spot >= 0) & (spot < 128), tile, 0.0)
        send(8 + at)
    for copy in sent:
        copy.wait()


def low_mask(shape):
    return lanes(shape) < 64


def window(core, places, then):
    for c in range(2):
        @pl.when(core[0] == c)
        def _():
            then(places[c])


def face(p, q):
    return 2.0 * p * q / jnp.maximum(p + q, tiny)


def cell_coefs(least, most, start, source, storage, perm, coef, fixed, inverse):
    keep_top = rows((32, 128)) < 31
    outer = face(perm(least - 1), perm(least)) if least else jnp.zeros((32, 128), f32)
    for x in range(least, most):
        p = perm(x)
        inner = face(p, perm(x + 1) if x < PLANES - 1 else roll(p, 64))
        up = jnp.where(keep_top, face(p, roll(p, 31, 0)), 0.0)
        deep = face(p, roll(p, 127))
        coef[0, x - least] = inner
        coef[1, x - least] = up
        coef[2, x - least] = deep
        total = inner + outer + up + roll(up, 1, 0) + deep + roll(deep, 1)
        outer = inner
        store = storage(x)
        inverse[x - least] = jnp.where(store > 0.0, 1.0 / (store + stabilize + total), 0.0)
        fixed[x - least] = source(x) + store * start(x)


def both(early, late):
    return lambda x: early[x] if x < EARLY else late[x - EARLY]


def both_faces(early, late):
    return lambda way, x: early[way, x] if x < EARLY else late[way, x - EARLY]


def one_sweep(src, dst, coef, rhs, inverse, least):
    outer = coef(0, least - 1) * src[least - 1]
    p = src[least]
    for x in range(least, PLANES):
        q = src[x + 1] if x < PLANES - 1 else roll(p, 64)
        inner, up, deep = coef(0, x), coef(1, x), coef(2, x)
        total = rhs[x] + inner * q + outer
        total = total + up * roll(p, 31, 0) + roll(up * p, 1, 0)
        total = total + deep * roll(p, 127) + roll(deep * p, 1)
        dst[x] = total * inverse(x)
        outer = inner * p
        p = q


def sweeps(press, coef, rhs, inverse, first):
    for n in range(SWEEPS):
        one_sweep(press.at[n % 2], press.at[1 - n % 2], coef, rhs, inverse, first + n)


def pair_matrix():
    cell = rows((128, 256))
    n = lanes((128, 256))
    hit = (cell // 2 % 32 == n % 32) & (cell // 64 == n // 128)
    return jnp.where(hit, 0.125, 0.0).astype(bf16)


def row_mask(shape):
    return lanes(shape) % 128 // 32 == rows(shape) % 8 // 2


def block_means(press, means, least, most):
    sums = jnp.concatenate([press[2 * q] + press[2 * q + 1] for q in range(3, 8)], axis=0)
    matrix = pair_matrix()
    got = jnp.zeros((160, 256), f32)
    for part in three_parts(sums):
        got = got + jnp.dot(part, matrix, preferred_element_type=f32)
    got = jnp.where(row_mask((160, 256)), got, 0.0)
    for b in range(least, most + 1):
        q, side = (b, 0) if b < 8 else (15 - b, 128)
        piece = got[32 * q - 96 : 32 * q - 64, side : side + 128]
        for y in range(4):
            means[b, 0:1, 128 * y : 128 * y + 128] = jnp.sum(piece[8 * y : 8 * y + 8], axis=0, keepdims=True)


def last_row(shape):
    return lanes(shape) // 32 % 16 == 15


def corner_rolls(u):
    last = last_row(u.shape)
    return [
        u,
        roll(u, 511),
        jnp.where(last, 0.0, roll(u, 480)),
        jnp.where(last, 0.0, roll(u, 479)),
    ]


def assembled(here, under):
    summed = [here[8 * j : 8 * j + 8] + roll(under[8 * j : 8 * j + 8], 4, 0) for j in range(4)]
    last = last_row((8, 512))
    return (
        summed[0]
        + roll(summed[1], 1)
        + roll(jnp.where(last, 0.0, summed[2] + roll(summed[3], 1)), 32)
    )


def diag_of(lam, mu, sup, aux, safe, gain):
    depth = lanes((8, 512)) % 32
    inside = (depth >= 6) & (depth < 26)
    terms = {}
    for b in range(3, 12):
        terms[b] = aux[:, 1:2] * lam[b] + aux[:, 2:3] * mu[b]
        if b > 3:
            node_sup = sup[b]
            total = node_sup + assembled(terms[b], terms[b - 1])
            valid = inside & (node_sup > 0.0)
            safe[b] = jnp.where(valid, total, 1.0)
            gain[b] = jnp.where(valid, damping, 0.0)


def stiff_parts(stiff):
    high = stiff.astype(bf16)
    low = (stiff - high.astype(f32)).astype(bf16)
    return jnp.concatenate([high, high, low], axis=1)


def element_terms(matrix, coupling, v_here, v_next, lam, mu, press):
    vals = jnp.concatenate([a + roll(b, 4, 0) for a, b in zip(v_here, v_next)], axis=0)
    high = vals.astype(bf16)
    low = (vals - high.astype(f32)).astype(bf16)
    both = jnp.dot(matrix, jnp.concatenate([high, low, high], axis=0), preferred_element_type=f32)
    return coupling * (biot_coef * press) - (lam * both[0:32] + mu * both[32:64])


def displacements(u, lam, mu, load, sup, safe, gain, means, stiff, aux, moved, least, most):
    matrix = stiff_parts(stiff[...])
    coupling = aux[:, 0:1]

    def half(old, new, least, most):
        under = None
        v_here = corner_rolls(old[least - 1])
        for b in range(least - 1, most + 1):
            v_next = corner_rolls(old[b + 1])
            terms = element_terms(matrix, coupling, v_here, v_next, lam[b], mu[b], means[b])
            if b >= least:
                value = old[b]
                residual = load[b] - sup[b] * value + assembled(terms, under)
                new[b] = value + gain[b] * residual / safe[b]
            under = terms
            v_here = v_next

    half(u, moved.at[0], least - 1, most + 1)
    half(moved.at[0], moved.at[1], least, most)


def pack_mid(core, press, moved, out):
    low = low_mask((32, 128))
    upper = rows((8, 512)) < 4
    extra = jnp.where(low, press[10], roll(press[11], 64))
    node = jnp.where(core[0] == 0, moved[1, 10], moved[1, 5])
    pairs = [(moved[1, 6], moved[1, 7]), (moved[1, 8], moved[1, 9])]
    held = [jnp.where(upper, a, roll(b, 4, 0)) for a, b in pairs] + [node]
    for y in range(4):
        for q in range(4):
            out[y, q] = press[12 + q, 8 * y : 8 * y + 8]
        out[y, 4] = extra[8 * y : 8 * y + 8]
        for q in range(3):
            out[y, 5 + q] = held[q][:, 128 * y : 128 * y + 128]


def pack_last(press, moved, out):
    lane = lanes((32, 128))
    for x in range(2):
        cells = jnp.zeros((32, 128), f32)
        for i in range(4):
            if x == 0:
                tile = roll(press[12 + i], 16 * i - 24)
            else:
                tile = roll(press[15 - i], 16 * i - 88)
            cells = jnp.where(lane // 16 == i, tile, cells)
        for y in range(4):
            total = cells[8 * y : 8 * y + 8]
            for i in range(2):
                tile = moved[1, 6 + 2 * x + i, :, 128 * y : 128 * y + 128]
                for j in range(4):
                    total = jnp.where(lane[0:8] // 8 == 8 + 4 * i + j, roll(tile, 52 + 32 * i - 24 * j), total)
            out[4 * x + y] = total


def inside_flags(core, layer):
    below = jnp.where(layer[0] > 0, 1.0, 0.0)
    above = jnp.where(layer[0] < 7, 1.0, 0.0)
    first = core[0] == 0
    return jnp.where(first, below, above), jnp.where(first, above, below)


def units_of(grid, halo, share, ok):
    def plane(x):
        return lambda y, at: grid[4 * x + y, at]

    none = jnp.zeros((8, 128), f32)

    def near(y, at):
        if at < 11:
            return halo[11 * y + at] * ok[0]
        return halo[33 + at] * ok[0] if y == 0 else none

    def middle(y, at):
        return halo[46 + 9 * y + at] * ok[0] if at < 9 else none

    def far(y, at):
        if at not in FAR:
            return none
        at = 82 + 2 * y + at - 2 if at < 4 else 90 + 3 * y + at - 6
        return halo[at] * ok[0]

    def beside(y, at):
        return none if share is None else share[11 * y + at] * ok[1]

    inside = [plane(x) for x in range(4)]
    return [[far, middle, near] + inside + [beside], [beside] + inside + [near, middle, far]]


def unpack_cells(units, planes, press, source, storage, perm):
    low = low_mask((32, 128))

    def tile(cell, at):
        return jnp.concatenate([units[cell // 4](y, at + cell % 4) for y in range(4)], axis=0)

    for x in planes:
        a = tile(x, 0)
        b = tile(31 - x, 0)
        press(x)[...] = jnp.where(low, a, roll(b, 64))
        source(x)[...] = jnp.where(low, roll(a, 64), b)
        a = tile(x, 4)
        b = tile(31 - x, 4)
        storage(x)[...] = jnp.where(low, a, roll(b, 64))
        perm(x)[...] = jnp.where(low, roll(a, 64), b)


def prepare_kernel(
    core, layer, grid, halo, aux,
    start, edge, coef, fixed, inverse, u, lam, mu, load, sup, safe, gain,
    source, storage, perm,
):
    ok = inside_flags(core, layer)
    def unpack(units):
        unpack_cells(
            units, range(4, PLANES), lambda x: start.at[x - 4], lambda x: source.at[x],
            lambda x: storage.at[x], lambda x: perm.at[x],
        )
        sub = rows((8, 128))
        for unit in range(8):
            for y in range(4):
                at = slice(128 * y, 128 * y + 128)
                for member, target in ((8, u), (9, load), (10, sup)):
                    if member > 8 and not 2 <= unit <= 5:
                        continue
                    tile = units[unit](y, member)
                    target[2 * unit, :, at] = jnp.where(sub < 3, tile, 0.0)
                    target[2 * unit + 1, :, at] = jnp.where(sub < 3, pltpu.roll(tile, 4, 0), 0.0)
            if 1 <= unit <= 5:
                for at, param in ((11, lam), (12, mu)):
                    total = units[unit](0, at) + units[unit](1, at) + units[unit](2, at) + units[unit](3, at)
                    for i in range(2):
                        for y in range(4):
                            row = 4 * i + y
                            param[2 * unit + i, :, 128 * y : 128 * y + 128] = total[row : row + 1]

    window(core, units_of(grid, halo, None, ok), unpack)
    cell_coefs(
        EARLY, PLANES, lambda x: start[x - 4], lambda x: source[x], lambda x: storage[x],
        lambda x: perm[x], coef, fixed, inverse,
    )
    edge[0] = perm[4]
    edge[1] = perm[5]
    edge[2] = source[4]
    edge[3] = storage[4]
    diag_of(lam, mu, sup, aux, safe, gain)


def first_kernel(
    core, layer, halo, share, stiff, aux,
    start, edge, coef_late, fixed_late, inverse_late, u, lam, mu, load, sup, safe, gain,
    mid, coef_early, fixed_early, inverse_early, beside,
    press, source, storage, perm, rhs, means, moved,
):
    ok = inside_flags(core, layer)
    sub = rows((8, 128))

    def unpack(units):
        unpack_cells(
            units, range(4), lambda x: press.at[0, x], lambda x: source.at[x],
            lambda x: storage.at[x], lambda x: perm.at[x],
        )

    window(core, units_of(None, halo, share, ok), unpack)
    for y in range(4):
        tile = share[11 * y + 8] * ok[1]
        beside[0, :, 128 * y : 128 * y + 128] = jnp.where(sub < 3, tile, 0.0)
        beside[1, :, 128 * y : 128 * y + 128] = jnp.where(sub < 3, pltpu.roll(tile, 4, 0), 0.0)
    for x in range(4, PLANES):
        press[0, x] = start[x - 4]
    cell_coefs(
        0, EARLY, lambda x: press[0, x],
        lambda x: source[x] if x < 4 else edge[2], lambda x: storage[x] if x < 4 else edge[3],
        lambda x: perm[x] if x < 4 else edge[x - 4], coef_early, fixed_early, inverse_early,
    )
    fixed = both(fixed_early, fixed_late)
    for x in range(PLANES):
        rhs[x] = fixed(x) + stabilize * press[0, x]
    sweeps(press, both_faces(coef_early, coef_late), rhs, both(inverse_early, inverse_late), 1)
    block_means(press.at[0], means, 3, 11)
    displacements(u, lam, mu, load, sup, safe, gain, means, stiff, aux, moved, 5, 10)
    pack_mid(core, press.at[0], moved, mid)


def node_of(ref, k, y):
    value = ref[y, 5 + k // 2]
    return jnp.where(rows((8, 128)) < 4, roll(value, 4, 0) if k % 2 else value, 0.0)


def strain_rows(aux, nodes, blocks, strain):
    last_y = last_row((8, 512))
    column = [jnp.broadcast_to(aux[8 * j : 8 * j + 8, 0:1], (8, 512)) for j in range(4)]
    for b in blocks:
        pair = nodes(b) + roll(nodes(b + 1), 4, 0)
        parts = [column[j] * pair for j in range(4)]
        total = (
            parts[0]
            + roll(parts[1], 511)
            + jnp.where(last_y, 0.0, roll(parts[2] + roll(parts[3], 511), 480))
        )
        strain[b] = jnp.sum(total, axis=0, keepdims=True)


def right_sides(strain, groups, press, fixed, rhs):
    mask = row_mask((8, 128))
    spread = []
    for q in groups:
        for y in range(4):
            at = slice(128 * y, 128 * y + 128)
            pair = [jnp.where(mask, strain[q, :, at], 0.0), jnp.where(mask, strain[15 - q, :, at], 0.0)]
            spread.append(jnp.concatenate(pair, axis=1))
    matrix = pair_matrix()
    got = jnp.zeros((32 * len(groups), 128), f32)
    for part in three_parts(jnp.concatenate(spread, axis=0)):
        got = got + nt_dot(part, matrix)
    for n, q in enumerate(groups):
        change = got[32 * n : 32 * n + 32]
        for x in (2 * q, 2 * q + 1):
            rhs[x] = fixed(x) + stabilize * press[x] - (8.0 * biot_coef) * change


def resume_kernel(core, layer, own, partner, near, aux, start, fixed_late, press, u, rhs, strain, moved):
    ok = inside_flags(core, layer)
    low = low_mask((32, 128))

    def unpack(runs, extra_cells, extra_node):
        def piece(cell, want_low):
            if cell in extra_cells:
                ref, q, is_low = near, 4, cell == 2
            elif 4 <= cell < 28:
                k = (cell - 4) % 8
                ref, q, is_low = runs[(cell - 4) // 8][0], min(k, 7 - k), k < 4
            else:
                return jnp.zeros((32, 128), f32)
            value = ref[:, q].reshape(32, 128)
            return value if is_low == want_low else roll(value, 64)

        for x in range(2, PLANES):
            press[x] = jnp.where(low, piece(x, True), piece(31 - x, False))
        for n in range(1, 15):
            if n == extra_node:
                ref, k, flag = near, 4, 0
            elif 2 <= n < 14:
                (ref, flag), k = runs[(n - 2) // 4], (n - 2) % 4
            else:
                u[n] = jnp.zeros((8, 512), f32)
                continue
            for y in range(4):
                value = node_of(ref, k, y)
                u[n, :, 128 * y : 128 * y + 128] = value if flag is None else value * ok[flag]

    @pl.when(core[0] == 0)
    def _():
        unpack([(near, 0), (own, None), (partner, None)], (2, 3), 1)

    @pl.when(core[0] == 1)
    def _():
        unpack([(partner, None), (own, None), (near, 0)], (), 14)

    for n in range(3, 14):
        moved[n] = u[n] - start[n]
    strain_rows(aux, lambda n: moved[n], range(3, 13), strain)
    right_sides(strain, range(3, 8), press, lambda x: fixed_late[x - EARLY], rhs)


def second_kernel(
    core, layer, across, stiff, aux, held, u, rhs_late,
    coef_late, fixed_late, inverse_late, start, lam, mu, load, sup, safe, gain,
    coef_early, fixed_early, inverse_early, beside,
    last, press, rhs, means, nodes, strain, moved,
):
    ok = inside_flags(core, layer)
    low = low_mask((32, 128))
    first = core[0] == 0
    for x in range(2, PLANES):
        press[0, x] = held[x]
    for x in range(6, PLANES):
        rhs[x] = rhs_late[x]
    for n in range(2, 14):
        nodes[n] = u[n]

    for x, q in ((2, 1), (3, 0)):
        turned = roll(across[:, q].reshape(32, 128), 64)
        press[0, x] = jnp.where(low & jnp.logical_not(first), turned, held[x])
    for y in range(4):
        at = slice(128 * y, 128 * y + 128)
        nodes[1, :, at] = jnp.where(first, u[1, :, at], node_of(across, 3, y) * ok[1])
        nodes[14, :, at] = jnp.where(first, node_of(across, 0, y) * ok[1], u[14, :, at])
    for n in (2, 3, 13):
        moved[0, n] = nodes[n] - start[n]
    moved[0, 1] = nodes[1] - jnp.where(first, start[1], beside[1])
    moved[0, 14] = nodes[14] - jnp.where(first, beside[0], start[14])
    strain[14] = jnp.zeros((1, 512), f32)
    strain_rows(aux, lambda n: moved[0, n], (1, 2, 13), strain)
    right_sides(strain, (1, 2), press.at[0], both(fixed_early, fixed_late), rhs)
    sweeps(press, both_faces(coef_early, coef_late), rhs, both(inverse_early, inverse_late), 3)
    block_means(press.at[0], means, 4, 10)
    displacements(nodes, lam, mu, load, sup, safe, gain, means, stiff, aux, moved, 6, 9)
    pack_last(press.at[0], moved, last)


def unpack_kernel(core, got, pressure, disp, held):
    lane = lanes((8, 128))
    base = core[0] * 8
    tiles = [got[base + s] for s in range(8)]
    for i in range(4):
        total = jnp.zeros((8, 128), f32)
        for s in range(8):
            total = jnp.where(lane // 16 == s, roll(tiles[s], 16 * s - 16 * i), total)
        pressure[i] = total
    for i in range(2):
        for pair in range(2):
            total = jnp.zeros((8, 128), f32)
            for s in range(8):
                for side in range(2):
                    shift = 64 * side + 8 * s - 64 - 32 * i - 8 * (2 * pair + side)
                    total = jnp.where(lane // 8 == 8 * side + s, roll(tiles[s], shift), total)
            held[:, 128 * (2 * i + pair) : 128 * (2 * i + pair) + 128] = total
    disp[...] = held[0:3]


def corner_major(stiff):
    grid = stiff.reshape(3, 2, 4, 3, 2, 4).transpose(2, 1, 0, 5, 4, 3)
    return jnp.pad(grid, ((0, 0), (0, 0), (0, 1), (0, 0), (0, 0), (0, 1))).reshape(32, 32)


def corner_column(vec):
    return jnp.pad(vec.reshape(3, 2, 4).transpose(2, 1, 0), ((0, 0), (0, 0), (0, 1))).reshape(32)


def shape(*dims):
    return jax.ShapeDtypeStruct(dims, f32)


def shards(
    pressure_start, source, storage, perm_class, class_perm, block_route, displacement_start,
    load, support, lame_lambda, lame_mu, stiff_lambda, stiff_mu, coupling_vec,
):
    core = lax.axis_index("grp")
    core_arg = jnp.full((1,), core, jnp.int32)
    row_arg = jnp.full((1,), lax.axis_index("gy"), jnp.int32)
    layer = lax.axis_index("gz")
    layer_arg = jnp.full((1,), layer, jnp.int32)
    swap = [(0, 1), (1, 0)]

    packed = call(
        pack_kernel,
        shape(16, TILES, 8, 128),
        [SM, SM, SM] + [HB] * 11,
        [
            pltpu.VMEM((16, 8, 128), f32),
            pltpu.VMEM((24, 512), f32),
            pltpu.VMEM((1, 8, 512), jnp.int32),
            pltpu.VMEM((4, 8, 128), jnp.int32),
            pltpu.VMEM((3, 3, 512), f32),
            pltpu.VMEM((2, 1, 512), f32),
            pltpu.SMEM((CLASSES,), f32),
            pltpu.VMEM((16, TILES, 8, 128), f32),
            pltpu.SemaphoreType.DMA((11,)),
            pltpu.SemaphoreType.DMA((TILES,)),
        ],
        WHOLE,
        HB,
    )(core_arg, row_arg, layer_arg, class_perm, pressure_start, source, storage, perm_class,
      displacement_start, load, support, lame_lambda, lame_mu, block_route)
    grid = lax.all_to_all(packed, ("gx", "gy"), 0, 0, tiled=True)
    grid, core, layer, stiff_lambda, stiff_mu, coupling_vec = lax.optimization_barrier(
        (grid, core, layer, stiff_lambda, stiff_mu, coupling_vec)
    )
    core_arg = jnp.full((1,), core, jnp.int32)
    layer_arg = jnp.full((1,), layer, jnp.int32)

    ring = [(8 + z, (z + 1) % 8) for z in range(8)] + [(z, 8 + (z - 1) % 8) for z in range(8)]
    grid = grid + lax.ppermute(grid, "grp", swap)
    first = core == 0
    sent = [
        jnp.where(first, grid[0:4, :11], grid[12:16, :11]),
        jnp.sum(jnp.where(first, grid[0:4, 11:], grid[12:16, 11:]), axis=0),
        jnp.where(first, grid[4:8, :9], grid[8:12, :9]),
        jnp.where(first, grid[8:12, 2:4], grid[4:8, 2:4]),
        jnp.where(first, grid[8:12, 6:9], grid[4:8, 6:9]),
    ]
    sent = jnp.concatenate([part.reshape(-1, 8, 128) for part in sent], axis=0)
    halo = lax.ppermute(sent, ("grp", "gz"), ring)
    share = lax.ppermute(halo[:44], "grp", swap)

    stiff = jnp.concatenate([corner_major(stiff_lambda), corner_major(stiff_mu)], axis=0)
    columns = [corner_column(coupling_vec), corner_column(jnp.diag(stiff_lambda)), corner_column(jnp.diag(stiff_mu))]
    aux = jnp.pad(jnp.stack(columns, axis=1), ((0, 0), (0, 125)))

    late = PLANES - EARLY
    statics = call(
        prepare_kernel,
        (
            shape(PLANES - 4, 32, 128), shape(4, 32, 128),
            shape(3, late, 32, 128), shape(late, 32, 128), shape(late, 32, 128),
            shape(NODES, 8, 512), shape(12, 1, 512), shape(12, 1, 512), shape(12, 8, 512),
            shape(12, 8, 512), shape(12, 8, 512), shape(12, 8, 512),
        ),
        [SM, SM] + [VM] * 3,
        [pltpu.VMEM((PLANES, 32, 128), f32)] * 3,
    )(core_arg, layer_arg, grid, halo, aux)
    mid, *early = call(
        first_kernel,
        (
            shape(4, 8, 8, 128), shape(3, EARLY, 32, 128), shape(EARLY, 32, 128),
            shape(EARLY, 32, 128), shape(2, 8, 512),
        ),
        [SM, SM] + [VM] * 16,
        [
            pltpu.VMEM((2, PLANES, 32, 128), f32),
            pltpu.VMEM((4, 32, 128), f32),
            pltpu.VMEM((4, 32, 128), f32),
            pltpu.VMEM((4, 32, 128), f32),
            pltpu.VMEM((PLANES, 32, 128), f32),
            pltpu.VMEM((PLANES, 1, 512), f32),
            pltpu.VMEM((2, NODES, 8, 512), f32),
        ],
    )(core_arg, layer_arg, halo, share, stiff, aux, *statics)

    near = lax.ppermute(mid, ("grp", "gz"), ring)
    partner = lax.ppermute(mid, "grp", swap)
    across = lax.ppermute(near, "grp", swap)
    resumed = call(
        resume_kernel,
        (shape(PLANES, 32, 128), shape(NODES, 8, 512), shape(PLANES, 32, 128)),
        [SM, SM] + [VM] * 6,
        [pltpu.VMEM((PLANES, 1, 512), f32), pltpu.VMEM((NODES, 8, 512), f32)],
    )(core_arg, layer_arg, mid, partner, near, aux, statics[5], statics[3])
    last = call(
        second_kernel,
        shape(8, 8, 128),
        [SM, SM] + [VM] * 20,
        [
            pltpu.VMEM((2, PLANES, 32, 128), f32),
            pltpu.VMEM((PLANES, 32, 128), f32),
            pltpu.VMEM((PLANES, 1, 512), f32),
            pltpu.VMEM((NODES, 8, 512), f32),
            pltpu.VMEM((PLANES, 1, 512), f32),
            pltpu.VMEM((2, NODES, 8, 512), f32),
        ],
    )(core_arg, layer_arg, across, stiff, aux, *resumed, *statics[2:], *early)

    other = lax.ppermute(last, "grp", swap)
    whole = jnp.concatenate([jnp.where(core == 0, last, other), jnp.where(core == 0, other, last)], axis=0)
    back = lax.all_to_all(whole, ("gx", "gy"), 0, 0, tiled=True)
    return call(
        unpack_kernel,
        (shape(4, 8, 128), shape(3, 512)),
        [SM, VM],
        [pltpu.VMEM((8, 512), f32)],
    )(core_arg, back)


def solution(mesh):
    fine = Mesh(np.asarray(mesh.devices).reshape(2, 8, 4, 4), ("grp", "gz", "gx", "gy"))
    cell = P(("gz", "gx"), "gy", "grp")
    node = P(None, ("grp", "gz", "gx", "gy"))
    elem = P(("grp", "gz", "gx", "gy"), None)
    return jax.shard_map(
        shards,
        mesh=fine,
        in_specs=(
            cell, cell, cell, cell, P(), P(("gz", "gx"), None, None), node, node, node, elem, elem,
            P(), P(), P(),
        ),
        out_specs=(cell, node),
        check_vma=False,
    )
```

```python
import jax
import jax.numpy as jnp
import numpy as np
from jax import lax
from jax.experimental import pallas as pl
from jax.experimental.pallas import tpu as pltpu
from jax.sharding import Mesh
from jax.sharding import PartitionSpec as P

SWEEPS = 6
CLASSES = 16
CHIPS = 16
PLANES = 16
NODES = 16
TILES = 13
EARLY = 5
FAR = (2, 3, 6, 7, 8)

stabilize = 0.5
biot_coef = 0.8
damping = 0.7
tiny = 1e-30

f32 = jnp.float32
bf16 = jnp.bfloat16

VM = pl.BlockSpec(memory_space=pltpu.VMEM)
SM = pl.BlockSpec(memory_space=pltpu.SMEM)
HB = pl.BlockSpec(memory_space=pltpu.HBM)
WHOLE = 64 * 1024 * 1024 - 65536


def call(body, out_shapes, in_specs, scratch=(), budget=40 * 1024 * 1024, out_spec=VM):
    return pl.pallas_call(
        body,
        out_shape=out_shapes,
        in_specs=in_specs,
        out_specs=jax.tree.map(lambda _: out_spec, out_shapes),
        scratch_shapes=list(scratch),
        compiler_params=pltpu.CompilerParams(vmem_limit_bytes=budget),
    )


def lanes(shape):
    return lax.broadcasted_iota(jnp.int32, shape, 1)


def rows(shape):
    return lax.broadcasted_iota(jnp.int32, shape, 0)


def roll(x, shift, axis=1):
    shift = shift % x.shape[axis]
    return x if shift == 0 else pltpu.roll(x, shift, axis)


def three_parts(x):
    high = x.astype(bf16)
    rest = x - high.astype(f32)
    middle = rest.astype(bf16)
    return high, middle, (rest - middle.astype(f32)).astype(bf16)


def nt_dot(a, b):
    return lax.dot_general(a, b, (((1,), (1,)), ((), ())), preferred_element_type=f32)


def pack_kernel(
    core, across, layer, perms, p0, src, sto, cls, disp, load, sup, lam, mu, blocks,
    packed, cells, nodes, routes, held, small, pair, classes, out, sems, done,
):
    copies = [
        pltpu.make_async_copy(perms, classes, sems.at[0]),
        pltpu.make_async_copy(cls, held, sems.at[1]),
        pltpu.make_async_copy(p0, cells.at[0:4], sems.at[2]),
        pltpu.make_async_copy(src, cells.at[4:8], sems.at[3]),
        pltpu.make_async_copy(sto, cells.at[8:12], sems.at[4]),
        pltpu.make_async_copy(disp, small.at[0], sems.at[5]),
        pltpu.make_async_copy(load, small.at[1], sems.at[6]),
        pltpu.make_async_copy(sup, small.at[2], sems.at[7]),
        pltpu.make_async_copy(lam, pair.at[0], sems.at[8]),
        pltpu.make_async_copy(mu, pair.at[1], sems.at[9]),
        pltpu.make_async_copy(blocks, routes, sems.at[10]),
    ]
    for copy in copies:
        copy.start()
    nodes[...] = jnp.zeros((24, 512), f32)
    for copy in copies:
        copy.wait()
    for i in range(4):
        which = held[i]
        perm = jnp.zeros((8, 128), f32)
        for member in range(CLASSES):
            perm = jnp.where(which == member, classes[member], perm)
        cells[12 + i] = perm
    nodes[0:3] = small[0]
    nodes[8:11] = small[1]
    nodes[16:19] = small[2]
    sent = []

    def send(at):
        sent.append(pltpu.make_async_copy(out.at[:, at], packed.at[:, at], done.at[at]))
        sent[-1].start()

    first = core[0] == 0
    lane = lanes((8, 128))
    low = lane < 64
    sub = rows((8, 128))

    device = lanes((1, 512)) // 64
    mine = jnp.zeros((8, 128), jnp.int32)
    for k in range(8):
        at = k // 2 * 128
        here = (core[0] == k // 4) & (across[0] == k % 4)
        mine = jnp.where(here, roll(routes[0, :, at : at + 128], 64 * (k % 2)), mine)
    block = jnp.concatenate(
        [jnp.where(low[0:1], mine[2 * m : 2 * m + 1], roll(mine[2 * m + 1 : 2 * m + 2], 64)) for m in range(4)],
        axis=1,
    )
    row = block // 64 % 4 * 8 + block // 256 * 4 + device % 4
    depth = device // 4 * 64 + block % 64
    at_row = rows((32, 512)) == row
    at_depth = jnp.where(rows((128, 512)) == depth, 1.0, 0.0).astype(bf16)
    spread = [
        jnp.where(at_row, part.astype(f32), 0.0) for v in range(2) for part in three_parts(pair[v])
    ]
    placed = nt_dot(jnp.concatenate(spread, axis=0).astype(bf16), at_depth)
    grids = [placed[96 * v : 96 * v + 32] + placed[96 * v + 32 : 96 * v + 64] + placed[96 * v + 64 : 96 * v + 96] for v in range(2)]

    for pair in range(2):
        for i in range(4):
            tiles = []
            for field in (2 * pair, 2 * pair + 1):
                own = cells[4 * field + i]
                tiles.append((jnp.where(first, own, 0.0), jnp.where(first, 0.0, own)))
            for chip in range(CHIPS):
                start = 16 * chip - 24
                spot = lane % 64 + start
                in_low = (spot >= 0) & (spot < 128)
                in_high = (spot >= 128) & (spot < 256)
                found = []
                for member in range(2):
                    shift = 64 * member - start
                    win = jnp.zeros((8, 128), f32)
                    if start < 128:
                        win = jnp.where(in_low, roll(tiles[member][0], shift), win)
                    if start + 64 > 128:
                        win = jnp.where(in_high, roll(tiles[member][1], shift), win)
                    found.append(win)
                out[chip, 4 * pair + i] = jnp.where(low, found[0], found[1])
            send(4 * pair + i)

    def full_depth(i, r):
        full = []
        for j in range(4):
            at = (i * 4 + j) // 2 * 128
            own = nodes[8 * r : 8 * r + 8, at : at + 128]
            near = jnp.where(first, own, 0.0)
            deep = jnp.where(first, 0.0, own)
            if j % 2 == 0:
                full.append(jnp.where(low, near, roll(deep, 64)))
            else:
                full.append(jnp.where(low, roll(near, 64), deep))
        return full

    members = [
        [jnp.where(sub < 4, a, pltpu.roll(b, 4, 0)) for a, b in zip(full_depth(0, r), full_depth(1, r))]
        for r in range(3)
    ]
    members += [[grid[8 * j : 8 * j + 8] for j in range(4)] for grid in grids]
    for at, full in enumerate(members):
        for chip in range(CHIPS):
            start = 8 * chip - 12
            spot = lane % 32 + start
            tile = jnp.zeros((8, 128), f32)
            for j in range(4):
                tile = jnp.where(lane // 32 == j, roll(full[j], 32 * j - start), tile)
            out[chip, 8 + at] = jnp.where((spot >= 0) & (spot < 128), tile, 0.0)
        send(8 + at)
    for copy in sent:
        copy.wait()


def low_mask(shape):
    return lanes(shape) < 64


def window(core, places, then):
    for c in range(2):
        @pl.when(core[0] == c)
        def _():
            then(places[c])


def face(p, q):
    return 2.0 * p * q / jnp.maximum(p + q, tiny)


def cell_coefs(least, most, start, source, storage, perm, coef, fixed, inverse):
    keep_top = rows((32, 128)) < 31
    outer = face(perm(least - 1), perm(least)) if least else jnp.zeros((32, 128), f32)
    for x in range(least, most):
        p = perm(x)
        inner = face(p, perm(x + 1) if x < PLANES - 1 else roll(p, 64))
        up = jnp.where(keep_top, face(p, roll(p, 31, 0)), 0.0)
        deep = face(p, roll(p, 127))
        coef[0, x - least] = inner
        coef[1, x - least] = up
        coef[2, x - least] = deep
        total = inner + outer + up + roll(up, 1, 0) + deep + roll(deep, 1)
        outer = inner
        store = storage(x)
        inverse[x - least] = jnp.where(store > 0.0, 1.0 / (store + stabilize + total), 0.0)
        fixed[x - least] = source(x) + store * start(x)


def both(early, late):
    return lambda x: early[x] if x < EARLY else late[x - EARLY]


def both_faces(early, late):
    return lambda way, x: early[way, x] if x < EARLY else late[way, x - EARLY]


def one_sweep(src, dst, coef, rhs, inverse, least, most=PLANES):
    outer = coef(0, least - 1) * src(least - 1)
    p = src(least)
    for x in range(least, most):
        q = src(x + 1) if x < PLANES - 1 else roll(p, 64)
        inner, up, deep = coef(0, x), coef(1, x), coef(2, x)
        total = rhs[x] + inner * q + outer
        total = total + up * roll(p, 31, 0) + roll(up * p, 1, 0)
        total = total + deep * roll(p, 127) + roll(deep * p, 1)
        dst[x] = total * inverse(x)
        outer = inner * p
        p = q


def sweeps(press, coef, rhs, inverse, first):
    for n in range(SWEEPS):
        one_sweep(lambda x, n=n: press[n % 2, x], press.at[1 - n % 2], coef, rhs, inverse, first + n)


def pair_matrix():
    cell = rows((128, 256))
    n = lanes((128, 256))
    hit = (cell // 2 % 32 == n % 32) & (cell // 64 == n // 128)
    return jnp.where(hit, 0.125, 0.0).astype(bf16)


def row_mask(shape):
    return lanes(shape) % 128 // 32 == rows(shape) % 8 // 2


def block_means(press, means, least, most):
    sums = jnp.concatenate([press[2 * q] + press[2 * q + 1] for q in range(3, 8)], axis=0)
    matrix = pair_matrix()
    got = jnp.zeros((160, 256), f32)
    for part in three_parts(sums):
        got = got + jnp.dot(part, matrix, preferred_element_type=f32)
    got = jnp.where(row_mask((160, 256)), got, 0.0)
    for b in range(least, most + 1):
        q, side = (b, 0) if b < 8 else (15 - b, 128)
        piece = got[32 * q - 96 : 32 * q - 64, side : side + 128]
        for y in range(4):
            means[b, 0:1, 128 * y : 128 * y + 128] = jnp.sum(piece[8 * y : 8 * y + 8], axis=0, keepdims=True)


def last_row(shape):
    return lanes(shape) // 32 % 16 == 15


def corner_rolls(u):
    last = last_row(u.shape)
    return [
        u,
        roll(u, 511),
        jnp.where(last, 0.0, roll(u, 480)),
        jnp.where(last, 0.0, roll(u, 479)),
    ]


def assembled(here, under):
    summed = [here[8 * j : 8 * j + 8] + roll(under[8 * j : 8 * j + 8], 4, 0) for j in range(4)]
    last = last_row((8, 512))
    return (
        summed[0]
        + roll(summed[1], 1)
        + roll(jnp.where(last, 0.0, summed[2] + roll(summed[3], 1)), 32)
    )


def diag_of(lam, mu, sup, aux, safe, gain):
    depth = lanes((8, 512)) % 32
    inside = (depth >= 6) & (depth < 26)
    terms = {}
    for b in range(3, 12):
        terms[b] = aux[:, 1:2] * lam[b] + aux[:, 2:3] * mu[b]
        if b > 3:
            node_sup = sup[b]
            total = node_sup + assembled(terms[b], terms[b - 1])
            valid = inside & (node_sup > 0.0)
            safe[b] = jnp.where(valid, total, 1.0)
            gain[b] = jnp.where(valid, damping, 0.0)


def stiff_parts(stiff):
    high = stiff.astype(bf16)
    low = (stiff - high.astype(f32)).astype(bf16)
    return jnp.concatenate([high, high, low], axis=1)


def element_terms(matrix, coupling, v_here, v_next, lam, mu, press):
    vals = jnp.concatenate([a + roll(b, 4, 0) for a, b in zip(v_here, v_next)], axis=0)
    high = vals.astype(bf16)
    low = (vals - high.astype(f32)).astype(bf16)
    both = jnp.dot(matrix, jnp.concatenate([high, low, high], axis=0), preferred_element_type=f32)
    return coupling * (biot_coef * press) - (lam * both[0:32] + mu * both[32:64])


def displacements(u, lam, mu, load, sup, safe, gain, means, stiff, aux, moved, least, most):
    matrix = stiff_parts(stiff[...])
    coupling = aux[:, 0:1]

    def half(old, new, least, most):
        under = None
        v_here = corner_rolls(old[least - 1])
        for b in range(least - 1, most + 1):
            v_next = corner_rolls(old[b + 1])
            terms = element_terms(matrix, coupling, v_here, v_next, lam[b], mu[b], means[b])
            if b >= least:
                value = old[b]
                residual = load[b] - sup[b] * value + assembled(terms, under)
                new[b] = value + gain[b] * residual / safe[b]
            under = terms
            v_here = v_next

    half(u, moved.at[0], least - 1, most + 1)
    half(moved.at[0], moved.at[1], least, most)


def pack_mid(core, press, moved, out):
    low = low_mask((32, 128))
    upper = rows((8, 512)) < 4
    extra = jnp.where(low, press[10], roll(press[11], 64))
    node = jnp.where(core[0] == 0, moved[1, 10], moved[1, 5])
    pairs = [(moved[1, 6], moved[1, 7]), (moved[1, 8], moved[1, 9])]
    held = [jnp.where(upper, a, roll(b, 4, 0)) for a, b in pairs] + [node]
    for y in range(4):
        for q in range(4):
            out[y, q] = press[12 + q, 8 * y : 8 * y + 8]
        out[y, 4] = extra[8 * y : 8 * y + 8]
        for q in range(3):
            out[y, 5 + q] = held[q][:, 128 * y : 128 * y + 128]


def pack_last(press, moved, out):
    lane = lanes((32, 128))
    for x in range(2):
        cells = jnp.zeros((32, 128), f32)
        for i in range(4):
            if x == 0:
                tile = roll(press[12 + i], 16 * i - 24)
            else:
                tile = roll(press[15 - i], 16 * i - 88)
            cells = jnp.where(lane // 16 == i, tile, cells)
        for y in range(4):
            total = cells[8 * y : 8 * y + 8]
            for i in range(2):
                tile = moved[1, 6 + 2 * x + i, :, 128 * y : 128 * y + 128]
                for j in range(4):
                    total = jnp.where(lane[0:8] // 8 == 8 + 4 * i + j, roll(tile, 52 + 32 * i - 24 * j), total)
            out[4 * x + y] = total


def inside_flags(core, layer):
    below = jnp.where(layer[0] > 0, 1.0, 0.0)
    above = jnp.where(layer[0] < 7, 1.0, 0.0)
    first = core[0] == 0
    return jnp.where(first, below, above), jnp.where(first, above, below)


def units_of(grid, halo, share, ok):
    def plane(x):
        return lambda y, at: grid[4 * x + y, at]

    none = jnp.zeros((8, 128), f32)

    def near(y, at):
        if at < 11:
            return halo[11 * y + at] * ok[0]
        return halo[33 + at] * ok[0] if y == 0 else none

    def middle(y, at):
        return halo[46 + 9 * y + at] * ok[0] if at < 9 else none

    def far(y, at):
        if at not in FAR:
            return none
        at = 82 + 2 * y + at - 2 if at < 4 else 90 + 3 * y + at - 6
        return halo[at] * ok[0]

    def beside(y, at):
        return none if share is None else share[11 * y + at] * ok[1]

    inside = [plane(x) for x in range(4)]
    return [[far, middle, near] + inside + [beside], [beside] + inside + [near, middle, far]]


def unpack_cells(units, planes, press, source, storage, perm):
    low = low_mask((32, 128))

    def tile(cell, at):
        return jnp.concatenate([units[cell // 4](y, at + cell % 4) for y in range(4)], axis=0)

    for x in planes:
        a = tile(x, 0)
        b = tile(31 - x, 0)
        press(x)[...] = jnp.where(low, a, roll(b, 64))
        source(x)[...] = jnp.where(low, roll(a, 64), b)
        a = tile(x, 4)
        b = tile(31 - x, 4)
        storage(x)[...] = jnp.where(low, a, roll(b, 64))
        perm(x)[...] = jnp.where(low, roll(a, 64), b)


def prepare_kernel(
    core, layer, grid, halo, aux,
    start, edge, coef, fixed, inverse, u, lam, mu, load, sup, safe, gain,
    source, storage, perm,
):
    ok = inside_flags(core, layer)
    def unpack(units):
        unpack_cells(
            units, range(4, PLANES), lambda x: start.at[x - 4], lambda x: source.at[x],
            lambda x: storage.at[x], lambda x: perm.at[x],
        )
        sub = rows((8, 128))
        for unit in range(8):
            for y in range(4):
                at = slice(128 * y, 128 * y + 128)
                for member, target in ((8, u), (9, load), (10, sup)):
                    if member > 8 and not 2 <= unit <= 5:
                        continue
                    tile = units[unit](y, member)
                    target[2 * unit, :, at] = jnp.where(sub < 3, tile, 0.0)
                    target[2 * unit + 1, :, at] = jnp.where(sub < 3, pltpu.roll(tile, 4, 0), 0.0)
            if 1 <= unit <= 5:
                for at, param in ((11, lam), (12, mu)):
                    total = units[unit](0, at) + units[unit](1, at) + units[unit](2, at) + units[unit](3, at)
                    for i in range(2):
                        for y in range(4):
                            row = 4 * i + y
                            param[2 * unit + i, :, 128 * y : 128 * y + 128] = total[row : row + 1]

    window(core, units_of(grid, halo, None, ok), unpack)
    cell_coefs(
        EARLY, PLANES, lambda x: start[x - 4], lambda x: source[x], lambda x: storage[x],
        lambda x: perm[x], coef, fixed, inverse,
    )
    edge[0] = perm[4]
    edge[1] = perm[5]
    edge[2] = source[4]
    edge[3] = storage[4]
    diag_of(lam, mu, sup, aux, safe, gain)


def first_kernel(
    core, layer, halo, share, stiff, aux,
    start, edge, coef_late, fixed_late, inverse_late, u, lam, mu, load, sup, safe, gain,
    mid, coef_early, fixed_early, inverse_early, beside,
    press, source, storage, perm, rhs, means, moved,
):
    ok = inside_flags(core, layer)
    sub = rows((8, 128))

    def unpack(units):
        unpack_cells(
            units, range(4), lambda x: press.at[0, x], lambda x: source.at[x],
            lambda x: storage.at[x], lambda x: perm.at[x],
        )

    window(core, units_of(None, halo, share, ok), unpack)
    for y in range(4):
        tile = share[11 * y + 8] * ok[1]
        beside[0, :, 128 * y : 128 * y + 128] = jnp.where(sub < 3, tile, 0.0)
        beside[1, :, 128 * y : 128 * y + 128] = jnp.where(sub < 3, pltpu.roll(tile, 4, 0), 0.0)
    for x in range(4, PLANES):
        press[0, x] = start[x - 4]
    cell_coefs(
        0, EARLY, lambda x: press[0, x],
        lambda x: source[x] if x < 4 else edge[2], lambda x: storage[x] if x < 4 else edge[3],
        lambda x: perm[x] if x < 4 else edge[x - 4], coef_early, fixed_early, inverse_early,
    )
    fixed = both(fixed_early, fixed_late)
    for x in range(PLANES):
        rhs[x] = fixed(x) + stabilize * press[0, x]
    sweeps(press, both_faces(coef_early, coef_late), rhs, both(inverse_early, inverse_late), 1)
    block_means(press.at[0], means, 3, 11)
    displacements(u, lam, mu, load, sup, safe, gain, means, stiff, aux, moved, 5, 10)
    pack_mid(core, press.at[0], moved, mid)


def node_of(ref, k, y):
    value = ref[y, 5 + k // 2]
    return jnp.where(rows((8, 128)) < 4, roll(value, 4, 0) if k % 2 else value, 0.0)


def strain_rows(aux, nodes, blocks, strain):
    last_y = last_row((8, 512))
    column = [jnp.broadcast_to(aux[8 * j : 8 * j + 8, 0:1], (8, 512)) for j in range(4)]
    for b in blocks:
        pair = nodes(b) + roll(nodes(b + 1), 4, 0)
        parts = [column[j] * pair for j in range(4)]
        total = (
            parts[0]
            + roll(parts[1], 511)
            + jnp.where(last_y, 0.0, roll(parts[2] + roll(parts[3], 511), 480))
        )
        strain[b] = jnp.sum(total, axis=0, keepdims=True)


def right_sides(strain, groups, press, fixed, rhs):
    mask = row_mask((8, 128))
    spread = []
    for q in groups:
        for y in range(4):
            at = slice(128 * y, 128 * y + 128)
            pair = [jnp.where(mask, strain[q, :, at], 0.0), jnp.where(mask, strain[15 - q, :, at], 0.0)]
            spread.append(jnp.concatenate(pair, axis=1))
    matrix = pair_matrix()
    got = jnp.zeros((32 * len(groups), 128), f32)
    for part in three_parts(jnp.concatenate(spread, axis=0)):
        got = got + nt_dot(part, matrix)
    for n, q in enumerate(groups):
        change = got[32 * n : 32 * n + 32]
        for x in (2 * q, 2 * q + 1):
            rhs[x] = fixed(x) + stabilize * press[x] - (8.0 * biot_coef) * change


def resume_kernel(
    core, layer, own, partner, near, aux, start, coef_late, fixed_late, inverse_late,
    press, u, rhs, edges, inner, strain, moved, swept,
):
    ok = inside_flags(core, layer)
    low = low_mask((32, 128))

    def unpack(runs, extra_cells, extra_node):
        def piece(cell, want_low):
            if cell in extra_cells:
                ref, q, is_low = near, 4, cell == 2
            elif 4 <= cell < 28:
                k = (cell - 4) % 8
                ref, q, is_low = runs[(cell - 4) // 8][0], min(k, 7 - k), k < 4
            else:
                return jnp.zeros((32, 128), f32)
            value = ref[:, q].reshape(32, 128)
            return value if is_low == want_low else roll(value, 64)

        for x in range(2, PLANES):
            press[x] = jnp.where(low, piece(x, True), piece(31 - x, False))
        for n in range(1, 15):
            if n == extra_node:
                ref, k, flag = near, 4, 0
            elif 2 <= n < 14:
                (ref, flag), k = runs[(n - 2) // 4], (n - 2) % 4
            else:
                u[n] = jnp.zeros((8, 512), f32)
                continue
            for y in range(4):
                value = node_of(ref, k, y)
                u[n, :, 128 * y : 128 * y + 128] = value if flag is None else value * ok[flag]

    @pl.when(core[0] == 0)
    def _():
        unpack([(near, 0), (own, None), (partner, None)], (2, 3), 1)

    @pl.when(core[0] == 1)
    def _():
        unpack([(partner, None), (own, None), (near, 0)], (), 14)

    for n in range(3, 14):
        moved[n] = u[n] - start[n]
    strain_rows(aux, lambda n: moved[n], range(3, 13), strain)
    right_sides(strain, range(3, 8), press, lambda x: fixed_late[x - EARLY], rhs)
    for k in range(SWEEPS + 1):
        if k:
            one_sweep(
                lambda x, k=k: press[x] if k == 1 else swept[k % 2, x], swept.at[1 - k % 2],
                lambda way, x: coef_late[way, x - EARLY], rhs, lambda x: inverse_late[x - EARLY], 5 + k,
            )
        level = press if k == 0 else swept.at[1 - k % 2]
        if k < SWEEPS:
            edges[k, 0] = level[5 + k]
            edges[k, 1] = level[6 + k]
    for x in range(11, PLANES):
        inner[x - 11] = swept[1, x]


def second_kernel(
    core, layer, across, stiff, aux, held, u, rhs_late, edges, inner,
    coef_late, fixed_late, inverse_late, start, lam, mu, load, sup, safe, gain,
    coef_early, fixed_early, inverse_early, beside,
    last, press, rhs, means, nodes, strain, moved,
):
    ok = inside_flags(core, layer)
    low = low_mask((32, 128))
    first = core[0] == 0
    for x in range(2, 6):
        press[0, x] = held[x]
    for x in range(6, 11):
        rhs[x] = rhs_late[x]
    for n in range(2, 14):
        nodes[n] = u[n]

    for x, q in ((2, 1), (3, 0)):
        turned = roll(across[:, q].reshape(32, 128), 64)
        press[0, x] = jnp.where(low & jnp.logical_not(first), turned, held[x])
    for y in range(4):
        at = slice(128 * y, 128 * y + 128)
        nodes[1, :, at] = jnp.where(first, u[1, :, at], node_of(across, 3, y) * ok[1])
        nodes[14, :, at] = jnp.where(first, node_of(across, 0, y) * ok[1], u[14, :, at])
    for n in (2, 3, 13):
        moved[0, n] = nodes[n] - start[n]
    moved[0, 1] = nodes[1] - jnp.where(first, start[1], beside[1])
    moved[0, 14] = nodes[14] - jnp.where(first, beside[0], start[14])
    strain[14] = jnp.zeros((1, 512), f32)
    strain_rows(aux, lambda n: moved[0, n], (1, 2, 13), strain)
    right_sides(strain, (1, 2), press.at[0], both(fixed_early, fixed_late), rhs)
    for k in range(1, SWEEPS + 1):
        one_sweep(
            lambda x, k=k: press[1 - k % 2, x] if x < 4 + k else edges[k - 1, x - 4 - k], press.at[k % 2],
            both_faces(coef_early, coef_late), rhs, both(inverse_early, inverse_late), 2 + k, 5 + k,
        )
    for x in range(11, PLANES):
        press[0, x] = inner[x - 11]
    block_means(press.at[0], means, 4, 10)
    displacements(nodes, lam, mu, load, sup, safe, gain, means, stiff, aux, moved, 6, 9)
    pack_last(press.at[0], moved, last)


def unpack_kernel(core, got, pressure, disp, held):
    lane = lanes((8, 128))
    base = core[0] * 8
    tiles = [got[base + s] for s in range(8)]
    for i in range(4):
        total = jnp.zeros((8, 128), f32)
        for s in range(8):
            total = jnp.where(lane // 16 == s, roll(tiles[s], 16 * s - 16 * i), total)
        pressure[i] = total
    for i in range(2):
        for pair in range(2):
            total = jnp.zeros((8, 128), f32)
            for s in range(8):
                for side in range(2):
                    shift = 64 * side + 8 * s - 64 - 32 * i - 8 * (2 * pair + side)
                    total = jnp.where(lane // 8 == 8 * side + s, roll(tiles[s], shift), total)
            held[:, 128 * (2 * i + pair) : 128 * (2 * i + pair) + 128] = total
    disp[...] = held[0:3]


def corner_major(stiff):
    grid = stiff.reshape(3, 2, 4, 3, 2, 4).transpose(2, 1, 0, 5, 4, 3)
    return jnp.pad(grid, ((0, 0), (0, 0), (0, 1), (0, 0), (0, 0), (0, 1))).reshape(32, 32)


def corner_column(vec):
    return jnp.pad(vec.reshape(3, 2, 4).transpose(2, 1, 0), ((0, 0), (0, 0), (0, 1))).reshape(32)


def shape(*dims):
    return jax.ShapeDtypeStruct(dims, f32)


def shards(
    pressure_start, source, storage, perm_class, class_perm, block_route, displacement_start,
    load, support, lame_lambda, lame_mu, stiff_lambda, stiff_mu, coupling_vec,
):
    core = lax.axis_index("grp")
    core_arg = jnp.full((1,), core, jnp.int32)
    row_arg = jnp.full((1,), lax.axis_index("gy"), jnp.int32)
    layer = lax.axis_index("gz")
    layer_arg = jnp.full((1,), layer, jnp.int32)
    swap = [(0, 1), (1, 0)]

    packed = call(
        pack_kernel,
        shape(16, TILES, 8, 128),
        [SM, SM, SM] + [HB] * 11,
        [
            pltpu.VMEM((16, 8, 128), f32),
            pltpu.VMEM((24, 512), f32),
            pltpu.VMEM((1, 8, 512), jnp.int32),
            pltpu.VMEM((4, 8, 128), jnp.int32),
            pltpu.VMEM((3, 3, 512), f32),
            pltpu.VMEM((2, 1, 512), f32),
            pltpu.SMEM((CLASSES,), f32),
            pltpu.VMEM((16, TILES, 8, 128), f32),
            pltpu.SemaphoreType.DMA((11,)),
            pltpu.SemaphoreType.DMA((TILES,)),
        ],
        WHOLE,
        HB,
    )(core_arg, row_arg, layer_arg, class_perm, pressure_start, source, storage, perm_class,
      displacement_start, load, support, lame_lambda, lame_mu, block_route)
    grid = lax.all_to_all(packed, ("gx", "gy"), 0, 0, tiled=True)
    grid, core, layer, stiff_lambda, stiff_mu, coupling_vec = lax.optimization_barrier(
        (grid, core, layer, stiff_lambda, stiff_mu, coupling_vec)
    )
    core_arg = jnp.full((1,), core, jnp.int32)
    layer_arg = jnp.full((1,), layer, jnp.int32)

    ring = [(8 + z, (z + 1) % 8) for z in range(8)] + [(z, 8 + (z - 1) % 8) for z in range(8)]
    grid = grid + lax.ppermute(grid, "grp", swap)
    first = core == 0
    sent = [
        jnp.where(first, grid[0:4, :11], grid[12:16, :11]),
        jnp.sum(jnp.where(first, grid[0:4, 11:], grid[12:16, 11:]), axis=0),
        jnp.where(first, grid[4:8, :9], grid[8:12, :9]),
        jnp.where(first, grid[8:12, 2:4], grid[4:8, 2:4]),
        jnp.where(first, grid[8:12, 6:9], grid[4:8, 6:9]),
    ]
    sent = jnp.concatenate([part.reshape(-1, 8, 128) for part in sent], axis=0)
    halo = lax.ppermute(sent, ("grp", "gz"), ring)
    share = lax.ppermute(halo[:44], "grp", swap)

    stiff = jnp.concatenate([corner_major(stiff_lambda), corner_major(stiff_mu)], axis=0)
    columns = [corner_column(coupling_vec), corner_column(jnp.diag(stiff_lambda)), corner_column(jnp.diag(stiff_mu))]
    aux = jnp.pad(jnp.stack(columns, axis=1), ((0, 0), (0, 125)))

    late = PLANES - EARLY
    statics = call(
        prepare_kernel,
        (
            shape(PLANES - 4, 32, 128), shape(4, 32, 128),
            shape(3, late, 32, 128), shape(late, 32, 128), shape(late, 32, 128),
            shape(NODES, 8, 512), shape(12, 1, 512), shape(12, 1, 512), shape(12, 8, 512),
            shape(12, 8, 512), shape(12, 8, 512), shape(12, 8, 512),
        ),
        [SM, SM] + [VM] * 3,
        [pltpu.VMEM((PLANES, 32, 128), f32)] * 3,
    )(core_arg, layer_arg, grid, halo, aux)
    mid, *early = call(
        first_kernel,
        (
            shape(4, 8, 8, 128), shape(3, EARLY, 32, 128), shape(EARLY, 32, 128),
            shape(EARLY, 32, 128), shape(2, 8, 512),
        ),
        [SM, SM] + [VM] * 16,
        [
            pltpu.VMEM((2, PLANES, 32, 128), f32),
            pltpu.VMEM((4, 32, 128), f32),
            pltpu.VMEM((4, 32, 128), f32),
            pltpu.VMEM((4, 32, 128), f32),
            pltpu.VMEM((PLANES, 32, 128), f32),
            pltpu.VMEM((PLANES, 1, 512), f32),
            pltpu.VMEM((2, NODES, 8, 512), f32),
        ],
    )(core_arg, layer_arg, halo, share, stiff, aux, *statics)

    near = lax.ppermute(mid, ("grp", "gz"), ring)
    partner = lax.ppermute(mid, "grp", swap)
    across = lax.ppermute(near, "grp", swap)
    resumed = call(
        resume_kernel,
        (
            shape(PLANES, 32, 128), shape(NODES, 8, 512), shape(PLANES, 32, 128),
            shape(SWEEPS, 2, 32, 128), shape(PLANES - 11, 32, 128),
        ),
        [SM, SM] + [VM] * 8,
        [
            pltpu.VMEM((PLANES, 1, 512), f32),
            pltpu.VMEM((NODES, 8, 512), f32),
            pltpu.VMEM((2, PLANES, 32, 128), f32),
        ],
    )(core_arg, layer_arg, mid, partner, near, aux, statics[5], *statics[2:5])
    last = call(
        second_kernel,
        shape(8, 8, 128),
        [SM, SM] + [VM] * 22,
        [
            pltpu.VMEM((2, PLANES, 32, 128), f32),
            pltpu.VMEM((PLANES, 32, 128), f32),
            pltpu.VMEM((PLANES, 1, 512), f32),
            pltpu.VMEM((NODES, 8, 512), f32),
            pltpu.VMEM((PLANES, 1, 512), f32),
            pltpu.VMEM((2, NODES, 8, 512), f32),
        ],
    )(core_arg, layer_arg, across, stiff, aux, *resumed, *statics[2:], *early)

    other = lax.ppermute(last, "grp", swap)
    whole = jnp.concatenate([jnp.where(core == 0, last, other), jnp.where(core == 0, other, last)], axis=0)
    back = lax.all_to_all(whole, ("gx", "gy"), 0, 0, tiled=True)
    return call(
        unpack_kernel,
        (shape(4, 8, 128), shape(3, 512)),
        [SM, VM],
        [pltpu.VMEM((8, 512), f32)],
    )(core_arg, back)


def solution(mesh):
    fine = Mesh(np.asarray(mesh.devices).reshape(2, 8, 4, 4), ("grp", "gz", "gx", "gy"))
    cell = P(("gz", "gx"), "gy", "grp")
    node = P(None, ("grp", "gz", "gx", "gy"))
    elem = P(("grp", "gz", "gx", "gy"), None)
    return jax.shard_map(
        shards,
        mesh=fine,
        in_specs=(
            cell, cell, cell, cell, P(), P(("gz", "gx"), None, None), node, node, node, elem, elem,
            P(), P(), P(),
        ),
        out_specs=(cell, node),
        check_vma=False,
    )
```

```python
import jax
import jax.numpy as jnp
import numpy as np
from jax import lax
from jax.experimental import pallas as pl
from jax.experimental.pallas import tpu as pltpu
from jax.sharding import Mesh
from jax.sharding import PartitionSpec as P

SWEEPS = 6
CLASSES = 16
CHIPS = 16
PLANES = 16
NODES = 16
TILES = 13
EARLY = 5
FAR = (2, 3, 6, 7, 8)

stabilize = 0.5
biot_coef = 0.8
damping = 0.7
tiny = 1e-30

f32 = jnp.float32
bf16 = jnp.bfloat16

VM = pl.BlockSpec(memory_space=pltpu.VMEM)
SM = pl.BlockSpec(memory_space=pltpu.SMEM)
HB = pl.BlockSpec(memory_space=pltpu.HBM)
WHOLE = 64 * 1024 * 1024 - 65536


def call(body, out_shapes, in_specs, scratch=(), budget=40 * 1024 * 1024, out_spec=VM):
    return pl.pallas_call(
        body,
        out_shape=out_shapes,
        in_specs=in_specs,
        out_specs=jax.tree.map(lambda _: out_spec, out_shapes),
        scratch_shapes=list(scratch),
        compiler_params=pltpu.CompilerParams(vmem_limit_bytes=budget),
    )


def lanes(shape):
    return lax.broadcasted_iota(jnp.int32, shape, 1)


def rows(shape):
    return lax.broadcasted_iota(jnp.int32, shape, 0)


def roll(x, shift, axis=1):
    shift = shift % x.shape[axis]
    return x if shift == 0 else pltpu.roll(x, shift, axis)


def three_parts(x):
    high = x.astype(bf16)
    rest = x - high.astype(f32)
    middle = rest.astype(bf16)
    return high, middle, (rest - middle.astype(f32)).astype(bf16)


def nt_dot(a, b):
    return lax.dot_general(a, b, (((1,), (1,)), ((), ())), preferred_element_type=f32)


def pack_kernel(
    core, across, layer, perms, p0, src, sto, cls, disp, load, sup, lam, mu, blocks,
    packed, cells, nodes, routes, held, small, pair, classes, out, sems, done,
):
    copies = [
        pltpu.make_async_copy(perms, classes, sems.at[0]),
        pltpu.make_async_copy(cls, held, sems.at[1]),
        pltpu.make_async_copy(p0, cells.at[0:4], sems.at[2]),
        pltpu.make_async_copy(src, cells.at[4:8], sems.at[3]),
        pltpu.make_async_copy(sto, cells.at[8:12], sems.at[4]),
        pltpu.make_async_copy(disp, small.at[0], sems.at[5]),
        pltpu.make_async_copy(load, small.at[1], sems.at[6]),
        pltpu.make_async_copy(sup, small.at[2], sems.at[7]),
        pltpu.make_async_copy(lam, pair.at[0], sems.at[8]),
        pltpu.make_async_copy(mu, pair.at[1], sems.at[9]),
        pltpu.make_async_copy(blocks, routes, sems.at[10]),
    ]
    for copy in copies:
        copy.start()
    nodes[...] = jnp.zeros((24, 512), f32)
    for copy in copies:
        copy.wait()
    for i in range(4):
        which = held[i]
        perm = jnp.zeros((8, 128), f32)
        for member in range(CLASSES):
            perm = jnp.where(which == member, classes[member], perm)
        cells[12 + i] = perm
    nodes[0:3] = small[0]
    nodes[8:11] = small[1]
    nodes[16:19] = small[2]
    sent = []

    def send(at):
        sent.append(pltpu.make_async_copy(out.at[:, at], packed.at[:, at], done.at[at]))
        sent[-1].start()

    first = core[0] == 0
    lane = lanes((8, 128))
    low = lane < 64
    sub = rows((8, 128))

    device = lanes((1, 512)) // 64
    mine = jnp.zeros((8, 128), jnp.int32)
    for k in range(8):
        at = k // 2 * 128
        here = (core[0] == k // 4) & (across[0] == k % 4)
        mine = jnp.where(here, roll(routes[0, :, at : at + 128], 64 * (k % 2)), mine)
    block = jnp.concatenate(
        [jnp.where(low[0:1], mine[2 * m : 2 * m + 1], roll(mine[2 * m + 1 : 2 * m + 2], 64)) for m in range(4)],
        axis=1,
    )
    row = block // 64 % 4 * 8 + block // 256 * 4 + device % 4
    depth = device // 4 * 64 + block % 64
    at_row = rows((32, 512)) == row
    at_depth = jnp.where(rows((128, 512)) == depth, 1.0, 0.0).astype(bf16)
    spread = [
        jnp.where(at_row, part.astype(f32), 0.0) for v in range(2) for part in three_parts(pair[v])
    ]
    placed = nt_dot(jnp.concatenate(spread, axis=0).astype(bf16), at_depth)
    grids = [placed[96 * v : 96 * v + 32] + placed[96 * v + 32 : 96 * v + 64] + placed[96 * v + 64 : 96 * v + 96] for v in range(2)]

    for pair in range(2):
        for i in range(4):
            tiles = []
            for field in (2 * pair, 2 * pair + 1):
                own = cells[4 * field + i]
                tiles.append((jnp.where(first, own, 0.0), jnp.where(first, 0.0, own)))
            for chip in range(CHIPS):
                start = 16 * chip - 24
                spot = lane % 64 + start
                in_low = (spot >= 0) & (spot < 128)
                in_high = (spot >= 128) & (spot < 256)
                found = []
                for member in range(2):
                    shift = 64 * member - start
                    win = jnp.zeros((8, 128), f32)
                    if start < 128:
                        win = jnp.where(in_low, roll(tiles[member][0], shift), win)
                    if start + 64 > 128:
                        win = jnp.where(in_high, roll(tiles[member][1], shift), win)
                    found.append(win)
                out[chip, 4 * pair + i] = jnp.where(low, found[0], found[1])
            send(4 * pair + i)

    def full_depth(i, r):
        full = []
        for j in range(4):
            at = (i * 4 + j) // 2 * 128
            own = nodes[8 * r : 8 * r + 8, at : at + 128]
            near = jnp.where(first, own, 0.0)
            deep = jnp.where(first, 0.0, own)
            if j % 2 == 0:
                full.append(jnp.where(low, near, roll(deep, 64)))
            else:
                full.append(jnp.where(low, roll(near, 64), deep))
        return full

    members = [
        [jnp.where(sub < 4, a, pltpu.roll(b, 4, 0)) for a, b in zip(full_depth(0, r), full_depth(1, r))]
        for r in range(3)
    ]
    members += [[grid[8 * j : 8 * j + 8] for j in range(4)] for grid in grids]
    for at, full in enumerate(members):
        for chip in range(CHIPS):
            start = 8 * chip - 12
            spot = lane % 32 + start
            tile = jnp.zeros((8, 128), f32)
            for j in range(4):
                tile = jnp.where(lane // 32 == j, roll(full[j], 32 * j - start), tile)
            out[chip, 8 + at] = jnp.where((spot >= 0) & (spot < 128), tile, 0.0)
        send(8 + at)
    for copy in sent:
        copy.wait()


def low_mask(shape):
    return lanes(shape) < 64


def window(core, places, then):
    for c in range(2):
        @pl.when(core[0] == c)
        def _():
            then(places[c])


def face(p, q):
    return 2.0 * p * q / jnp.maximum(p + q, tiny)


def cell_coefs(least, most, start, source, storage, perm, coef, fixed, inverse):
    keep_top = rows((32, 128)) < 31
    outer = face(perm(least - 1), perm(least)) if least else jnp.zeros((32, 128), f32)
    for x in range(least, most):
        p = perm(x)
        inner = face(p, perm(x + 1) if x < PLANES - 1 else roll(p, 64))
        up = jnp.where(keep_top, face(p, roll(p, 31, 0)), 0.0)
        deep = face(p, roll(p, 127))
        coef[0, x - least] = inner
        coef[1, x - least] = up
        coef[2, x - least] = deep
        total = inner + outer + up + roll(up, 1, 0) + deep + roll(deep, 1)
        outer = inner
        store = storage(x)
        inverse[x - least] = jnp.where(store > 0.0, 1.0 / (store + stabilize + total), 0.0)
        fixed[x - least] = source(x) + store * start(x)


def both(early, late):
    return lambda x: early[x] if x < EARLY else late[x - EARLY]


def both_faces(early, late):
    return lambda way, x: early[way, x] if x < EARLY else late[way, x - EARLY]


def one_sweep(src, dst, coef, rhs, inverse, least, most=PLANES):
    outer = coef(0, least - 1) * src(least - 1)
    p = src(least)
    for x in range(least, most):
        q = src(x + 1) if x < PLANES - 1 else roll(p, 64)
        inner, up, deep = coef(0, x), coef(1, x), coef(2, x)
        total = rhs[x] + inner * q + outer
        total = total + up * roll(p, 31, 0) + roll(up * p, 1, 0)
        total = total + deep * roll(p, 127) + roll(deep * p, 1)
        dst[x] = total * inverse(x)
        outer = inner * p
        p = q


def sweeps(press, coef, rhs, inverse, first):
    for n in range(SWEEPS):
        one_sweep(lambda x, n=n: press[n % 2, x], press.at[1 - n % 2], coef, rhs, inverse, first + n)


def pair_matrix():
    cell = rows((128, 256))
    n = lanes((128, 256))
    hit = (cell // 2 % 32 == n % 32) & (cell // 64 == n // 128)
    return jnp.where(hit, 0.125, 0.0).astype(bf16)


def row_mask(shape):
    return lanes(shape) % 128 // 32 == rows(shape) % 8 // 2


def block_means(press, means, least, most):
    sums = jnp.concatenate([press[2 * q] + press[2 * q + 1] for q in range(3, 8)], axis=0)
    matrix = pair_matrix()
    got = jnp.zeros((160, 256), f32)
    for part in three_parts(sums):
        got = got + jnp.dot(part, matrix, preferred_element_type=f32)
    got = jnp.where(row_mask((160, 256)), got, 0.0)
    for b in range(least, most + 1):
        q, side = (b, 0) if b < 8 else (15 - b, 128)
        piece = got[32 * q - 96 : 32 * q - 64, side : side + 128]
        for y in range(4):
            means[b, 0:1, 128 * y : 128 * y + 128] = jnp.sum(piece[8 * y : 8 * y + 8], axis=0, keepdims=True)


def last_row(shape):
    return lanes(shape) // 32 % 16 == 15


def corner_rolls(u):
    last = last_row(u.shape)
    return [
        u,
        roll(u, 511),
        jnp.where(last, 0.0, roll(u, 480)),
        jnp.where(last, 0.0, roll(u, 479)),
    ]


def assembled(here, under):
    summed = [here[8 * j : 8 * j + 8] + roll(under[8 * j : 8 * j + 8], 4, 0) for j in range(4)]
    last = last_row((8, 512))
    return (
        summed[0]
        + roll(summed[1], 1)
        + roll(jnp.where(last, 0.0, summed[2] + roll(summed[3], 1)), 32)
    )


def diag_of(lam, mu, sup, aux, safe, gain):
    depth = lanes((8, 512)) % 32
    inside = (depth >= 6) & (depth < 26)
    terms = {}
    for b in range(3, 12):
        terms[b] = aux[:, 1:2] * lam[b] + aux[:, 2:3] * mu[b]
        if b > 3:
            node_sup = sup[b]
            total = node_sup + assembled(terms[b], terms[b - 1])
            valid = inside & (node_sup > 0.0)
            safe[b] = jnp.where(valid, total, 1.0)
            gain[b] = jnp.where(valid, damping, 0.0)


def stiff_parts(stiff):
    high = stiff.astype(bf16)
    low = (stiff - high.astype(f32)).astype(bf16)
    return jnp.concatenate([high, high, low], axis=1)


def element_terms(matrix, coupling, v_here, v_next, lam, mu, press):
    vals = jnp.concatenate([a + roll(b, 4, 0) for a, b in zip(v_here, v_next)], axis=0)
    high = vals.astype(bf16)
    low = (vals - high.astype(f32)).astype(bf16)
    both = jnp.dot(matrix, jnp.concatenate([high, low, high], axis=0), preferred_element_type=f32)
    return coupling * (biot_coef * press) - (lam * both[0:32] + mu * both[32:64])


def displacements(u, lam, mu, load, sup, safe, gain, means, stiff, aux, moved, least, most):
    matrix = stiff_parts(stiff[...])
    coupling = aux[:, 0:1]

    def half(old, new, least, most):
        under = None
        v_here = corner_rolls(old[least - 1])
        for b in range(least - 1, most + 1):
            v_next = corner_rolls(old[b + 1])
            terms = element_terms(matrix, coupling, v_here, v_next, lam[b], mu[b], means[b])
            if b >= least:
                value = old[b]
                residual = load[b] - sup[b] * value + assembled(terms, under)
                new[b] = value + gain[b] * residual / safe[b]
            under = terms
            v_here = v_next

    half(u, moved.at[0], least - 1, most + 1)
    half(moved.at[0], moved.at[1], least, most)


def pack_mid(core, press, moved, out):
    low = low_mask((32, 128))
    upper = rows((8, 512)) < 4
    extra = jnp.where(low, press[10], roll(press[11], 64))
    node = jnp.where(core[0] == 0, moved[1, 10], moved[1, 5])
    pairs = [(moved[1, 6], moved[1, 7]), (moved[1, 8], moved[1, 9])]
    held = [jnp.where(upper, a, roll(b, 4, 0)) for a, b in pairs] + [node]
    for y in range(4):
        for q in range(4):
            out[y, q] = press[12 + q, 8 * y : 8 * y + 8]
        out[y, 4] = extra[8 * y : 8 * y + 8]
        for q in range(3):
            out[y, 5 + q] = held[q][:, 128 * y : 128 * y + 128]


def pack_last(press, moved, out):
    lane = lanes((32, 128))
    for x in range(2):
        cells = jnp.zeros((32, 128), f32)
        for i in range(4):
            if x == 0:
                tile = roll(press[12 + i], 16 * i - 24)
            else:
                tile = roll(press[15 - i], 16 * i - 88)
            cells = jnp.where(lane // 16 == i, tile, cells)
        for y in range(4):
            total = cells[8 * y : 8 * y + 8]
            for i in range(2):
                tile = moved[1, 6 + 2 * x + i, :, 128 * y : 128 * y + 128]
                for j in range(4):
                    total = jnp.where(lane[0:8] // 8 == 8 + 4 * i + j, roll(tile, 52 + 32 * i - 24 * j), total)
            out[4 * x + y] = total


def inside_flags(core, layer):
    below = jnp.where(layer[0] > 0, 1.0, 0.0)
    above = jnp.where(layer[0] < 7, 1.0, 0.0)
    first = core[0] == 0
    return jnp.where(first, below, above), jnp.where(first, above, below)


def units_of(grid, halo, share, ok):
    def plane(x):
        return lambda y, at: grid[4 * x + y, at]

    none = jnp.zeros((8, 128), f32)

    def near(y, at):
        if at < 11:
            return halo[11 * y + at] * ok[0]
        return halo[33 + at] * ok[0] if y == 0 else none

    def middle(y, at):
        return halo[46 + 9 * y + at] * ok[0] if at < 9 else none

    def far(y, at):
        if at not in FAR:
            return none
        at = 82 + 2 * y + at - 2 if at < 4 else 90 + 3 * y + at - 6
        return halo[at] * ok[0]

    def beside(y, at):
        return none if share is None else share[11 * y + at] * ok[1]

    inside = [plane(x) for x in range(4)]
    return [[far, middle, near] + inside + [beside], [beside] + inside + [near, middle, far]]


def unpack_cells(units, planes, press, source, storage, perm):
    low = low_mask((32, 128))

    def tile(cell, at):
        return jnp.concatenate([units[cell // 4](y, at + cell % 4) for y in range(4)], axis=0)

    for x in planes:
        a = tile(x, 0)
        b = tile(31 - x, 0)
        press(x)[...] = jnp.where(low, a, roll(b, 64))
        source(x)[...] = jnp.where(low, roll(a, 64), b)
        a = tile(x, 4)
        b = tile(31 - x, 4)
        storage(x)[...] = jnp.where(low, a, roll(b, 64))
        perm(x)[...] = jnp.where(low, roll(a, 64), b)


def prepare_kernel(
    core, layer, grid, halo, aux,
    start, edge, coef, fixed, inverse, u, lam, mu, load, sup, safe, gain,
    source, storage, perm,
):
    ok = inside_flags(core, layer)
    def unpack(units):
        unpack_cells(
            units, range(4, PLANES), lambda x: start.at[x - 4], lambda x: source.at[x],
            lambda x: storage.at[x], lambda x: perm.at[x],
        )
        sub = rows((8, 128))
        for unit in range(8):
            for y in range(4):
                at = slice(128 * y, 128 * y + 128)
                for member, target in ((8, u), (9, load), (10, sup)):
                    if member > 8 and not 2 <= unit <= 5:
                        continue
                    tile = units[unit](y, member)
                    target[2 * unit, :, at] = jnp.where(sub < 3, tile, 0.0)
                    target[2 * unit + 1, :, at] = jnp.where(sub < 3, pltpu.roll(tile, 4, 0), 0.0)
            if 1 <= unit <= 5:
                for at, param in ((11, lam), (12, mu)):
                    total = units[unit](0, at) + units[unit](1, at) + units[unit](2, at) + units[unit](3, at)
                    for i in range(2):
                        for y in range(4):
                            row = 4 * i + y
                            param[2 * unit + i, :, 128 * y : 128 * y + 128] = total[row : row + 1]

    window(core, units_of(grid, halo, None, ok), unpack)
    cell_coefs(
        EARLY, PLANES, lambda x: start[x - 4], lambda x: source[x], lambda x: storage[x],
        lambda x: perm[x], coef, fixed, inverse,
    )
    edge[0] = perm[4]
    edge[1] = perm[5]
    edge[2] = source[4]
    edge[3] = storage[4]
    diag_of(lam, mu, sup, aux, safe, gain)


def first_kernel(
    core, layer, halo, share, stiff, aux,
    start, edge, coef_late, fixed_late, inverse_late, u, lam, mu, load, sup, safe, gain,
    mid, coef_early, fixed_early, inverse_early, beside,
    press, source, storage, perm, rhs, means, moved,
):
    ok = inside_flags(core, layer)
    sub = rows((8, 128))

    def unpack(units):
        unpack_cells(
            units, range(4), lambda x: press.at[0, x], lambda x: source.at[x],
            lambda x: storage.at[x], lambda x: perm.at[x],
        )

    window(core, units_of(None, halo, share, ok), unpack)
    for y in range(4):
        tile = share[11 * y + 8] * ok[1]
        beside[0, :, 128 * y : 128 * y + 128] = jnp.where(sub < 3, tile, 0.0)
        beside[1, :, 128 * y : 128 * y + 128] = jnp.where(sub < 3, pltpu.roll(tile, 4, 0), 0.0)
    for x in range(4, PLANES):
        press[0, x] = start[x - 4]
    cell_coefs(
        0, EARLY, lambda x: press[0, x],
        lambda x: source[x] if x < 4 else edge[2], lambda x: storage[x] if x < 4 else edge[3],
        lambda x: perm[x] if x < 4 else edge[x - 4], coef_early, fixed_early, inverse_early,
    )
    fixed = both(fixed_early, fixed_late)
    for x in range(PLANES):
        rhs[x] = fixed(x) + stabilize * press[0, x]
    sweeps(press, both_faces(coef_early, coef_late), rhs, both(inverse_early, inverse_late), 1)
    block_means(press.at[0], means, 3, 11)
    displacements(u, lam, mu, load, sup, safe, gain, means, stiff, aux, moved, 5, 10)
    pack_mid(core, press.at[0], moved, mid)


def node_of(ref, k, y, least=5):
    value = ref[y, least + k // 2]
    return jnp.where(rows((8, 128)) < 4, roll(value, 4, 0) if k % 2 else value, 0.0)


def strain_rows(aux, nodes, blocks, strain):
    last_y = last_row((8, 512))
    column = [jnp.broadcast_to(aux[8 * j : 8 * j + 8, 0:1], (8, 512)) for j in range(4)]
    for b in blocks:
        pair = nodes(b) + roll(nodes(b + 1), 4, 0)
        parts = [column[j] * pair for j in range(4)]
        total = (
            parts[0]
            + roll(parts[1], 511)
            + jnp.where(last_y, 0.0, roll(parts[2] + roll(parts[3], 511), 480))
        )
        strain[b] = jnp.sum(total, axis=0, keepdims=True)


def right_sides(strain, groups, press, fixed, rhs):
    mask = row_mask((8, 128))
    spread = []
    for q in groups:
        for y in range(4):
            at = slice(128 * y, 128 * y + 128)
            pair = [jnp.where(mask, strain[q, :, at], 0.0), jnp.where(mask, strain[15 - q, :, at], 0.0)]
            spread.append(jnp.concatenate(pair, axis=1))
    matrix = pair_matrix()
    got = jnp.zeros((32 * len(groups), 128), f32)
    for part in three_parts(jnp.concatenate(spread, axis=0)):
        got = got + nt_dot(part, matrix)
    for n, q in enumerate(groups):
        change = got[32 * n : 32 * n + 32]
        for x in (2 * q, 2 * q + 1):
            rhs[x] = fixed(x) + stabilize * press[x] - (8.0 * biot_coef) * change


def resume_kernel(
    core, layer, own, partner, near, aux, start, coef_late, fixed_late, inverse_late,
    press, u, rhs, edges, inner, strain, moved, swept,
):
    ok = inside_flags(core, layer)
    low = low_mask((32, 128))

    def unpack(runs, extra_cells, extra_node):
        def piece(cell, want_low):
            if cell in extra_cells:
                ref, q, is_low = near, 4, cell == 2
            elif 4 <= cell < 28:
                k = (cell - 4) % 8
                ref, q, is_low = runs[(cell - 4) // 8][0], min(k, 7 - k), k < 4
            else:
                return jnp.zeros((32, 128), f32)
            value = ref[:, q].reshape(32, 128)
            return value if is_low == want_low else roll(value, 64)

        for x in range(2, PLANES):
            press[x] = jnp.where(low, piece(x, True), piece(31 - x, False))
        for n in range(1, 15):
            if n == extra_node:
                ref, k, flag = near, 4, 0
            elif 2 <= n < 14:
                (ref, flag), k = runs[(n - 2) // 4], (n - 2) % 4
            else:
                u[n] = jnp.zeros((8, 512), f32)
                continue
            for y in range(4):
                value = node_of(ref, k, y)
                u[n, :, 128 * y : 128 * y + 128] = value if flag is None else value * ok[flag]

    @pl.when(core[0] == 0)
    def _():
        unpack([(near, 0), (own, None), (partner, None)], (2, 3), 1)

    @pl.when(core[0] == 1)
    def _():
        unpack([(partner, None), (own, None), (near, 0)], (), 14)

    for n in range(3, 14):
        moved[n] = u[n] - start[n]
    strain_rows(aux, lambda n: moved[n], range(3, 13), strain)
    right_sides(strain, range(3, 8), press, lambda x: fixed_late[x - EARLY], rhs)
    for k in range(SWEEPS + 1):
        if k:
            one_sweep(
                lambda x, k=k: press[x] if k == 1 else swept[k % 2, x], swept.at[1 - k % 2],
                lambda way, x: coef_late[way, x - EARLY], rhs, lambda x: inverse_late[x - EARLY], 5 + k,
            )
        level = press if k == 0 else swept.at[1 - k % 2]
        if k < SWEEPS:
            edges[k, 0] = level[5 + k]
            edges[k, 1] = level[6 + k]
    for x in range(11, PLANES):
        inner[x - 11] = swept[1, x]


def second_kernel(
    core, layer, across, stiff, aux, held, u, rhs_late, edges, inner,
    coef_late, fixed_late, inverse_late, start, lam, mu, load, sup, safe, gain,
    coef_early, fixed_early, inverse_early, beside,
    last, press, rhs, means, nodes, strain, moved,
):
    ok = inside_flags(core, layer)
    low = low_mask((32, 128))
    first = core[0] == 0
    for x in range(2, 6):
        press[0, x] = held[x]
    for x in range(6, 11):
        rhs[x] = rhs_late[x]
    for n in range(2, 14):
        nodes[n] = u[n]

    for x, q in ((2, 1), (3, 0)):
        turned = roll(across[:, q].reshape(32, 128), 64)
        press[0, x] = jnp.where(low & jnp.logical_not(first), turned, held[x])
    for y in range(4):
        at = slice(128 * y, 128 * y + 128)
        nodes[1, :, at] = jnp.where(first, u[1, :, at], node_of(across, 3, y, 2) * ok[1])
        nodes[14, :, at] = jnp.where(first, node_of(across, 0, y, 2) * ok[1], u[14, :, at])
    for n in (2, 3, 13):
        moved[0, n] = nodes[n] - start[n]
    moved[0, 1] = nodes[1] - jnp.where(first, start[1], beside[1])
    moved[0, 14] = nodes[14] - jnp.where(first, beside[0], start[14])
    strain[14] = jnp.zeros((1, 512), f32)
    strain_rows(aux, lambda n: moved[0, n], (1, 2, 13), strain)
    right_sides(strain, (1, 2), press.at[0], both(fixed_early, fixed_late), rhs)
    for k in range(1, SWEEPS + 1):
        one_sweep(
            lambda x, k=k: press[1 - k % 2, x] if x < 4 + k else edges[k - 1, x - 4 - k], press.at[k % 2],
            both_faces(coef_early, coef_late), rhs, both(inverse_early, inverse_late), 2 + k, 5 + k,
        )
    for x in range(11, PLANES):
        press[0, x] = inner[x - 11]
    block_means(press.at[0], means, 4, 10)
    displacements(nodes, lam, mu, load, sup, safe, gain, means, stiff, aux, moved, 6, 9)
    pack_last(press.at[0], moved, last)


def unpack_kernel(core, got, pressure, disp, held):
    lane = lanes((8, 128))
    base = core[0] * 8
    tiles = [got[base + s] for s in range(8)]
    for i in range(4):
        total = jnp.zeros((8, 128), f32)
        for s in range(8):
            total = jnp.where(lane // 16 == s, roll(tiles[s], 16 * s - 16 * i), total)
        pressure[i] = total
    for i in range(2):
        for pair in range(2):
            total = jnp.zeros((8, 128), f32)
            for s in range(8):
                for side in range(2):
                    shift = 64 * side + 8 * s - 64 - 32 * i - 8 * (2 * pair + side)
                    total = jnp.where(lane // 8 == 8 * side + s, roll(tiles[s], shift), total)
            held[:, 128 * (2 * i + pair) : 128 * (2 * i + pair) + 128] = total
    disp[...] = held[0:3]


def corner_major(stiff):
    grid = stiff.reshape(3, 2, 4, 3, 2, 4).transpose(2, 1, 0, 5, 4, 3)
    return jnp.pad(grid, ((0, 0), (0, 0), (0, 1), (0, 0), (0, 0), (0, 1))).reshape(32, 32)


def corner_column(vec):
    return jnp.pad(vec.reshape(3, 2, 4).transpose(2, 1, 0), ((0, 0), (0, 0), (0, 1))).reshape(32)


def shape(*dims):
    return jax.ShapeDtypeStruct(dims, f32)


def shards(
    pressure_start, source, storage, perm_class, class_perm, block_route, displacement_start,
    load, support, lame_lambda, lame_mu, stiff_lambda, stiff_mu, coupling_vec,
):
    core = lax.axis_index("grp")
    core_arg = jnp.full((1,), core, jnp.int32)
    row_arg = jnp.full((1,), lax.axis_index("gy"), jnp.int32)
    layer = lax.axis_index("gz")
    layer_arg = jnp.full((1,), layer, jnp.int32)
    swap = [(0, 1), (1, 0)]

    packed = call(
        pack_kernel,
        shape(16, TILES, 8, 128),
        [SM, SM, SM] + [HB] * 11,
        [
            pltpu.VMEM((16, 8, 128), f32),
            pltpu.VMEM((24, 512), f32),
            pltpu.VMEM((1, 8, 512), jnp.int32),
            pltpu.VMEM((4, 8, 128), jnp.int32),
            pltpu.VMEM((3, 3, 512), f32),
            pltpu.VMEM((2, 1, 512), f32),
            pltpu.SMEM((CLASSES,), f32),
            pltpu.VMEM((16, TILES, 8, 128), f32),
            pltpu.SemaphoreType.DMA((11,)),
            pltpu.SemaphoreType.DMA((TILES,)),
        ],
        WHOLE,
        HB,
    )(core_arg, row_arg, layer_arg, class_perm, pressure_start, source, storage, perm_class,
      displacement_start, load, support, lame_lambda, lame_mu, block_route)
    grid = lax.all_to_all(packed, ("gx", "gy"), 0, 0, tiled=True)
    grid, core, layer, stiff_lambda, stiff_mu, coupling_vec = lax.optimization_barrier(
        (grid, core, layer, stiff_lambda, stiff_mu, coupling_vec)
    )
    core_arg = jnp.full((1,), core, jnp.int32)
    layer_arg = jnp.full((1,), layer, jnp.int32)

    ring = [(8 + z, (z + 1) % 8) for z in range(8)] + [(z, 8 + (z - 1) % 8) for z in range(8)]
    grid = grid + lax.ppermute(grid, "grp", swap)
    first = core == 0
    sent = [
        jnp.where(first, grid[0:4, :11], grid[12:16, :11]),
        jnp.sum(jnp.where(first, grid[0:4, 11:], grid[12:16, 11:]), axis=0),
        jnp.where(first, grid[4:8, :9], grid[8:12, :9]),
        jnp.where(first, grid[8:12, 2:4], grid[4:8, 2:4]),
        jnp.where(first, grid[8:12, 6:9], grid[4:8, 6:9]),
    ]
    sent = jnp.concatenate([part.reshape(-1, 8, 128) for part in sent], axis=0)
    halo = lax.ppermute(sent, ("grp", "gz"), ring)
    share = lax.ppermute(halo[:44], "grp", swap)

    stiff = jnp.concatenate([corner_major(stiff_lambda), corner_major(stiff_mu)], axis=0)
    columns = [corner_column(coupling_vec), corner_column(jnp.diag(stiff_lambda)), corner_column(jnp.diag(stiff_mu))]
    aux = jnp.pad(jnp.stack(columns, axis=1), ((0, 0), (0, 125)))

    late = PLANES - EARLY
    statics = call(
        prepare_kernel,
        (
            shape(PLANES - 4, 32, 128), shape(4, 32, 128),
            shape(3, late, 32, 128), shape(late, 32, 128), shape(late, 32, 128),
            shape(NODES, 8, 512), shape(12, 1, 512), shape(12, 1, 512), shape(12, 8, 512),
            shape(12, 8, 512), shape(12, 8, 512), shape(12, 8, 512),
        ),
        [SM, SM] + [VM] * 3,
        [pltpu.VMEM((PLANES, 32, 128), f32)] * 3,
    )(core_arg, layer_arg, grid, halo, aux)
    mid, *early = call(
        first_kernel,
        (
            shape(4, 8, 8, 128), shape(3, EARLY, 32, 128), shape(EARLY, 32, 128),
            shape(EARLY, 32, 128), shape(2, 8, 512),
        ),
        [SM, SM] + [VM] * 16,
        [
            pltpu.VMEM((2, PLANES, 32, 128), f32),
            pltpu.VMEM((4, 32, 128), f32),
            pltpu.VMEM((4, 32, 128), f32),
            pltpu.VMEM((4, 32, 128), f32),
            pltpu.VMEM((PLANES, 32, 128), f32),
            pltpu.VMEM((PLANES, 1, 512), f32),
            pltpu.VMEM((2, NODES, 8, 512), f32),
        ],
    )(core_arg, layer_arg, halo, share, stiff, aux, *statics)

    near = lax.ppermute(mid, ("grp", "gz"), ring)
    partner = lax.ppermute(mid, "grp", swap)
    across = lax.ppermute(jnp.concatenate([near[:, 0:2], near[:, 5:7]], axis=1), "grp", swap)
    resumed = call(
        resume_kernel,
        (
            shape(PLANES, 32, 128), shape(NODES, 8, 512), shape(PLANES, 32, 128),
            shape(SWEEPS, 2, 32, 128), shape(PLANES - 11, 32, 128),
        ),
        [SM, SM] + [VM] * 8,
        [
            pltpu.VMEM((PLANES, 1, 512), f32),
            pltpu.VMEM((NODES, 8, 512), f32),
            pltpu.VMEM((2, PLANES, 32, 128), f32),
        ],
    )(core_arg, layer_arg, mid, partner, near, aux, statics[5], *statics[2:5])
    last = call(
        second_kernel,
        shape(8, 8, 128),
        [SM, SM] + [VM] * 22,
        [
            pltpu.VMEM((2, PLANES, 32, 128), f32),
            pltpu.VMEM((PLANES, 32, 128), f32),
            pltpu.VMEM((PLANES, 1, 512), f32),
            pltpu.VMEM((NODES, 8, 512), f32),
            pltpu.VMEM((PLANES, 1, 512), f32),
            pltpu.VMEM((2, NODES, 8, 512), f32),
        ],
    )(core_arg, layer_arg, across, stiff, aux, *resumed, *statics[2:], *early)

    other = lax.ppermute(last, "grp", swap)
    whole = jnp.concatenate([jnp.where(core == 0, last, other), jnp.where(core == 0, other, last)], axis=0)
    back = lax.all_to_all(whole, ("gx", "gy"), 0, 0, tiled=True)
    return call(
        unpack_kernel,
        (shape(4, 8, 128), shape(3, 512)),
        [SM, VM],
        [pltpu.VMEM((8, 512), f32)],
    )(core_arg, back)


def solution(mesh):
    fine = Mesh(np.asarray(mesh.devices).reshape(2, 8, 4, 4), ("grp", "gz", "gx", "gy"))
    cell = P(("gz", "gx"), "gy", "grp")
    node = P(None, ("grp", "gz", "gx", "gy"))
    elem = P(("grp", "gz", "gx", "gy"), None)
    return jax.shard_map(
        shards,
        mesh=fine,
        in_specs=(
            cell, cell, cell, cell, P(), P(("gz", "gx"), None, None), node, node, node, elem, elem,
            P(), P(), P(),
        ),
        out_specs=(cell, node),
        check_vma=False,
    )
```
